256 devices in a mesh: py: 32 (over x_lo, z, core), pz: 8 (over x_hi, y).
Axes of the slice: x: 4 (x_hi: 2, x_lo: 2; x = x_hi * 2 + x_lo), y: 4, z: 8, core: 2. Of those that a mesh axis runs over, the one named last changes fastest.
Arguments:
- velocity: float32 [3, 256, 256, 256], P(None, 'py', 'pz'), may hold values from -6 to 6
- target: float32 [3, 256, 256, 256], P(None, 'py', 'pz'), may hold values from -48 to 48
- closure_weight: float32 [3, 3, 3, 3, 3], replicated, may hold values from -0.625 to 0.625
- closure_bias: float32 [3], replicated, may hold values from -1 to 1
Outputs:
- grad_velocity: float32 [3, 256, 256, 256], P(None, 'py', 'pz')
- grad_weight: float32 [3, 3, 3, 3, 3], replicated
- grad_bias: float32 [3], replicated
- loss: float32 [], replicated
The draws below stay inside these ranges and needn't reach their ends.
All inputs are finite; a program needn't handle non-finite values.
Results may differ from the reference program's by a relative error of at most 0.0045.
Values may be sent and summed in bfloat16 or wider, within the bound.
A program may use at most 128 MiB of HBM per device.

```python
import math
import jax
import jax.numpy as jnp
from jax import lax

NX = 256
NY = 256
NZ = 256


def draw_target(key, part):
    key = jax.random.fold_in(key, 7)
    noise_key, row_key, column_key, line_key = jax.random.split(key, 4)
    positions = jnp.arange(NY).astype(jnp.float32) / NY
    rows_scale = 3.0 ** positions * 2.0 ** jax.random.uniform(row_key, (NY,))
    columns_scale = 2.0 ** jax.random.uniform(column_key, (NZ,))
    lines_scale = 2.0 ** jax.random.uniform(line_key, (NX,))
    factor = 0.4 * rows_scale[:, None, None] * columns_scale[None, :, None] * lines_scale[None, None, :]
    noise_part = jnp.clip(jax.random.normal(noise_key, (3, NY, NZ, NX)), -5.0, 5.0)
    return (noise_part * factor[None]).astype(jnp.float32)


def steps_of(rng, extent, shards, least, largest):
    def one(position, blocks):
        heights = jax.random.uniform(jax.random.fold_in(jax.random.fold_in(rng, 6), position), (blocks,), jnp.float32, least / len(shards), largest / len(shards))
        return jnp.repeat(jnp.exp(heights), extent[position] // blocks).reshape((-1,) + (1,) * (len(extent) - position - 1))

    level = one(*shards[0])
    for cut in shards[1:]:
        level = level * one(*cut)
    return level


def noise(own_key, extent, deviation, limit, shards=(), dtype=jnp.bfloat16):
    array = jax.random.normal(own_key, extent, jnp.float32) * deviation
    if len(shards) > 0:
        array = steps_of(own_key, extent, shards, -0.22, 0.18) * array
    return jnp.clip(array, min=-limit, max=limit).astype(dtype)


def setup_inputs(seed: int = 0) -> dict:
    arg_keys = jax.random.split(jax.random.key(seed), 5)
    velocity = noise(arg_keys[0], (3, NY, NZ, NX), 1.0, 6.0, ((1, 32), (2, 8)), jnp.float32)
    target = draw_target(jax.random.fold_in(arg_keys[4], 71), 0)
    closure_weight = noise(arg_keys[2], (3, 3, 3, 3, 3), 81 ** -0.5, 0.625, (), jnp.float32)
    closure_bias = jnp.clip(jax.random.uniform(arg_keys[3], (3,), jnp.float32, -1.0, 1.0), -1.0, 1.0)
    return dict(velocity=velocity, target=target, closure_weight=closure_weight, closure_bias=closure_bias)


time_step = 0.01
viscosity = 0.002
highest = lax.Precision.HIGHEST

def phases(positions, wavenumbers, length):
    turns = positions[:, None] * (wavenumbers[None, :] % length) % length
    angles = turns.astype(jnp.float32) * (2.0 * math.pi / length)
    return (jnp.cos(angles), jnp.sin(angles))

def x_tables(length, kmodes):
    factor = 1.0 / math.sqrt(length)
    cosine, sine_part = phases(jnp.arange(length), jnp.arange(kmodes), length)
    forward = jnp.stack([factor * cosine, -factor * sine_part], axis=1)
    weights = jnp.where(jnp.arange(kmodes) == 0, 1.0, 2.0).astype(jnp.float32)[:, None]
    backward = jnp.stack([weights * factor * cosine.T, -weights * factor * sine_part.T], axis=0)
    return (forward.astype(jnp.bfloat16), backward.astype(jnp.bfloat16))

def line_tables(length, kmodes, mode_total):
    factor = 1.0 / math.sqrt(length)
    wavenumbers = jnp.arange(mode_total) - mode_total // 2
    retained = (jnp.abs(wavenumbers) < kmodes).astype(jnp.float32)[None, :]
    cosine, sine_part = phases(jnp.arange(length), wavenumbers, length)
    real_part = factor * cosine * retained
    imag_part = factor * sine_part * retained
    forward = jnp.stack([jnp.stack([real_part, -imag_part], 1), jnp.stack([imag_part, real_part], 1)], 0)
    backward = jnp.stack([jnp.stack([real_part.T, imag_part.T], 1), jnp.stack([-imag_part.T, real_part.T], 1)], 0)
    return (forward.astype(jnp.bfloat16), backward.astype(jnp.bfloat16))

def cross_product(left_side, right_side):
    return jnp.stack([left_side[1] * right_side[2] - left_side[2] * right_side[1], left_side[2] * right_side[0] - left_side[0] * right_side[2], left_side[0] * right_side[1] - left_side[1] * right_side[0]], 0)

def rotate(field, wavenumbers):
    turned = cross_product(wavenumbers, field)
    return jnp.concatenate([-turned[:, :, :, 1:2], turned[:, :, :, 0:1]], axis=3)

def project(field, wavenumbers, square):
    fraction = (wavenumbers[0] * field[0] + wavenumbers[1] * field[1] + wavenumbers[2] * field[2]) / jnp.maximum(square, 1.0)
    return field - jnp.stack([wavenumbers[0] * fraction, wavenumbers[1] * fraction, wavenumbers[2] * fraction], 0)

def convolve(padded, kernel):
    return lax.conv_general_dilated(padded[None], kernel, (1, 1, 1), 'VALID', dimension_numbers=('NCDHW', 'OIDHW', 'NCDHW'), precision=highest)[0]

def to_spectral(field, x_table, y_table, z_table):

    def component(values):
        sectioned = jnp.einsum('yzx,xrk->rkyz', values.astype(jnp.float32), x_table.astype(jnp.float32), precision=highest).astype(jnp.bfloat16)
        middle = jnp.einsum('rkyz,ryqm->qkmz', sectioned.astype(jnp.float32), y_table.astype(jnp.float32), precision=highest).astype(jnp.bfloat16)
        return jnp.einsum('qkmz,qzpn->kmpn', middle.astype(jnp.float32), z_table.astype(jnp.float32), precision=highest).astype(jnp.bfloat16)
    return lax.map(component, field)

def to_physical(spectral, z_table, y_table, x_table):

    def component(values):
        sectioned = jnp.einsum('kmrn,rnqz->qkmz', values.astype(jnp.float32), z_table.astype(jnp.float32), precision=highest).astype(jnp.bfloat16)
        middle = jnp.einsum('qkmz,qmpy->pkyz', sectioned.astype(jnp.float32), y_table.astype(jnp.float32), precision=highest).astype(jnp.bfloat16)
        return jnp.einsum('pkyz,pkx->yzx', middle.astype(jnp.float32), x_table.astype(jnp.float32), precision=highest)
    return lax.map(component, spectral)

def wrap_pad(field):
    return jnp.pad(field, ((0, 0), (1, 1), (1, 1), (1, 1)), mode='wrap')

def reference(velocity, target, closure_weight, closure_bias):
    rows_total = velocity.shape[1]
    depth_total = velocity.shape[2]
    length = velocity.shape[3]
    kmodes = length // 4
    y_bound = rows_total // 4
    z_bound = depth_total // 4
    x_forward, x_backward = x_tables(length, kmodes)
    y_forward, y_backward = line_tables(rows_total, y_bound, 2 * y_bound)
    z_forward, z_backward = line_tables(depth_total, z_bound, 2 * z_bound)
    wavenumbers = (jnp.arange(kmodes).astype(jnp.float32)[:, None, None, None], (jnp.arange(2 * y_bound) - y_bound).astype(jnp.float32)[None, :, None, None], (jnp.arange(2 * z_bound) - z_bound).astype(jnp.float32)[None, None, None, :])
    square = wavenumbers[0] ** 2 + wavenumbers[1] ** 2 + wavenumbers[2] ** 2
    velocity_hat = to_spectral(velocity.astype(jnp.bfloat16), x_forward, y_forward, z_forward)
    vorticity_hat = rotate(velocity_hat.astype(jnp.float32), wavenumbers).astype(jnp.bfloat16)
    vorticity = to_physical(vorticity_hat, z_backward, y_backward, x_backward)
    nonlinear = cross_product(velocity, vorticity).astype(jnp.bfloat16)
    nonlinear_hat = to_spectral(nonlinear, x_forward, y_forward, z_forward)
    rate_hat = (project(nonlinear_hat.astype(jnp.float32), wavenumbers, square) - viscosity * square * velocity_hat.astype(jnp.float32)).astype(jnp.bfloat16)
    rate_field = to_physical(rate_hat, z_backward, y_backward, x_backward)
    padded_velocity = wrap_pad(velocity)

    def closure_of(kernel):
        return convolve(padded_velocity, kernel)
    closure, pullback = jax.vjp(closure_of, closure_weight)
    closure = closure + closure_bias[:, None, None, None]
    misfit = velocity + time_step * rate_field + closure - target
    cell_count = float(length * rows_total * depth_total)
    loss = 0.5 * jnp.sum(misfit * misfit) / cell_count
    grad_weight = pullback(misfit)[0] / cell_count
    grad_bias = lax.optimization_barrier(jnp.sum(misfit, axis=(1, 2, 3))) / cell_count
    flipped = jnp.transpose(jnp.flip(closure_weight, (2, 3, 4)), (1, 0, 2, 3, 4))
    closure_grad = convolve(wrap_pad(misfit), flipped)
    rate_grad = to_spectral((time_step * misfit).astype(jnp.bfloat16), jnp.transpose(x_backward, (2, 0, 1)), jnp.transpose(y_backward, (2, 3, 0, 1)), jnp.transpose(z_backward, (2, 3, 0, 1)))
    projected = project(rate_grad.astype(jnp.float32), wavenumbers, square).astype(jnp.bfloat16)
    nonlinear_grad = to_physical(projected, jnp.transpose(z_forward, (2, 3, 0, 1)), jnp.transpose(y_forward, (2, 3, 0, 1)), jnp.transpose(x_forward, (1, 2, 0)))
    cross_grad = cross_product(vorticity, nonlinear_grad)
    vorticity_field_grad = cross_product(nonlinear_grad, velocity).astype(jnp.bfloat16)
    vorticity_grad = to_spectral(vorticity_field_grad, jnp.transpose(x_backward, (2, 0, 1)), jnp.transpose(y_backward, (2, 3, 0, 1)), jnp.transpose(z_backward, (2, 3, 0, 1)))
    velocity_grad_hat = (rotate(vorticity_grad.astype(jnp.float32), wavenumbers) - viscosity * square * rate_grad.astype(jnp.float32)).astype(jnp.bfloat16)
    spectral_grad = to_physical(velocity_grad_hat, jnp.transpose(z_forward, (2, 3, 0, 1)), jnp.transpose(y_forward, (2, 3, 0, 1)), jnp.transpose(x_forward, (1, 2, 0)))
    grad_velocity = misfit + closure_grad + cross_grad + spectral_grad
    return (grad_velocity, grad_weight, grad_bias, loss)
```

```python
import functools
import math

import jax
import jax.numpy as jnp
import ml_dtypes
import numpy as np
from jax import lax
from jax.experimental import pallas as pl
from jax.experimental.pallas import tpu as pltpu
from jax.sharding import PartitionSpec as P

NX = 256
NY = 256
NZ = 256
PY = 32
PZ = 8
ROWS = NY // PY
DEPTH = NZ // PZ
KX = NX // 4
KL = KX // PZ
MODES = 128
LANES = 128
CELLS = float(NX * NY * NZ)
time_step = 0.01
viscosity = 0.002
MESH = pl.DeviceIdType.MESH
f32 = jnp.float32
bf16 = jnp.bfloat16


def ring(offset, length):
    return min(offset, length - offset)


FAR_PY = sorted(
    [(x, z, c) for x in range(2) for z in range(8) for c in range(2) if x + z + c > 0],
    key=lambda o: (-ring(o[1], 8) - o[0], o[1] > 4, o),
)
FAR_PZ = sorted(
    [(x, y) for x in range(2) for y in range(4) if x + y > 0],
    key=lambda o: (-ring(o[1], 4) - 2 * o[0], o),
)


def phases(positions, wavenumbers, length):
    turns = positions[:, None] * (wavenumbers[None, :] % length) % length
    angles = turns.astype(np.float32) * np.float32(2.0 * math.pi / length)
    return np.cos(angles), np.sin(angles)


def tables():
    factor = np.float32(1.0 / math.sqrt(NX))
    cosine, sine = phases(np.arange(NX), np.arange(KX), NX)
    pair = np.stack([factor * cosine, -factor * sine], axis=0)
    plain = pair.transpose(0, 2, 1).reshape(2, PZ, KL, NX).transpose(1, 0, 2, 3)
    plain = plain.reshape(2 * KX, NX)
    weights = np.where(np.arange(KX) == 0, 1.0, 2.0).astype(np.float32)
    weights = np.broadcast_to(weights.reshape(PZ, 1, KL), (PZ, 2, KL)).reshape(2 * KX, 1)
    wavenumbers = np.arange(MODES) - MODES // 2
    retained = (np.abs(wavenumbers) < MODES // 2).astype(np.float32)[None, :]
    cosine, sine = phases(np.arange(NZ), wavenumbers, NZ)
    real = factor * cosine * retained
    imag = -factor * sine * retained
    z_out = np.concatenate([real, imag], axis=1)
    z_back = np.concatenate([real.T, imag.T], axis=1)
    full = np.stack([np.stack([real, imag], 0), np.stack([-imag, real], 0)], 0)
    y_out = full.reshape(2, 2, PY, ROWS, MODES).transpose(1, 4, 2, 0, 3)
    y_out = y_out.reshape(2 * MODES, 2 * NY)
    given = (plain, plain * weights, z_out, z_back, y_out, y_out.T)
    return tuple(np.ascontiguousarray(t).astype(ml_dtypes.bfloat16) for t in given)


def swap_groups(tiles, lane):
    a0, a1, a2, a3 = tiles
    low = lane < 64
    b0 = jnp.where(low, a0, pltpu.roll(a2, 64, 1))
    b2 = jnp.where(low, pltpu.roll(a0, 64, 1), a2)
    b1 = jnp.where(low, a1, pltpu.roll(a3, 64, 1))
    b3 = jnp.where(low, pltpu.roll(a1, 64, 1), a3)
    even = (lane // 32) % 2 == 0
    c0 = jnp.where(even, b0, pltpu.roll(b1, 32, 1))
    c1 = jnp.where(even, pltpu.roll(b0, 96, 1), b1)
    c2 = jnp.where(even, b2, pltpu.roll(b3, 32, 1))
    c3 = jnp.where(even, pltpu.roll(b2, 96, 1), b3)
    return c0, c1, c2, c3


def dot(left, right, over):
    return lax.dot_general(left, right, (over, ((), ())), preferred_element_type=f32)


def kernel(
    vel, target, weight, flipped, bias, x_plain, x_twice, z_out, z_back, y_out, y_back,
    grad, sums,
    pz_send, pz_recv, py_send, py_recv, field_in, z_in, stage, spec_out,
    vort, push, v_pad, m_pad, v_shift, m_shift, closure, halo_out, halo_in,
    w_parts, r_own, r_pz, r_mid, r_py, hat_v, hat_r,
    pz_ss, pz_rs, py_ss, py_rs, halo_ss, halo_rs, red_ss, red_rs,
):
    py = lax.axis_index("py")
    pz = lax.axis_index("pz")

    barrier = pltpu.get_barrier_semaphore()

    def greet(k, _):
        pl.semaphore_signal(
            barrier, inc=1, device_id=(lax.rem(py + k, PY), pz), device_id_type=MESH
        )
        return 0

    lax.fori_loop(1, PY, greet, 0)
    for k in range(1, PZ):
        pl.semaphore_signal(
            barrier, inc=1, device_id=(py, lax.rem(pz + k, PZ)), device_id_type=MESH
        )

    def remote(src, dst, ss, rs, device):
        return pltpu.make_async_remote_copy(
            src_ref=src, dst_ref=dst, send_sem=ss, recv_sem=rs, device_id=device,
            device_id_type=MESH,
        )

    def send_pz(send_of, recv, ss, rs):
        for dx, dy in FAR_PZ:
            to = lax.rem(pz // 4 + dx, 2) * 4 + lax.rem(lax.rem(pz, 4) + dy, 4)
            remote(send_of(to), recv.at[pz], ss, rs, (py, to)).start()
        pltpu.make_async_copy(send_of(pz), recv.at[pz], rs).start()

    def send_py(send_of, recv, ss, rs):
        x, z, core = py // 16, lax.rem(py, 16) // 2, lax.rem(py, 2)
        for dx, dz, dc in FAR_PY:
            to = lax.rem(x + dx, 2) * 16 + lax.rem(z + dz, 8) * 2 + lax.rem(core + dc, 2)
            remote(send_of(to), recv.at[py], ss, rs, (to, pz)).start()
        pltpu.make_async_copy(send_of(py), recv.at[py], rs).start()

    def arrived(ref, sem):
        pltpu.make_async_copy(ref, ref, sem).wait()

    lane16 = lax.broadcasted_iota(jnp.int32, (16, LANES), 1)
    lane64 = lax.broadcasted_iota(jnp.int32, (64, LANES), 1)

    def halo_y_start(pad, n):
        up = lax.rem(py + 1, PY)
        down = lax.rem(py + PY - 1, PY)
        remote(pad.at[:, ROWS], pad.at[:, 0], halo_ss.at[n], halo_rs.at[n], (up, pz)).start()
        remote(
            pad.at[:, 1], pad.at[:, ROWS + 1], halo_ss.at[n + 1], halo_rs.at[n + 1], (down, pz)
        ).start()

    def halo_z_start(pad, n):
        arrived(pad.at[:, 0], halo_rs.at[n])
        arrived(pad.at[:, ROWS + 1], halo_rs.at[n + 1])
        s = n // 4
        halo_out[s, :, 24:, :] = jnp.zeros((2, 8, NX), f32)
        for j in range(3):
            for y in range(ROWS + 2):
                r = j * (ROWS + 2) + y
                halo_out[s, 0, r : r + 1, :] = pad[j, y, DEPTH - 1 : DEPTH, :]
                halo_out[s, 1, r : r + 1, :] = pad[j, y, 0:1, :]
        up = lax.rem(pz + 1, PZ)
        down = lax.rem(pz + PZ - 1, PZ)
        for side, to in ((0, up), (1, down)):
            remote(
                halo_out.at[s, side], halo_in.at[s, side], halo_ss.at[n + 2 + side],
                halo_rs.at[n + 2 + side], (py, to),
            ).start()

    def shifts(pad, out, n):
        s = n // 4
        arrived(halo_in.at[s, 0], halo_rs.at[n + 2])
        arrived(halo_in.at[s, 1], halo_rs.at[n + 3])
        row = lax.broadcasted_iota(jnp.int32, (DEPTH, NX), 0)
        for j in range(3):
            for y in range(ROWS + 2):
                r = j * (ROWS + 2) + y
                here = pad[j, y]
                below = jnp.where(row == 0, halo_in[s, 0, r : r + 1, :], pltpu.roll(here, 1, 0))
                above = jnp.where(
                    row == DEPTH - 1, halo_in[s, 1, r : r + 1, :], pltpu.roll(here, DEPTH - 1, 0)
                )
                for b, cells in enumerate((below, here, above)):
                    out[j * 9 + b * 3, y] = pltpu.roll(cells, 1, 1)
                    out[j * 9 + b * 3 + 1, y] = cells
                    out[j * 9 + b * 3 + 2, y] = pltpu.roll(cells, NX - 1, 1)

    def convolve_row(shifted, factors, y):
        def step(t, sums_here):
            at = t + (t // 9) * 18
            sums_here = list(sums_here)
            for a in range(3):
                cells = shifted[t, y + a]
                for i in range(3):
                    sums_here[i] = sums_here[i] + factors[i * 81 + a * 9 + at] * cells
            return tuple(sums_here)

        zero = jnp.zeros((DEPTH, NX), f32)
        return lax.fori_loop(0, 27, step, (zero, zero, zero))

    def closure_rows(rows):
        for y in rows:
            for i, cells in enumerate(convolve_row(v_shift, weight, y)):
                closure[i, y] = cells + bias[i]

    def grad_rows(rows):
        for y in rows:
            for i, cells in enumerate(convolve_row(m_shift, flipped, y)):
                closure[i, y] = cells

    def fold(cells):
        total = cells[0:8]
        for k in range(8, DEPTH, 8):
            total = total + cells[k : k + 8]
        return total[:, :LANES] + total[:, LANES:]

    def weight_parts(first, last):
        def one(t, _):
            def row(y, parts):
                parts = list(parts)
                for a in range(3):
                    cells = v_shift[t, y + a]
                    for i in range(3):
                        parts[i * 3 + a] = parts[i * 3 + a] + fold(m_pad[i, y + 1] * cells)
                return tuple(parts)

            zero = jnp.zeros((8, LANES), f32)
            parts = lax.fori_loop(0, ROWS, row, (zero,) * 9)
            at = t + (t // 9) * 18
            for i in range(3):
                for a in range(3):
                    w_parts[i * 81 + a * 9 + at] = parts[i * 3 + a]
            return 0

        lax.fori_loop(first, last, one, 0)

    def reduce_start():
        by_lane = jnp.sum(w_parts[...], axis=1)
        r_own[...] = jnp.sum(by_lane.T, axis=0, keepdims=True) * (1.0 / CELLS)
        send_pz(lambda to: r_own, r_pz, red_ss.at[0], red_rs.at[0])

    def reduce_next():
        arrived(r_pz, red_rs.at[0])
        total = r_pz[0]
        for k in range(1, PZ):
            total = total + r_pz[k]
        r_mid[...] = total
        send_py(lambda to: r_mid, r_py, red_ss.at[1], red_rs.at[1])

    def reduce_end():
        arrived(r_py, red_rs.at[1])
        total = r_py[0]
        for k in range(1, PY):
            total = total + r_py[k]
        sums[...] = total

    lane = lax.broadcasted_iota(jnp.int32, (MODES, LANES), 1)
    group = lane // 32
    kx = (pz * KL + py // 4).astype(f32) + jnp.zeros((MODES, LANES), f32)
    ky = (lax.broadcasted_iota(jnp.int32, (MODES, LANES), 0) - MODES // 2).astype(f32)
    kz = (lane % 32 + (py % 4) * 32 - MODES // 2).astype(f32)
    square = kx * kx + ky * ky + kz * kz

    def pick(first, second, third):
        return jnp.where(group == 0, first, jnp.where(group == 1, second, third))

    def next_one(cells):
        return jnp.where(group == 2, pltpu.roll(cells, 64, 1), pltpu.roll(cells, 96, 1))

    def next_two(cells):
        return jnp.where(group == 0, pltpu.roll(cells, 64, 1), pltpu.roll(cells, 32, 1))

    def turned(cells):
        return pick(ky, kz, kx) * next_two(cells) - pick(kz, kx, ky) * next_one(cells)

    def curl(real, imag):
        return -turned(imag), turned(real)

    def project(cells):
        along = pick(kx, ky, kz)
        part = along * cells
        part = part + next_one(part) + next_two(part)
        return cells - along * (part / jnp.maximum(square, 1.0))

    def out_pz(n):
        send_pz(lambda to: pz_send.at[n, to], pz_recv.at[n], pz_ss.at[n], pz_rs.at[n])

    def out_py(n):
        send_py(lambda to: py_send.at[n, to], py_recv.at[n], py_ss.at[n], py_rs.at[n])

    def in_pz(n):
        arrived(pz_recv.at[n], pz_rs.at[n])

    def in_py(n):
        arrived(py_recv.at[n], py_rs.at[n])

    def x_stage(n, table):
        for t in range(6):
            out = dot(table[...], field_in[t * 128 : (t + 1) * 128, :], ((1,), (1,)))
            out = out.astype(bf16)
            for p in range(PZ):
                pz_send[n, p, t] = out[p * 16 : (p + 1) * 16]

    def z_stage(n):
        in_pz(n)
        for t in range(6):
            for h in range(2):
                tiles = [pz_recv[n, 4 * h + g, t].astype(f32) for g in range(4)]
                for m, tile in enumerate(swap_groups(tiles, lane16)):
                    at = (m * 6 + t) * 16
                    z_in[at : at + 16, h * 128 : (h + 1) * 128] = tile.astype(bf16)
        for m in range(4):
            both = dot(z_in[m * 96 : (m + 1) * 96, :], z_out[...], ((1,), (0,)))
            for c in range(3):
                for h in range(2):
                    at = (c * 2 + h) * 16
                    r0 = both[at : at + 8]
                    r1 = both[at + 8 : at + 16]
                    y = h * 4 + m
                    stage[c, 0, pl.ds(y, 8, stride=8), :] = r0[:, :128] - r1[:, 128:]
                    stage[c, 1, pl.ds(y, 8, stride=8), :] = r0[:, 128:] + r1[:, :128]
        blocks = [
            swap_groups(
                [stage[0, q], stage[1, q], stage[2, q], jnp.zeros((64, LANES), f32)], lane64
            )
            for q in range(2)
        ]
        for g in range(4):
            for k in range(KL):
                py_send[n, k * 4 + g] = jnp.concatenate(
                    [blocks[0][g][k * 8 : k * 8 + 8], blocks[1][g][k * 8 : k * 8 + 8]], axis=0
                ).astype(bf16)

    def y_stage(n):
        in_py(n)
        return dot(y_out[...], py_recv[n].reshape(512, LANES), ((1,), (0,)))

    def y_back_stage(n, modes):
        rows = dot(y_back[...], modes, ((1,), (0,))).astype(bf16)
        for d in range(PY):
            py_send[n, d] = rows[d * 16 : (d + 1) * 16]

    def z_back_stage(n):
        in_py(n)
        for k in range(KL):
            tiles = [py_recv[n, k * 4 + g].astype(f32) for g in range(4)]
            for c, tile in enumerate(swap_groups(tiles, lane16)[:3]):
                at = c * 128 + k * 16
                z_in[at : at + 16, 0:128] = tile.astype(bf16)
        for c in range(3):
            both = dot(z_in[c * 128 : (c + 1) * 128, 0:128], z_back[...], ((1,), (0,)))
            for k in range(KL):
                r0 = both[k * 16 : k * 16 + 8]
                r1 = both[k * 16 + 8 : k * 16 + 16]
                for half in range(2):
                    re = slice(half * 128, half * 128 + 128)
                    im = slice(half * 128 + 256, half * 128 + 384)
                    spec_out[c, half, pl.ds(k, 8, stride=16), :] = r0[:, re] + r1[:, im]
                    spec_out[c, half, pl.ds(8 + k, 8, stride=16), :] = r1[:, re] - r0[:, im]
        for c in range(3):
            for h in range(2):
                for half in range(2):
                    tiles = [
                        spec_out[c, half, (h * 4 + m) * 16 : (h * 4 + m + 1) * 16]
                        for m in range(4)
                    ]
                    for g, tile in enumerate(swap_groups(tiles, lane16)):
                        pz_send[n, half * 4 + g, c * 2 + h] = tile.astype(bf16)

    def x_back_stage(n, table, out):
        in_pz(n)
        for t in range(6):
            block = pz_recv[n, :, t].reshape(128, LANES)
            out(t, dot(block, table[...], ((0,), (0,))))

    def keep(ref):
        def store(t, cells):
            ref[t * 128 : (t + 1) * 128, :] = cells

        return store

    def rows_of(c, y):
        at = (c * ROWS + y) * DEPTH
        return slice(at, at + DEPTH)

    def cross(left, right):
        return (
            left[1] * right[2] - left[2] * right[1],
            left[2] * right[0] - left[0] * right[2],
            left[0] * right[1] - left[1] * right[0],
        )

    for c in range(3):
        for y in range(ROWS):
            cells = vel[c, y]
            v_pad[c, y + 1] = cells
            field_in[rows_of(c, y), :] = cells.astype(bf16)
    x_stage(0, x_plain)
    pl.semaphore_wait(barrier, PY - 1 + PZ - 1)
    out_pz(0)
    halo_y_start(v_pad, 0)
    halo_z_start(v_pad, 0)
    z_stage(0)
    out_py(0)
    shifts(v_pad, v_shift, 0)
    modes = y_stage(0).astype(bf16)
    hat_v[...] = modes
    real, imag = curl(modes[:MODES].astype(f32), modes[MODES:].astype(f32))
    y_back_stage(1, jnp.concatenate([real, imag], axis=0).astype(bf16))
    out_py(1)
    closure_rows(range(0, 4))
    z_back_stage(1)
    out_pz(1)

    closure_rows(range(4, ROWS))
    for c in range(3):
        for y in range(ROWS):
            cells = vel[c, y] + closure[c, y] - target[c, y]
            closure[c, y] = cells
            field_in[rows_of(c, y), :] = (time_step * cells).astype(bf16)
    x_stage(2, x_twice)
    x_back_stage(1, x_twice, keep(vort))
    for y in range(ROWS):
        here = [vel[c, y] for c in range(3)]
        there = [vort[rows_of(c, y), :] for c in range(3)]
        for c, cells in enumerate(cross(here, there)):
            field_in[rows_of(c, y), :] = cells.astype(bf16)
    x_stage(3, x_plain)
    out_pz(3)
    out_pz(2)
    z_stage(3)
    out_py(3)
    z_stage(2)
    out_py(2)
    modes = y_stage(3).astype(bf16).astype(f32)
    drag = viscosity * square
    real = project(modes[:MODES]) - drag * hat_v[:MODES].astype(f32)
    imag = project(modes[MODES:]) - drag * hat_v[MODES:].astype(f32)
    rate_hat = jnp.concatenate([real, imag], axis=0).astype(bf16)
    twice = jnp.where(kx == 0.0, 1.0, 2.0) * (time_step * time_step)
    again = y_stage(2)
    real = (again[:MODES] + twice * rate_hat[:MODES].astype(f32)).astype(bf16)
    imag = (again[MODES:] + twice * rate_hat[MODES:].astype(f32)).astype(bf16)
    hat_r[:MODES] = real
    hat_r[MODES:] = imag
    modes = jnp.concatenate([project(real.astype(f32)), project(imag.astype(f32))], axis=0)
    y_back_stage(4, modes.astype(bf16))
    out_py(4)
    y_back_stage(5, rate_hat)
    out_py(5)
    z_back_stage(4)
    out_pz(4)
    z_back_stage(5)
    out_pz(5)

    x_back_stage(4, x_plain, keep(push))
    for y in range(ROWS):
        here = [vel[c, y] for c in range(3)]
        there = [push[rows_of(c, y), :] for c in range(3)]
        for c, cells in enumerate(cross(there, here)):
            field_in[rows_of(c, y), :] = cells.astype(bf16)
    x_stage(6, x_twice)
    out_pz(6)

    parts = [jnp.zeros((8, LANES), f32) for _ in range(4)]

    def misfit(t, rate):
        c = t // 2
        for m in range(4):
            y = (t % 2) * 4 + m
            cells = closure[c, y] + time_step * rate[m * DEPTH : (m + 1) * DEPTH]
            m_pad[c, y + 1] = cells
            parts[c] = parts[c] + fold(cells)
            parts[3] = parts[3] + fold(cells * cells)

    x_back_stage(5, x_twice, misfit)
    halo_y_start(m_pad, 4)
    for c in range(3):
        w_parts[243 + c] = parts[c]
    w_parts[246] = 0.5 * parts[3]
    for k in range(247, 256):
        w_parts[k] = jnp.zeros((8, LANES), f32)
    z_stage(6)
    out_py(6)
    halo_z_start(m_pad, 4)
    weight_parts(0, 27)
    reduce_start()
    modes = y_stage(6).astype(bf16).astype(f32)
    real, imag = curl(modes[:MODES], modes[MODES:])
    real = real - drag * hat_r[:MODES].astype(f32)
    imag = imag - drag * hat_r[MODES:].astype(f32)
    y_back_stage(7, jnp.concatenate([real, imag], axis=0).astype(bf16))
    out_py(7)
    shifts(m_pad, m_shift, 4)
    reduce_next()
    z_back_stage(7)
    out_pz(7)
    grad_rows(range(ROWS))
    for y in range(ROWS):
        here = [vort[rows_of(c, y), :] for c in range(3)]
        there = [push[rows_of(c, y), :] for c in range(3)]
        for c, cells in enumerate(cross(here, there)):
            closure[c, y] = closure[c, y] + m_pad[c, y + 1] + cells
    reduce_end()

    def finish(t, cells):
        for m in range(4):
            y = (t % 2) * 4 + m
            grad[t // 2, y] = closure[t // 2, y] + cells[m * DEPTH : (m + 1) * DEPTH]

    x_back_stage(7, x_plain, finish)

    for n in range(8):
        arrived(pz_send.at[n, 0 : PZ - 1], pz_ss.at[n])
        arrived(py_send.at[n, 0 : PY - 1], py_ss.at[n])
    for n in (0, 4):
        pad = v_pad if n == 0 else m_pad
        arrived(pad.at[:, 0], halo_ss.at[n])
        arrived(pad.at[:, 0], halo_ss.at[n + 1])
        arrived(halo_out.at[n // 4, 0], halo_ss.at[n + 2])
        arrived(halo_out.at[n // 4, 1], halo_ss.at[n + 3])
    arrived(r_pz.at[0 : PZ - 1], red_ss.at[0])
    arrived(r_py.at[0 : PY - 1], red_ss.at[1])


def on_device(velocity, target, closure_weight, closure_bias):
    shape = velocity.shape
    factors = closure_weight.reshape(243)
    flipped = jnp.transpose(jnp.flip(closure_weight, (2, 3, 4)), (1, 0, 2, 3, 4)).reshape(243)
    given = [jnp.asarray(t) for t in tables()]
    in_vmem = pl.BlockSpec(memory_space=pltpu.VMEM)
    in_smem = pl.BlockSpec(memory_space=pltpu.SMEM)
    dma = pltpu.SemaphoreType.DMA
    pad = (3, ROWS + 2, DEPTH, NX)
    grad, sums = pl.pallas_call(
        kernel,
        out_shape=(
            jax.ShapeDtypeStruct(shape, f32),
            jax.ShapeDtypeStruct((1, 256), f32),
        ),
        in_specs=[in_vmem, in_vmem, in_smem, in_smem, in_smem] + [in_vmem] * 6,
        out_specs=(in_vmem, in_vmem),
        scratch_shapes=[
            pltpu.VMEM((8, PZ, 6, 16, LANES), bf16),
            pltpu.VMEM((8, PZ, 6, 16, LANES), bf16),
            pltpu.VMEM((8, PY, 16, LANES), bf16),
            pltpu.VMEM((8, PY, 16, LANES), bf16),
            pltpu.VMEM((768, NX), bf16),
            pltpu.VMEM((384, 256), bf16),
            pltpu.VMEM((3, 2, 64, LANES), f32),
            pltpu.VMEM((3, 2, 128, LANES), f32),
            pltpu.VMEM((768, NX), f32),
            pltpu.VMEM((768, NX), f32),
            pltpu.VMEM(pad, f32),
            pltpu.VMEM(pad, f32),
            pltpu.VMEM((27, ROWS + 2, DEPTH, NX), f32),
            pltpu.VMEM((27, ROWS + 2, DEPTH, NX), f32),
            pltpu.VMEM((3, ROWS, DEPTH, NX), f32),
            pltpu.VMEM((2, 2, 32, NX), f32),
            pltpu.VMEM((2, 2, 32, NX), f32),
            pltpu.VMEM((256, 8, LANES), f32),
            pltpu.VMEM((1, 256), f32),
            pltpu.VMEM((PZ, 1, 256), f32),
            pltpu.VMEM((1, 256), f32),
            pltpu.VMEM((PY, 1, 256), f32),
            pltpu.VMEM((256, LANES), bf16),
            pltpu.VMEM((256, LANES), bf16),
            dma((8,)), dma((8,)), dma((8,)), dma((8,)), dma((8,)), dma((8,)), dma((2,)), dma((2,)),
        ],
        compiler_params=pltpu.CompilerParams(
            collective_id=0, has_side_effects=True, vmem_limit_bytes=56 << 20
        ),
        name="euler",
    )(velocity, target, factors, flipped, closure_bias, *given)
    return (grad, sums[0, :243].reshape(3, 3, 3, 3, 3), sums[0, 243:246], sums[0, 246])


def solution(mesh):
    in_specs = (P(None, "py", "pz", None), P(None, "py", "pz", None), P(), P())
    out_specs = (P(None, "py", "pz", None), P(), P(), P())
    return jax.shard_map(
        on_device, mesh=mesh, in_specs=in_specs, out_specs=out_specs, check_vma=False
    )
```

```python
import functools
import math

import jax
import jax.numpy as jnp
import ml_dtypes
import numpy as np
from jax import lax
from jax.experimental import pallas as pl
from jax.experimental.pallas import tpu as pltpu
from jax.sharding import PartitionSpec as P

NX = 256
NY = 256
NZ = 256
PY = 32
PZ = 8
ROWS = NY // PY
DEPTH = NZ // PZ
KX = NX // 4
KL = KX // PZ
MODES = 128
LANES = 128
CELLS = float(NX * NY * NZ)
time_step = 0.01
viscosity = 0.002
MESH = pl.DeviceIdType.MESH
f32 = jnp.float32
bf16 = jnp.bfloat16


def ring(offset, length):
    return min(offset, length - offset)


FAR_PY = sorted(
    [(x, z, c) for x in range(2) for z in range(8) for c in range(2) if x + z + c > 0],
    key=lambda o: (-ring(o[1], 8) - o[0], o[1] > 4, o),
)
FAR_PZ = sorted(
    [(x, y) for x in range(2) for y in range(4) if x + y > 0],
    key=lambda o: (-ring(o[1], 4) - 2 * o[0], o),
)


def phases(positions, wavenumbers, length):
    turns = positions[:, None] * (wavenumbers[None, :] % length) % length
    angles = turns.astype(np.float32) * np.float32(2.0 * math.pi / length)
    return np.cos(angles), np.sin(angles)


def tables():
    factor = np.float32(1.0 / math.sqrt(NX))
    cosine, sine = phases(np.arange(NX), np.arange(KX), NX)
    pair = np.stack([factor * cosine, -factor * sine], axis=0)
    plain = pair.transpose(0, 2, 1).reshape(2, PZ, KL, NX).transpose(1, 0, 2, 3)
    plain = plain.reshape(2 * KX, NX)
    weights = np.where(np.arange(KX) == 0, 1.0, 2.0).astype(np.float32)
    weights = np.broadcast_to(weights.reshape(PZ, 1, KL), (PZ, 2, KL)).reshape(2 * KX, 1)
    wavenumbers = np.arange(MODES) - MODES // 2
    retained = (np.abs(wavenumbers) < MODES // 2).astype(np.float32)[None, :]
    cosine, sine = phases(np.arange(NZ), wavenumbers, NZ)
    real = factor * cosine * retained
    imag = -factor * sine * retained
    z_out = np.concatenate([real, imag], axis=1)
    z_back = np.concatenate([real.T, imag.T], axis=1)
    full = np.stack([np.stack([real, imag], 0), np.stack([-imag, real], 0)], 0)
    y_out = full.reshape(2, 2, PY, ROWS, MODES).transpose(1, 4, 2, 0, 3)
    y_out = y_out.reshape(2 * MODES, 2 * NY)
    given = (plain, plain * weights, z_out, z_back, y_out, y_out.T)
    return tuple(np.ascontiguousarray(t).astype(ml_dtypes.bfloat16) for t in given)


def swap_groups(tiles, lane):
    a0, a1, a2, a3 = tiles
    low = lane < 64
    b0 = jnp.where(low, a0, pltpu.roll(a2, 64, 1))
    b2 = jnp.where(low, pltpu.roll(a0, 64, 1), a2)
    b1 = jnp.where(low, a1, pltpu.roll(a3, 64, 1))
    b3 = jnp.where(low, pltpu.roll(a1, 64, 1), a3)
    even = (lane // 32) % 2 == 0
    c0 = jnp.where(even, b0, pltpu.roll(b1, 32, 1))
    c1 = jnp.where(even, pltpu.roll(b0, 96, 1), b1)
    c2 = jnp.where(even, b2, pltpu.roll(b3, 32, 1))
    c3 = jnp.where(even, pltpu.roll(b2, 96, 1), b3)
    return c0, c1, c2, c3


def dot(left, right, over):
    return lax.dot_general(left, right, (over, ((), ())), preferred_element_type=f32)


def kernel(
    vel_in, target_in, weight, bias, *refs,
):
    tables_in, refs = refs[:6], refs[6:]
    base_out, last_recv, sums = refs[:3]
    (x_plain, x_twice, z_out, z_back, y_out, y_back, target), refs = refs[3:10], refs[10:]
    (
        pz_send, pz_recv, py_send, py_recv, field_in, z_in, stage, spec_out,
        vort, push, v_pad, m_pad, v_shift, m_shift, closure, halo_out, halo_in,
        w_parts, r_own, r_pz, r_mid, r_py, hat_v, hat_r,
        pz_ss, pz_rs, py_ss, py_rs, halo_ss, halo_rs, red_ss, red_rs, in_sem, base_sem,
    ) = refs
    py = lax.axis_index("py")
    pz = lax.axis_index("pz")

    barrier = pltpu.get_barrier_semaphore()

    def greet(k, _):
        pl.semaphore_signal(
            barrier, inc=1, device_id=(lax.rem(py + k, PY), pz), device_id_type=MESH
        )
        return 0

    lax.fori_loop(1, PY, greet, 0)
    for k in range(1, PZ):
        pl.semaphore_signal(
            barrier, inc=1, device_id=(py, lax.rem(pz + k, PZ)), device_id_type=MESH
        )

    loads = [pltpu.make_async_copy(tables_in[0], x_plain, in_sem.at[0])]
    for c in range(3):
        loads.append(
            pltpu.make_async_copy(
                vel_in.at[c], v_pad.at[c, pl.ds(1, ROWS)], in_sem.at[1 + c]
            )
        )
    later = ((2, z_out), (4, y_out), (5, y_back), (3, z_back), (1, x_twice))
    for k, (at, ref) in enumerate(later):
        loads.append(pltpu.make_async_copy(tables_in[at], ref, in_sem.at[4 + k]))
    loads.append(pltpu.make_async_copy(target_in, target, in_sem.at[9]))
    for load in loads:
        load.start()

    def remote(src, dst, ss, rs, device):
        return pltpu.make_async_remote_copy(
            src_ref=src, dst_ref=dst, send_sem=ss, recv_sem=rs, device_id=device,
            device_id_type=MESH,
        )

    def send_pz(send_of, recv, ss, rs):
        for dx, dy in FAR_PZ:
            to = lax.rem(pz // 4 + dx, 2) * 4 + lax.rem(lax.rem(pz, 4) + dy, 4)
            remote(send_of(to), recv.at[pz], ss, rs, (py, to)).start()
        pltpu.make_async_copy(send_of(pz), recv.at[pz], rs).start()

    def send_py(send_of, recv, ss, rs):
        x, z, core = py // 16, lax.rem(py, 16) // 2, lax.rem(py, 2)
        for dx, dz, dc in FAR_PY:
            to = lax.rem(x + dx, 2) * 16 + lax.rem(z + dz, 8) * 2 + lax.rem(core + dc, 2)
            remote(send_of(to), recv.at[py], ss, rs, (to, pz)).start()
        pltpu.make_async_copy(send_of(py), recv.at[py], rs).start()

    def arrived(ref, sem):
        pltpu.make_async_copy(ref, ref, sem).wait()

    lane16 = lax.broadcasted_iota(jnp.int32, (16, LANES), 1)
    lane64 = lax.broadcasted_iota(jnp.int32, (64, LANES), 1)

    def halo_y_start(pad, n):
        up = lax.rem(py + 1, PY)
        down = lax.rem(py + PY - 1, PY)
        remote(pad.at[:, ROWS], pad.at[:, 0], halo_ss.at[n], halo_rs.at[n], (up, pz)).start()
        remote(
            pad.at[:, 1], pad.at[:, ROWS + 1], halo_ss.at[n + 1], halo_rs.at[n + 1], (down, pz)
        ).start()

    def halo_z_start(pad, n):
        arrived(pad.at[:, 0], halo_rs.at[n])
        arrived(pad.at[:, ROWS + 1], halo_rs.at[n + 1])
        s = n // 4
        halo_out[s, :, 24:, :] = jnp.zeros((2, 8, NX), f32)
        for j in range(3):
            for y in range(ROWS + 2):
                r = j * (ROWS + 2) + y
                halo_out[s, 0, r : r + 1, :] = pad[j, y, DEPTH - 1 : DEPTH, :]
                halo_out[s, 1, r : r + 1, :] = pad[j, y, 0:1, :]
        up = lax.rem(pz + 1, PZ)
        down = lax.rem(pz + PZ - 1, PZ)
        for side, to in ((0, up), (1, down)):
            remote(
                halo_out.at[s, side], halo_in.at[s, side], halo_ss.at[n + 2 + side],
                halo_rs.at[n + 2 + side], (py, to),
            ).start()

    def shifts(pad, out, n):
        s = n // 4
        arrived(halo_in.at[s, 0], halo_rs.at[n + 2])
        arrived(halo_in.at[s, 1], halo_rs.at[n + 3])
        row = lax.broadcasted_iota(jnp.int32, (DEPTH, NX), 0)
        for j in range(3):
            for y in range(ROWS + 2):
                r = j * (ROWS + 2) + y
                here = pad[j, y]
                below = jnp.where(row == 0, halo_in[s, 0, r : r + 1, :], pltpu.roll(here, 1, 0))
                above = jnp.where(
                    row == DEPTH - 1, halo_in[s, 1, r : r + 1, :], pltpu.roll(here, DEPTH - 1, 0)
                )
                for b, cells in enumerate((below, here, above)):
                    out[j * 9 + b * 3, y] = pltpu.roll(cells, 1, 1)
                    out[j * 9 + b * 3 + 1, y] = cells
                    out[j * 9 + b * 3 + 2, y] = pltpu.roll(cells, NX - 1, 1)

    def convolve_row(shifted, factor, y):
        def step(t, sums_here):
            sums_here = list(sums_here)
            for a in range(3):
                cells = shifted[t, y + a]
                for i in range(3):
                    sums_here[i] = sums_here[i] + factor(i, a, t) * cells
            return tuple(sums_here)

        zero = jnp.zeros((DEPTH, NX), f32)
        return lax.fori_loop(0, 27, step, (zero, zero, zero))

    def forward_factor(i, a, t):
        return weight[i, t // 9, a, (t // 3) % 3, t % 3]

    def backward_factor(i, a, t):
        return weight[t // 9, i, 2 - a, 2 - (t // 3) % 3, 2 - t % 3]

    def closure_rows(rows):
        for y in rows:
            for i, cells in enumerate(convolve_row(v_shift, forward_factor, y)):
                closure[i, y] = cells + bias[i]

    def grad_rows(rows):
        for y in rows:
            for i, cells in enumerate(convolve_row(m_shift, backward_factor, y)):
                closure[i, y] = cells

    def fold(cells):
        total = cells[0:8]
        for k in range(8, DEPTH, 8):
            total = total + cells[k : k + 8]
        return total[:, :LANES] + total[:, LANES:]

    def weight_parts(first, last):
        def one(t, _):
            def row(y, parts):
                parts = list(parts)
                for a in range(3):
                    cells = v_shift[t, y + a]
                    for i in range(3):
                        parts[i * 3 + a] = parts[i * 3 + a] + fold(m_pad[i, y + 1] * cells)
                return tuple(parts)

            zero = jnp.zeros((8, LANES), f32)
            parts = lax.fori_loop(0, ROWS, row, (zero,) * 9)
            at = t + (t // 9) * 18
            for i in range(3):
                for a in range(3):
                    w_parts[i * 81 + a * 9 + at] = parts[i * 3 + a]
            return 0

        lax.fori_loop(first, last, one, 0)

    def reduce_start():
        by_lane = jnp.sum(w_parts[...], axis=1)
        r_own[...] = jnp.sum(by_lane.T, axis=0, keepdims=True) * (1.0 / CELLS)
        send_pz(lambda to: r_own, r_pz, red_ss.at[0], red_rs.at[0])

    def reduce_next():
        arrived(r_pz, red_rs.at[0])
        total = r_pz[0]
        for k in range(1, PZ):
            total = total + r_pz[k]
        r_mid[...] = total
        send_py(lambda to: r_mid, r_py, red_ss.at[1], red_rs.at[1])

    def reduce_end():
        arrived(r_py, red_rs.at[1])
        total = r_py[0]
        for k in range(1, PY):
            total = total + r_py[k]
        sums[...] = total

    lane = lax.broadcasted_iota(jnp.int32, (MODES, LANES), 1)
    group = lane // 32
    kx = (pz * KL + py // 4).astype(f32) + jnp.zeros((MODES, LANES), f32)
    ky = (lax.broadcasted_iota(jnp.int32, (MODES, LANES), 0) - MODES // 2).astype(f32)
    kz = (lane % 32 + (py % 4) * 32 - MODES // 2).astype(f32)
    square = kx * kx + ky * ky + kz * kz

    def pick(first, second, third):
        return jnp.where(group == 0, first, jnp.where(group == 1, second, third))

    def next_one(cells):
        return jnp.where(group == 2, pltpu.roll(cells, 64, 1), pltpu.roll(cells, 96, 1))

    def next_two(cells):
        return jnp.where(group == 0, pltpu.roll(cells, 64, 1), pltpu.roll(cells, 32, 1))

    def turned(cells):
        return pick(ky, kz, kx) * next_two(cells) - pick(kz, kx, ky) * next_one(cells)

    def curl(real, imag):
        return -turned(imag), turned(real)

    def project(cells):
        along = pick(kx, ky, kz)
        part = along * cells
        part = part + next_one(part) + next_two(part)
        return cells - along * (part / jnp.maximum(square, 1.0))

    def out_pz(n, recv=None):
        recv = pz_recv.at[n] if recv is None else recv
        send_pz(lambda to: pz_send.at[n, to], recv, pz_ss.at[n], pz_rs.at[n])

    def out_py(n):
        send_py(lambda to: py_send.at[n, to], py_recv.at[n], py_ss.at[n], py_rs.at[n])

    def in_pz(n):
        arrived(pz_recv.at[n], pz_rs.at[n])

    def in_py(n):
        arrived(py_recv.at[n], py_rs.at[n])

    def x_stage(n, table):
        x_tiles(n, table, range(6))

    def x_tiles(n, table, tiles):
        for t in tiles:
            out = dot(table[...], field_in[t * 128 : (t + 1) * 128, :], ((1,), (1,)))
            out = out.astype(bf16)
            for p in range(PZ):
                pz_send[n, p, t] = out[p * 16 : (p + 1) * 16]

    def z_stage(n):
        in_pz(n)
        for t in range(6):
            for h in range(2):
                tiles = [pz_recv[n, 4 * h + g, t].astype(f32) for g in range(4)]
                for m, tile in enumerate(swap_groups(tiles, lane16)):
                    at = (m * 6 + t) * 16
                    z_in[at : at + 16, h * 128 : (h + 1) * 128] = tile.astype(bf16)
        for m in range(4):
            both = dot(z_in[m * 96 : (m + 1) * 96, :], z_out[...], ((1,), (0,)))
            for c in range(3):
                for h in range(2):
                    at = (c * 2 + h) * 16
                    r0 = both[at : at + 8]
                    r1 = both[at + 8 : at + 16]
                    y = h * 4 + m
                    stage[c, 0, pl.ds(y, 8, stride=8), :] = r0[:, :128] - r1[:, 128:]
                    stage[c, 1, pl.ds(y, 8, stride=8), :] = r0[:, 128:] + r1[:, :128]
        blocks = [
            swap_groups(
                [stage[0, q], stage[1, q], stage[2, q], jnp.zeros((64, LANES), f32)], lane64
            )
            for q in range(2)
        ]
        for g in range(4):
            for k in range(KL):
                py_send[n, k * 4 + g] = jnp.concatenate(
                    [blocks[0][g][k * 8 : k * 8 + 8], blocks[1][g][k * 8 : k * 8 + 8]], axis=0
                ).astype(bf16)

    def y_stage(n):
        in_py(n)
        return dot(y_out[...], py_recv[n].reshape(512, LANES), ((1,), (0,)))

    def y_back_stage(n, modes):
        rows = dot(y_back[...], modes, ((1,), (0,))).astype(bf16)
        for d in range(PY):
            py_send[n, d] = rows[d * 16 : (d + 1) * 16]

    def z_back_stage(n):
        in_py(n)
        for k in range(KL):
            tiles = [py_recv[n, k * 4 + g].astype(f32) for g in range(4)]
            for c, tile in enumerate(swap_groups(tiles, lane16)[:3]):
                at = c * 128 + k * 16
                z_in[at : at + 16, 0:128] = tile.astype(bf16)
        for c in range(3):
            both = dot(z_in[c * 128 : (c + 1) * 128, 0:128], z_back[...], ((1,), (0,)))
            for k in range(KL):
                r0 = both[k * 16 : k * 16 + 8]
                r1 = both[k * 16 + 8 : k * 16 + 16]
                for half in range(2):
                    re = slice(half * 128, half * 128 + 128)
                    im = slice(half * 128 + 256, half * 128 + 384)
                    spec_out[c, half, pl.ds(k, 8, stride=16), :] = r0[:, re] + r1[:, im]
                    spec_out[c, half, pl.ds(8 + k, 8, stride=16), :] = r1[:, re] - r0[:, im]
        for c in range(3):
            for h in range(2):
                for half in range(2):
                    tiles = [
                        spec_out[c, half, (h * 4 + m) * 16 : (h * 4 + m + 1) * 16]
                        for m in range(4)
                    ]
                    for g, tile in enumerate(swap_groups(tiles, lane16)):
                        pz_send[n, half * 4 + g, c * 2 + h] = tile.astype(bf16)

    def x_back_stage(n, table, out):
        in_pz(n)
        for t in range(6):
            block = pz_recv[n, :, t].reshape(128, LANES)
            out(t, dot(block, table[...], ((0,), (0,))))

    def keep(ref):
        def store(t, cells):
            ref[t * 128 : (t + 1) * 128, :] = cells

        return store

    def rows_of(c, y):
        at = (c * ROWS + y) * DEPTH
        return slice(at, at + DEPTH)

    def cross(left, right):
        return (
            left[1] * right[2] - left[2] * right[1],
            left[2] * right[0] - left[0] * right[2],
            left[0] * right[1] - left[1] * right[0],
        )

    loads[0].wait()
    for c in range(3):
        loads[1 + c].wait()
        for y in range(ROWS):
            field_in[rows_of(c, y), :] = v_pad[c, y + 1].astype(bf16)
        x_tiles(0, x_plain, (2 * c, 2 * c + 1))
    pl.semaphore_wait(barrier, PY - 1 + PZ - 1)
    out_pz(0)
    halo_y_start(v_pad, 0)
    for load in loads[4:]:
        load.wait()
    halo_z_start(v_pad, 0)
    z_stage(0)
    out_py(0)
    shifts(v_pad, v_shift, 0)
    modes = y_stage(0).astype(bf16)
    hat_v[...] = modes
    real, imag = curl(modes[:MODES].astype(f32), modes[MODES:].astype(f32))
    y_back_stage(1, jnp.concatenate([real, imag], axis=0).astype(bf16))
    out_py(1)
    closure_rows(range(0, 4))
    z_back_stage(1)
    out_pz(1)

    closure_rows(range(4, ROWS))
    for c in range(3):
        for y in range(ROWS):
            cells = v_pad[c, y + 1] + closure[c, y] - target[c, y]
            closure[c, y] = cells
            field_in[rows_of(c, y), :] = (time_step * cells).astype(bf16)
    x_stage(2, x_twice)
    x_back_stage(1, x_twice, keep(vort))
    for y in range(ROWS):
        here = [v_pad[c, y + 1] for c in range(3)]
        there = [vort[rows_of(c, y), :] for c in range(3)]
        for c, cells in enumerate(cross(here, there)):
            field_in[rows_of(c, y), :] = cells.astype(bf16)
    x_stage(3, x_plain)
    out_pz(3)
    out_pz(2)
    z_stage(3)
    out_py(3)
    z_stage(2)
    out_py(2)
    modes = y_stage(3).astype(bf16).astype(f32)
    drag = viscosity * square
    real = project(modes[:MODES]) - drag * hat_v[:MODES].astype(f32)
    imag = project(modes[MODES:]) - drag * hat_v[MODES:].astype(f32)
    rate_hat = jnp.concatenate([real, imag], axis=0).astype(bf16)
    twice = jnp.where(kx == 0.0, 1.0, 2.0) * (time_step * time_step)
    again = y_stage(2)
    real = (again[:MODES] + twice * rate_hat[:MODES].astype(f32)).astype(bf16)
    imag = (again[MODES:] + twice * rate_hat[MODES:].astype(f32)).astype(bf16)
    hat_r[:MODES] = real
    hat_r[MODES:] = imag
    modes = jnp.concatenate([project(real.astype(f32)), project(imag.astype(f32))], axis=0)
    y_back_stage(4, modes.astype(bf16))
    out_py(4)
    y_back_stage(5, rate_hat)
    out_py(5)
    z_back_stage(4)
    out_pz(4)
    z_back_stage(5)
    out_pz(5)

    x_back_stage(4, x_plain, keep(push))
    for y in range(ROWS):
        here = [v_pad[c, y + 1] for c in range(3)]
        there = [push[rows_of(c, y), :] for c in range(3)]
        for c, cells in enumerate(cross(there, here)):
            field_in[rows_of(c, y), :] = cells.astype(bf16)
    x_stage(6, x_twice)
    out_pz(6)

    parts = [jnp.zeros((8, LANES), f32) for _ in range(4)]

    def misfit(t, rate):
        c = t // 2
        for m in range(4):
            y = (t % 2) * 4 + m
            cells = closure[c, y] + time_step * rate[m * DEPTH : (m + 1) * DEPTH]
            m_pad[c, y + 1] = cells
            parts[c] = parts[c] + fold(cells)
            parts[3] = parts[3] + fold(cells * cells)

    x_back_stage(5, x_twice, misfit)
    halo_y_start(m_pad, 4)
    for c in range(3):
        w_parts[243 + c] = parts[c]
    w_parts[246] = 0.5 * parts[3]
    for k in range(247, 256):
        w_parts[k] = jnp.zeros((8, LANES), f32)
    z_stage(6)
    out_py(6)
    halo_z_start(m_pad, 4)
    weight_parts(0, 27)
    reduce_start()
    modes = y_stage(6).astype(bf16).astype(f32)
    real, imag = curl(modes[:MODES], modes[MODES:])
    real = real - drag * hat_r[:MODES].astype(f32)
    imag = imag - drag * hat_r[MODES:].astype(f32)
    y_back_stage(7, jnp.concatenate([real, imag], axis=0).astype(bf16))
    out_py(7)
    shifts(m_pad, m_shift, 4)
    reduce_next()
    z_back_stage(7)
    out_pz(7, last_recv)
    grad_rows(range(ROWS))
    for y in range(ROWS):
        here = [vort[rows_of(c, y), :] for c in range(3)]
        there = [push[rows_of(c, y), :] for c in range(3)]
        for c, cells in enumerate(cross(here, there)):
            closure[c, y] = closure[c, y] + m_pad[c, y + 1] + cells
    base = pltpu.make_async_copy(closure, base_out, base_sem)
    base.start()
    reduce_end()
    arrived(last_recv, pz_rs.at[7])

    for n in range(8):
        arrived(pz_send.at[n, 0 : PZ - 1], pz_ss.at[n])
        arrived(py_send.at[n, 0 : PY - 1], py_ss.at[n])
    for n in (0, 4):
        pad = v_pad if n == 0 else m_pad
        arrived(pad.at[:, 0], halo_ss.at[n])
        arrived(pad.at[:, 0], halo_ss.at[n + 1])
        arrived(halo_out.at[n // 4, 0], halo_ss.at[n + 2])
        arrived(halo_out.at[n // 4, 1], halo_ss.at[n + 3])
    arrived(r_pz.at[0 : PZ - 1], red_ss.at[0])
    arrived(r_py.at[0 : PY - 1], red_ss.at[1])
    base.wait()


def last_kernel(modes, base, table, sums, grad, grad_weight, grad_bias, loss):
    block = modes[...].reshape(128, LANES)
    cells = dot(block, table[...], ((0,), (0,)))
    for m in range(4):
        grad[0, m] = base[0, m] + cells[m * DEPTH : (m + 1) * DEPTH]

    @pl.when(pl.program_id(0) == 0)
    def _():
        def one(t, _):
            i, j, a = t // 27, (t // 9) % 3, (t // 3) % 3
            for e in range(3):
                grad_weight[i, j, a, t % 3, e] = sums[0, t * 3 + e]
            return 0

        lax.fori_loop(0, 81, one, 0)
        for i in range(3):
            grad_bias[i] = sums[0, 243 + i]
        loss[0] = sums[0, 246]


def on_device(velocity, target, closure_weight, closure_bias):
    shape = velocity.shape
    given = [jnp.asarray(t) for t in tables()]
    in_vmem = pl.BlockSpec(memory_space=pltpu.VMEM)
    in_smem = pl.BlockSpec(memory_space=pltpu.SMEM)
    dma = pltpu.SemaphoreType.DMA
    pad = (3, ROWS + 2, DEPTH, NX)
    in_hbm = pl.BlockSpec(memory_space=pl.ANY)
    landing = (PZ, 6, 16, LANES)
    base, modes, sums = pl.pallas_call(
        kernel,
        out_shape=(
            jax.ShapeDtypeStruct(shape, f32),
            jax.ShapeDtypeStruct(landing, bf16),
            jax.ShapeDtypeStruct((1, 256), f32),
        ),
        in_specs=[in_hbm, in_hbm, in_smem, in_smem] + [in_hbm] * 6,
        out_specs=(in_hbm, in_hbm, in_vmem),
        scratch_shapes=[pltpu.VMEM(t.shape, bf16) for t in given]
        + [
            pltpu.VMEM(shape, f32),
            pltpu.VMEM((8,) + landing, bf16),
            pltpu.VMEM((8,) + landing, bf16),
            pltpu.VMEM((8, PY, 16, LANES), bf16),
            pltpu.VMEM((8, PY, 16, LANES), bf16),
            pltpu.VMEM((768, NX), bf16),
            pltpu.VMEM((384, 256), bf16),
            pltpu.VMEM((3, 2, 64, LANES), f32),
            pltpu.VMEM((3, 2, 128, LANES), f32),
            pltpu.VMEM((768, NX), f32),
            pltpu.VMEM((768, NX), f32),
            pltpu.VMEM(pad, f32),
            pltpu.VMEM(pad, f32),
            pltpu.VMEM((27, ROWS + 2, DEPTH, NX), f32),
            pltpu.VMEM((27, ROWS + 2, DEPTH, NX), f32),
            pltpu.VMEM((3, ROWS, DEPTH, NX), f32),
            pltpu.VMEM((2, 2, 32, NX), f32),
            pltpu.VMEM((2, 2, 32, NX), f32),
            pltpu.VMEM((256, 8, LANES), f32),
            pltpu.VMEM((1, 256), f32),
            pltpu.VMEM((PZ, 1, 256), f32),
            pltpu.VMEM((1, 256), f32),
            pltpu.VMEM((PY, 1, 256), f32),
            pltpu.VMEM((256, LANES), bf16),
            pltpu.VMEM((256, LANES), bf16),
            dma((8,)), dma((8,)), dma((8,)), dma((8,)), dma((8,)), dma((8,)), dma((2,)), dma((2,)),
            dma((10,)), dma,
        ],
        compiler_params=pltpu.CompilerParams(
            collective_id=0, has_side_effects=True, vmem_limit_bytes=56 << 20
        ),
        name="euler",
    )(velocity, target, closure_weight, closure_bias, *given)
    half = pl.BlockSpec((1, 4, DEPTH, NX), lambda t: (t // 2, t % 2, 0, 0))
    grad, grad_weight, grad_bias, loss = pl.pallas_call(
        last_kernel,
        grid=(6,),
        out_shape=(
            jax.ShapeDtypeStruct(shape, f32),
            jax.ShapeDtypeStruct(closure_weight.shape, f32),
            jax.ShapeDtypeStruct((3,), f32),
            jax.ShapeDtypeStruct((1,), f32),
        ),
        in_specs=[
            pl.BlockSpec((PZ, 1, 16, LANES), lambda t: (0, t, 0, 0)),
            half,
            pl.BlockSpec((128, NX), lambda t: (0, 0)),
            in_smem,
        ],
        out_specs=(half, in_smem, in_smem, in_smem),
        name="last",
    )(modes, base, given[0], sums)
    return grad, grad_weight, grad_bias, loss.reshape(())


def solution(mesh):
    in_specs = (P(None, "py", "pz", None), P(None, "py", "pz", None), P(), P())
    out_specs = (P(None, "py", "pz", None), P(), P(), P())
    return jax.shard_map(
        on_device, mesh=mesh, in_specs=in_specs, out_specs=out_specs, check_vma=False
    )
```

```python
import functools
import math

import jax
import jax.numpy as jnp
import ml_dtypes
import numpy as np
from jax import lax
from jax.experimental import pallas as pl
from jax.experimental.pallas import tpu as pltpu
from jax.sharding import PartitionSpec as P

NX = 256
NY = 256
NZ = 256
PY = 32
PZ = 8
ROWS = NY // PY
DEPTH = NZ // PZ
KX = NX // 4
KL = KX // PZ
MODES = 128
LANES = 128
CELLS = float(NX * NY * NZ)
time_step = 0.01
viscosity = 0.002
MESH = pl.DeviceIdType.MESH
f32 = jnp.float32
bf16 = jnp.bfloat16


def ring(offset, length):
    return min(offset, length - offset)


FAR_PY = sorted(
    [(x, z, c) for x in range(2) for z in range(8) for c in range(2) if x + z + c > 0],
    key=lambda o: (-ring(o[1], 8) - o[0], o[1] > 4, o),
)
FAR_PZ = sorted(
    [(x, y) for x in range(2) for y in range(4) if x + y > 0],
    key=lambda o: (-ring(o[1], 4) - 2 * o[0], o),
)


def phases(positions, wavenumbers, length):
    turns = positions[:, None] * (wavenumbers[None, :] % length) % length
    angles = turns.astype(np.float32) * np.float32(2.0 * math.pi / length)
    return np.cos(angles), np.sin(angles)


def tables():
    factor = np.float32(1.0 / math.sqrt(NX))
    cosine, sine = phases(np.arange(NX), np.arange(KX), NX)
    pair = np.stack([factor * cosine, -factor * sine], axis=0)
    plain = pair.transpose(0, 2, 1).reshape(2, PZ, KL, NX).transpose(1, 0, 2, 3)
    plain = plain.reshape(2 * KX, NX)
    weights = np.where(np.arange(KX) == 0, 1.0, 2.0).astype(np.float32)
    weights = np.broadcast_to(weights.reshape(PZ, 1, KL), (PZ, 2, KL)).reshape(2 * KX, 1)
    wavenumbers = np.arange(MODES) - MODES // 2
    retained = (np.abs(wavenumbers) < MODES // 2).astype(np.float32)[None, :]
    cosine, sine = phases(np.arange(NZ), wavenumbers, NZ)
    real = factor * cosine * retained
    imag = -factor * sine * retained
    z_out = np.concatenate([real, imag], axis=1)
    z_back = np.concatenate([real.T, imag.T], axis=1)
    full = np.stack([np.stack([real, imag], 0), np.stack([-imag, real], 0)], 0)
    y_out = full.reshape(2, 2, PY, ROWS, MODES).transpose(1, 4, 2, 0, 3)
    y_out = y_out.reshape(2 * MODES, 2 * NY)
    given = (plain, plain * weights, z_out, z_back, y_out, y_out.T)
    return tuple(np.ascontiguousarray(t).astype(ml_dtypes.bfloat16) for t in given)


def swap_groups(tiles, lane):
    a0, a1, a2, a3 = tiles
    low = lane < 64
    b0 = jnp.where(low, a0, pltpu.roll(a2, 64, 1))
    b2 = jnp.where(low, pltpu.roll(a0, 64, 1), a2)
    b1 = jnp.where(low, a1, pltpu.roll(a3, 64, 1))
    b3 = jnp.where(low, pltpu.roll(a1, 64, 1), a3)
    even = (lane // 32) % 2 == 0
    c0 = jnp.where(even, b0, pltpu.roll(b1, 32, 1))
    c1 = jnp.where(even, pltpu.roll(b0, 96, 1), b1)
    c2 = jnp.where(even, b2, pltpu.roll(b3, 32, 1))
    c3 = jnp.where(even, pltpu.roll(b2, 96, 1), b3)
    return c0, c1, c2, c3


def dot(left, right, over):
    return lax.dot_general(left, right, (over, ((), ())), preferred_element_type=f32)


def kernel(
    vel_in, target_in, weight_in, bias, *refs,
):
    tables_in, refs = refs[:6], refs[6:]
    grad, grad_weight, grad_bias, loss = refs[:4]
    (x_plain, x_twice, z_out, z_back, y_out, y_back, target), refs = refs[4:11], refs[11:]
    (
        pz_send, pz_recv, py_send, py_recv, field_in, z_in, stage, spec_out,
        vort, push, v_pad, m_pad, v_shift, m_shift, closure, halo_out, halo_in,
        w_parts, r_own, r_pz, r_mid, r_py, hat_v, hat_r,
        pz_ss, pz_rs, py_ss, py_rs, halo_ss, halo_rs, red_ss, red_rs, in_sem, weight, flat,
    ) = refs
    py = lax.axis_index("py")
    pz = lax.axis_index("pz")

    barrier = pltpu.get_barrier_semaphore()

    def greet(k, _):
        pl.semaphore_signal(
            barrier, inc=1, device_id=(lax.rem(py + k, PY), pz), device_id_type=MESH
        )
        return 0

    lax.fori_loop(1, PY, greet, 0)
    for k in range(1, PZ):
        pl.semaphore_signal(
            barrier, inc=1, device_id=(py, lax.rem(pz + k, PZ)), device_id_type=MESH
        )

    loads = [pltpu.make_async_copy(tables_in[0], x_plain, in_sem.at[0])]
    for c in range(3):
        loads.append(
            pltpu.make_async_copy(
                vel_in.at[c], v_pad.at[c, pl.ds(1, ROWS)], in_sem.at[1 + c]
            )
        )
    later = ((2, z_out), (4, y_out), (5, y_back), (3, z_back), (1, x_twice))
    for k, (at, ref) in enumerate(later):
        loads.append(pltpu.make_async_copy(tables_in[at], ref, in_sem.at[4 + k]))
    loads.append(pltpu.make_async_copy(target_in, target, in_sem.at[9]))
    loads.append(pltpu.make_async_copy(weight_in, weight, in_sem.at[10]))
    for load in loads:
        load.start()

    def remote(src, dst, ss, rs, device):
        return pltpu.make_async_remote_copy(
            src_ref=src, dst_ref=dst, send_sem=ss, recv_sem=rs, device_id=device,
            device_id_type=MESH,
        )

    def send_pz(send_of, landing, ss, rs):
        for dx, dy in FAR_PZ:
            to = lax.rem(pz // 4 + dx, 2) * 4 + lax.rem(lax.rem(pz, 4) + dy, 4)
            remote(send_of(to), landing, ss, rs, (py, to)).start()
        pltpu.make_async_copy(send_of(pz), landing, rs).start()

    def send_py(send_of, recv, ss, rs):
        x, z, core = py // 16, lax.rem(py, 16) // 2, lax.rem(py, 2)
        for dx, dz, dc in FAR_PY:
            to = lax.rem(x + dx, 2) * 16 + lax.rem(z + dz, 8) * 2 + lax.rem(core + dc, 2)
            remote(send_of(to), recv.at[py], ss, rs, (to, pz)).start()
        pltpu.make_async_copy(send_of(py), recv.at[py], rs).start()

    def arrived(ref, sem):
        pltpu.make_async_copy(ref, ref, sem).wait()

    lane16 = lax.broadcasted_iota(jnp.int32, (16, LANES), 1)
    lane64 = lax.broadcasted_iota(jnp.int32, (64, LANES), 1)

    def halo_y_start(pad, n):
        up = lax.rem(py + 1, PY)
        down = lax.rem(py + PY - 1, PY)
        remote(pad.at[:, ROWS], pad.at[:, 0], halo_ss.at[n], halo_rs.at[n], (up, pz)).start()
        remote(
            pad.at[:, 1], pad.at[:, ROWS + 1], halo_ss.at[n + 1], halo_rs.at[n + 1], (down, pz)
        ).start()

    def halo_z_start(pad, n):
        arrived(pad.at[:, 0], halo_rs.at[n])
        arrived(pad.at[:, ROWS + 1], halo_rs.at[n + 1])
        s = n // 4
        halo_out[s, :, 24:, :] = jnp.zeros((2, 8, NX), f32)
        for j in range(3):
            for y in range(ROWS + 2):
                r = j * (ROWS + 2) + y
                halo_out[s, 0, r : r + 1, :] = pad[j, y, DEPTH - 1 : DEPTH, :]
                halo_out[s, 1, r : r + 1, :] = pad[j, y, 0:1, :]
        up = lax.rem(pz + 1, PZ)
        down = lax.rem(pz + PZ - 1, PZ)
        for side, to in ((0, up), (1, down)):
            remote(
                halo_out.at[s, side], halo_in.at[s, side], halo_ss.at[n + 2 + side],
                halo_rs.at[n + 2 + side], (py, to),
            ).start()

    def shifts(pad, out, n):
        s = n // 4
        arrived(halo_in.at[s, 0], halo_rs.at[n + 2])
        arrived(halo_in.at[s, 1], halo_rs.at[n + 3])
        row = lax.broadcasted_iota(jnp.int32, (DEPTH, NX), 0)
        for j in range(3):
            for y in range(ROWS + 2):
                r = j * (ROWS + 2) + y
                here = pad[j, y]
                below = jnp.where(row == 0, halo_in[s, 0, r : r + 1, :], pltpu.roll(here, 1, 0))
                above = jnp.where(
                    row == DEPTH - 1, halo_in[s, 1, r : r + 1, :], pltpu.roll(here, DEPTH - 1, 0)
                )
                for b, cells in enumerate((below, here, above)):
                    out[j * 9 + b * 3, y] = pltpu.roll(cells, 1, 1)
                    out[j * 9 + b * 3 + 1, y] = cells
                    out[j * 9 + b * 3 + 2, y] = pltpu.roll(cells, NX - 1, 1)

    def convolve_row(shifted, factor, y):
        def step(u, sums_here):
            sums_here = list(sums_here)
            for e in range(3):
                for a in range(3):
                    cells = shifted[u * 3 + e, y + a]
                    for i in range(3):
                        sums_here[i] = sums_here[i] + factor(i, a, u, e) * cells
            return tuple(sums_here)

        zero = jnp.zeros((DEPTH, NX), f32)
        return lax.fori_loop(0, 9, step, (zero, zero, zero))

    def flatten_weight():
        loads[10].wait()

        def one(t, _):
            for e in range(3):
                flat[t * 3 + e] = weight[t // 27, (t // 9) % 3, (t // 3) % 3, t % 3, e]
            return 0

        lax.fori_loop(0, 81, one, 0)

    def forward_factor(i, a, u, e):
        return flat[i * 81 + a * 9 + e + u * 3 + (u // 3) * 18]

    def backward_factor(i, a, u, e):
        return flat[i * 27 + (2 - a) * 9 + 8 - e + (u // 3) * 81 - (u % 3) * 3]

    def closure_rows(rows):
        for y in rows:
            for i, cells in enumerate(convolve_row(v_shift, forward_factor, y)):
                closure[i, y] = cells + bias[i]

    def grad_rows(rows):
        for y in rows:
            for i, cells in enumerate(convolve_row(m_shift, backward_factor, y)):
                closure[i, y] = cells

    def fold(cells):
        total = cells[0:8]
        for k in range(8, DEPTH, 8):
            total = total + cells[k : k + 8]
        return total[:, :LANES] + total[:, LANES:]

    def weight_parts(first, last):
        def one(t, _):
            def row(y, parts):
                parts = list(parts)
                for k in range(0, DEPTH, 8):
                    here = [m_pad[i, y + 1, k : k + 8] for i in range(3)]
                    for a in range(3):
                        cells = v_shift[t, y + a, k : k + 8]
                        for i in range(3):
                            parts[i * 3 + a] = parts[i * 3 + a] + here[i] * cells
                return tuple(parts)

            zero = jnp.zeros((8, NX), f32)
            parts = lax.fori_loop(0, ROWS, row, (zero,) * 9)
            at = t + (t // 9) * 18
            for i in range(3):
                for a in range(3):
                    both = parts[i * 3 + a]
                    w_parts[i * 81 + a * 9 + at] = both[:, :LANES] + both[:, LANES:]
            return 0

        lax.fori_loop(first, last, one, 0)

    def reduce_start():
        by_lane = jnp.sum(w_parts[...], axis=1)
        r_own[...] = jnp.sum(by_lane.T, axis=0, keepdims=True) * (1.0 / CELLS)
        send_pz(lambda to: r_own, r_pz.at[pz], red_ss.at[0], red_rs.at[0])

    def reduce_next():
        arrived(r_pz, red_rs.at[0])
        total = r_pz[0]
        for k in range(1, PZ):
            total = total + r_pz[k]
        r_mid[...] = total
        send_py(lambda to: r_mid, r_py, red_ss.at[1], red_rs.at[1])

    def reduce_end():
        arrived(r_py, red_rs.at[1])
        total = r_py[0]
        for k in range(1, PY):
            total = total + r_py[k]
        row = jnp.broadcast_to(total, (8, 256))
        for t in range(81):
            here = pltpu.roll(row, (256 - 3 * t) % 256, 1)
            i, j, a, b = t // 27, (t // 9) % 3, (t // 3) % 3, t % 3
            grad_weight[i, j, a, b : b + 1, :] = here[0:1, 0:3]
        at = lax.broadcasted_iota(jnp.int32, (1, 256), 1)
        for i in range(3):
            grad_bias[i] = jnp.sum(jnp.where(at == 243 + i, total, 0.0))
        loss[0] = jnp.sum(jnp.where(at == 246, total, 0.0))

    lane = lax.broadcasted_iota(jnp.int32, (MODES, LANES), 1)
    group = lane // 32
    kx = (pz * KL + py // 4).astype(f32) + jnp.zeros((MODES, LANES), f32)
    ky = (lax.broadcasted_iota(jnp.int32, (MODES, LANES), 0) - MODES // 2).astype(f32)
    kz = (lane % 32 + (py % 4) * 32 - MODES // 2).astype(f32)
    square = kx * kx + ky * ky + kz * kz

    def pick(first, second, third):
        return jnp.where(group == 0, first, jnp.where(group == 1, second, third))

    def next_one(cells):
        return jnp.where(group == 2, pltpu.roll(cells, 64, 1), pltpu.roll(cells, 96, 1))

    def next_two(cells):
        return jnp.where(group == 0, pltpu.roll(cells, 64, 1), pltpu.roll(cells, 32, 1))

    def turned(cells):
        return pick(ky, kz, kx) * next_two(cells) - pick(kz, kx, ky) * next_one(cells)

    def curl(real, imag):
        return -turned(imag), turned(real)

    def project(cells):
        along = pick(kx, ky, kz)
        part = along * cells
        part = part + next_one(part) + next_two(part)
        return cells - along * (part / jnp.maximum(square, 1.0))

    def out_pz(n, c):
        tiles = pl.ds(2 * c, 2)
        send_pz(
            lambda to: pz_send.at[n, to, tiles], pz_recv.at[n, pz, tiles], pz_ss.at[n],
            pz_rs.at[n, c],
        )

    def out_py(n):
        send_py(lambda to: py_send.at[n, to], py_recv.at[n], py_ss.at[n], py_rs.at[n])

    def in_pz(n, c):
        here = pz_recv.at[n, :, pl.ds(2 * c, 2)]
        arrived(here, pz_rs.at[n, c])

    def in_py(n):
        arrived(py_recv.at[n], py_rs.at[n])

    def x_stage(n, table):
        for c in range(3):
            x_tiles(n, table, c)
            out_pz(n, c)

    def x_tiles(n, table, c):
        for t in (2 * c, 2 * c + 1):
            out = dot(table[...], field_in[t * 128 : (t + 1) * 128, :], ((1,), (1,)))
            out = out.astype(bf16)
            for p in range(PZ):
                pz_send[n, p, t] = out[p * 16 : (p + 1) * 16]

    def z_stage(n):
        for c in range(3):
            in_pz(n, c)
            for yh in range(2):
                for h in range(2):
                    tiles = [pz_recv[n, 4 * h + g, 2 * c + yh].astype(f32) for g in range(4)]
                    for m, tile in enumerate(swap_groups(tiles, lane16)):
                        at = c * 128 + (yh * 4 + m) * 16
                        z_in[at : at + 16, h * 128 : (h + 1) * 128] = tile.astype(bf16)
            both = dot(z_in[c * 128 : (c + 1) * 128, :], z_out[...], ((1,), (0,)))
            for y in range(ROWS):
                r0 = both[y * 16 : y * 16 + 8]
                r1 = both[y * 16 + 8 : y * 16 + 16]
                stage[c, 0, pl.ds(y, 8, stride=8), :] = r0[:, :128] - r1[:, 128:]
                stage[c, 1, pl.ds(y, 8, stride=8), :] = r0[:, 128:] + r1[:, :128]
        blocks = [
            swap_groups(
                [stage[0, q], stage[1, q], stage[2, q], jnp.zeros((64, LANES), f32)], lane64
            )
            for q in range(2)
        ]
        for g in range(4):
            for k in range(KL):
                py_send[n, k * 4 + g] = jnp.concatenate(
                    [blocks[0][g][k * 8 : k * 8 + 8], blocks[1][g][k * 8 : k * 8 + 8]], axis=0
                ).astype(bf16)

    def y_stage(n):
        in_py(n)
        return dot(y_out[...], py_recv[n].reshape(512, LANES), ((1,), (0,)))

    def y_back_stage(n, modes):
        rows = dot(y_back[...], modes, ((1,), (0,))).astype(bf16)
        for d in range(PY):
            py_send[n, d] = rows[d * 16 : (d + 1) * 16]

    def z_back_stage(n):
        in_py(n)
        for k in range(KL):
            tiles = [py_recv[n, k * 4 + g].astype(f32) for g in range(4)]
            for c, tile in enumerate(swap_groups(tiles, lane16)[:3]):
                at = c * 128 + k * 16
                z_in[at : at + 16, 0:128] = tile.astype(bf16)
        for c in range(3):
            both = dot(z_in[c * 128 : (c + 1) * 128, 0:128], z_back[...], ((1,), (0,)))
            for k in range(KL):
                r0 = both[k * 16 : k * 16 + 8]
                r1 = both[k * 16 + 8 : k * 16 + 16]
                for half in range(2):
                    re = slice(half * 128, half * 128 + 128)
                    im = slice(half * 128 + 256, half * 128 + 384)
                    spec_out[c, half, pl.ds(k, 8, stride=16), :] = r0[:, re] + r1[:, im]
                    spec_out[c, half, pl.ds(8 + k, 8, stride=16), :] = r1[:, re] - r0[:, im]
            for h in range(2):
                for half in range(2):
                    tiles = [
                        spec_out[c, half, (h * 4 + m) * 16 : (h * 4 + m + 1) * 16]
                        for m in range(4)
                    ]
                    for g, tile in enumerate(swap_groups(tiles, lane16)):
                        pz_send[n, half * 4 + g, c * 2 + h] = tile.astype(bf16)
            out_pz(n, c)

    def x_back_stage(n, table, out):
        for c in range(3):
            in_pz(n, c)
            for t in (2 * c, 2 * c + 1):
                block = pz_recv[n, :, t].reshape(128, LANES)
                out(t, dot(block, table[...], ((0,), (0,))))

    def keep(ref):
        def store(t, cells):
            ref[t * 128 : (t + 1) * 128, :] = cells

        return store

    def rows_of(c, y):
        at = (c * ROWS + y) * DEPTH
        return slice(at, at + DEPTH)

    def cross(left, right):
        return (
            left[1] * right[2] - left[2] * right[1],
            left[2] * right[0] - left[0] * right[2],
            left[0] * right[1] - left[1] * right[0],
        )

    loads[0].wait()
    for c in range(3):
        loads[1 + c].wait()
        for y in range(ROWS):
            field_in[rows_of(c, y), :] = v_pad[c, y + 1].astype(bf16)
        x_tiles(0, x_plain, c)
    pl.semaphore_wait(barrier, PY - 1 + PZ - 1)
    for c in range(3):
        out_pz(0, c)
    halo_y_start(v_pad, 0)
    for load in loads[4:10]:
        load.wait()
    halo_z_start(v_pad, 0)
    z_stage(0)
    out_py(0)
    shifts(v_pad, v_shift, 0)
    flatten_weight()
    modes = y_stage(0).astype(bf16)
    hat_v[...] = modes
    real, imag = curl(modes[:MODES].astype(f32), modes[MODES:].astype(f32))
    y_back_stage(1, jnp.concatenate([real, imag], axis=0).astype(bf16))
    out_py(1)
    closure_rows(range(0, 4))
    z_back_stage(1)

    closure_rows(range(4, ROWS))
    for c in range(3):
        for y in range(ROWS):
            cells = v_pad[c, y + 1] + closure[c, y] - target[c, y]
            closure[c, y] = cells
            field_in[rows_of(c, y), :] = (time_step * cells).astype(bf16)
    x_stage(2, x_twice)
    x_back_stage(1, x_twice, keep(vort))
    for y in range(ROWS):
        here = [v_pad[c, y + 1] for c in range(3)]
        there = [vort[rows_of(c, y), :] for c in range(3)]
        for c, cells in enumerate(cross(here, there)):
            field_in[rows_of(c, y), :] = cells.astype(bf16)
    x_stage(3, x_plain)
    z_stage(2)
    out_py(2)
    z_stage(3)
    out_py(3)
    again = y_stage(2)
    modes = y_stage(3).astype(bf16).astype(f32)
    drag = viscosity * square
    real = project(modes[:MODES]) - drag * hat_v[:MODES].astype(f32)
    imag = project(modes[MODES:]) - drag * hat_v[MODES:].astype(f32)
    rate_hat = jnp.concatenate([real, imag], axis=0).astype(bf16)
    twice = jnp.where(kx == 0.0, 1.0, 2.0) * (time_step * time_step)
    real = (again[:MODES] + twice * rate_hat[:MODES].astype(f32)).astype(bf16)
    imag = (again[MODES:] + twice * rate_hat[MODES:].astype(f32)).astype(bf16)
    hat_r[:MODES] = real
    hat_r[MODES:] = imag
    modes = jnp.concatenate([project(real.astype(f32)), project(imag.astype(f32))], axis=0)
    y_back_stage(4, modes.astype(bf16))
    out_py(4)
    y_back_stage(5, rate_hat)
    out_py(5)
    z_back_stage(4)
    z_back_stage(5)

    x_back_stage(4, x_plain, keep(push))
    for y in range(ROWS):
        here = [v_pad[c, y + 1] for c in range(3)]
        there = [push[rows_of(c, y), :] for c in range(3)]
        for c, cells in enumerate(cross(there, here)):
            field_in[rows_of(c, y), :] = cells.astype(bf16)
    x_stage(6, x_twice)

    parts = [jnp.zeros((8, LANES), f32) for _ in range(4)]

    def misfit(t, rate):
        c = t // 2
        for m in range(4):
            y = (t % 2) * 4 + m
            cells = closure[c, y] + time_step * rate[m * DEPTH : (m + 1) * DEPTH]
            m_pad[c, y + 1] = cells
            parts[c] = parts[c] + fold(cells)
            parts[3] = parts[3] + fold(cells * cells)

    x_back_stage(5, x_twice, misfit)
    halo_y_start(m_pad, 4)
    for c in range(3):
        w_parts[243 + c] = parts[c]
    w_parts[246] = 0.5 * parts[3]
    for k in range(247, 256):
        w_parts[k] = jnp.zeros((8, LANES), f32)
    weight_parts(0, 10)
    z_stage(6)
    out_py(6)
    halo_z_start(m_pad, 4)
    weight_parts(10, 27)
    reduce_start()
    modes = y_stage(6).astype(bf16).astype(f32)
    real, imag = curl(modes[:MODES], modes[MODES:])
    real = real - drag * hat_r[:MODES].astype(f32)
    imag = imag - drag * hat_r[MODES:].astype(f32)
    y_back_stage(7, jnp.concatenate([real, imag], axis=0).astype(bf16))
    out_py(7)
    shifts(m_pad, m_shift, 4)
    grad_rows(range(0, 2))
    reduce_next()
    z_back_stage(7)
    grad_rows(range(2, ROWS))
    for y in range(ROWS):
        here = [vort[rows_of(c, y), :] for c in range(3)]
        there = [push[rows_of(c, y), :] for c in range(3)]
        for c, cells in enumerate(cross(here, there)):
            closure[c, y] = closure[c, y] + m_pad[c, y + 1] + cells
    reduce_end()

    def finish(t, cells):
        for m in range(4):
            y = (t % 2) * 4 + m
            grad[t // 2, y] = closure[t // 2, y] + cells[m * DEPTH : (m + 1) * DEPTH]

    x_back_stage(7, x_plain, finish)

    for n in range(8):
        arrived(pz_send.at[n, 0 : PZ - 1], pz_ss.at[n])
        arrived(py_send.at[n, 0 : PY - 1], py_ss.at[n])
    for n in (0, 4):
        pad = v_pad if n == 0 else m_pad
        arrived(pad.at[:, 0], halo_ss.at[n])
        arrived(pad.at[:, 0], halo_ss.at[n + 1])
        arrived(halo_out.at[n // 4, 0], halo_ss.at[n + 2])
        arrived(halo_out.at[n // 4, 1], halo_ss.at[n + 3])
    arrived(r_pz.at[0 : PZ - 1], red_ss.at[0])
    arrived(r_py.at[0 : PY - 1], red_ss.at[1])


def on_device(velocity, target, closure_weight, closure_bias):
    shape = velocity.shape
    given = [jnp.asarray(t) for t in tables()]
    in_vmem = pl.BlockSpec(memory_space=pltpu.VMEM)
    in_smem = pl.BlockSpec(memory_space=pltpu.SMEM)
    dma = pltpu.SemaphoreType.DMA
    pad = (3, ROWS + 2, DEPTH, NX)
    in_hbm = pl.BlockSpec(memory_space=pl.ANY)
    landing = (PZ, 6, 16, LANES)
    grad, grad_weight, grad_bias, loss = pl.pallas_call(
        kernel,
        out_shape=(
            jax.ShapeDtypeStruct(shape, f32),
            jax.ShapeDtypeStruct(closure_weight.shape, f32),
            jax.ShapeDtypeStruct((3,), f32),
            jax.ShapeDtypeStruct((1,), f32),
        ),
        in_specs=[in_hbm, in_hbm, in_hbm, in_smem] + [in_hbm] * 6,
        out_specs=(in_vmem, in_vmem, in_smem, in_smem),
        scratch_shapes=[pltpu.VMEM(t.shape, bf16) for t in given]
        + [
            pltpu.VMEM(shape, f32),
            pltpu.VMEM((8,) + landing, bf16),
            pltpu.VMEM((8,) + landing, bf16),
            pltpu.VMEM((8, PY, 16, LANES), bf16),
            pltpu.VMEM((8, PY, 16, LANES), bf16),
            pltpu.VMEM((768, NX), bf16),
            pltpu.VMEM((384, 256), bf16),
            pltpu.VMEM((3, 2, 64, LANES), f32),
            pltpu.VMEM((3, 2, 128, LANES), f32),
            pltpu.VMEM((768, NX), f32),
            pltpu.VMEM((768, NX), f32),
            pltpu.VMEM(pad, f32),
            pltpu.VMEM(pad, f32),
            pltpu.VMEM((27, ROWS + 2, DEPTH, NX), f32),
            pltpu.VMEM((27, ROWS + 2, DEPTH, NX), f32),
            pltpu.VMEM((3, ROWS, DEPTH, NX), f32),
            pltpu.VMEM((2, 2, 32, NX), f32),
            pltpu.VMEM((2, 2, 32, NX), f32),
            pltpu.VMEM((256, 8, LANES), f32),
            pltpu.VMEM((1, 256), f32),
            pltpu.VMEM((PZ, 1, 256), f32),
            pltpu.VMEM((1, 256), f32),
            pltpu.VMEM((PY, 1, 256), f32),
            pltpu.VMEM((256, LANES), bf16),
            pltpu.VMEM((256, LANES), bf16),
            dma((8,)), dma((8, 3)), dma((8,)), dma((8,)), dma((8,)), dma((8,)), dma((2,)), dma((2,)),
            dma((11,)), pltpu.SMEM(closure_weight.shape, f32),
            pltpu.SMEM((243,), f32),
        ],
        compiler_params=pltpu.CompilerParams(
            collective_id=0, has_side_effects=True, vmem_limit_bytes=56 << 20
        ),
        name="euler",
    )(velocity, target, closure_weight, closure_bias, *given)
    return grad, grad_weight, grad_bias, loss.reshape(())


def solution(mesh):
    in_specs = (P(None, "py", "pz", None), P(None, "py", "pz", None), P(), P())
    out_specs = (P(None, "py", "pz", None), P(), P(), P())
    return jax.shard_map(
        on_device, mesh=mesh, in_specs=in_specs, out_specs=out_specs, check_vma=False
    )
```

```python
import functools
import math

import jax
import jax.numpy as jnp
import ml_dtypes
import numpy as np
from jax import lax
from jax.experimental import pallas as pl
from jax.experimental.pallas import tpu as pltpu
from jax.sharding import PartitionSpec as P

NX = 256
NY = 256
NZ = 256
PY = 32
PZ = 8
ROWS = NY // PY
DEPTH = NZ // PZ
KX = NX // 4
KL = KX // PZ
MODES = 128
LANES = 128
CELLS = float(NX * NY * NZ)
time_step = 0.01
viscosity = 0.002
MESH = pl.DeviceIdType.MESH
f32 = jnp.float32
bf16 = jnp.bfloat16


def ring(offset, length):
    return min(offset, length - offset)


FAR_PY = sorted(
    [(x, z, c) for x in range(2) for z in range(8) for c in range(2) if x + z + c > 0],
    key=lambda o: (-ring(o[1], 8) - o[0], o[1] > 4, o),
)
FAR_PZ = sorted(
    [(x, y) for x in range(2) for y in range(4) if x + y > 0],
    key=lambda o: (-ring(o[1], 4) - 2 * o[0], o),
)


def phases(positions, wavenumbers, length):
    turns = positions[:, None] * (wavenumbers[None, :] % length) % length
    angles = turns.astype(np.float32) * np.float32(2.0 * math.pi / length)
    return np.cos(angles), np.sin(angles)


def tables():
    factor = np.float32(1.0 / math.sqrt(NX))
    cosine, sine = phases(np.arange(NX), np.arange(KX), NX)
    pair = np.stack([factor * cosine, -factor * sine], axis=0)
    plain = pair.transpose(0, 2, 1).reshape(2, PZ, KL, NX).transpose(1, 0, 2, 3)
    plain = plain.reshape(2 * KX, NX)
    weights = np.where(np.arange(KX) == 0, 1.0, 2.0).astype(np.float32)
    weights = np.broadcast_to(weights.reshape(PZ, 1, KL), (PZ, 2, KL)).reshape(2 * KX, 1)
    wavenumbers = np.arange(MODES) - MODES // 2
    retained = (np.abs(wavenumbers) < MODES // 2).astype(np.float32)[None, :]
    cosine, sine = phases(np.arange(NZ), wavenumbers, NZ)
    real = factor * cosine * retained
    imag = -factor * sine * retained
    z_out = np.concatenate([real, imag], axis=1)
    z_back = np.concatenate([real.T, imag.T], axis=1)
    full = np.stack([np.stack([real, imag], 0), np.stack([-imag, real], 0)], 0)
    y_out = full.reshape(2, 2, PY, ROWS, MODES).transpose(1, 4, 2, 0, 3)
    y_out = y_out.reshape(2 * MODES, 2 * NY)
    given = (plain, plain * weights, z_out, z_back, y_out, y_out.T)
    return tuple(np.ascontiguousarray(t).astype(ml_dtypes.bfloat16) for t in given)


def swap_groups(tiles, lane):
    a0, a1, a2, a3 = tiles
    low = lane < 64
    b0 = jnp.where(low, a0, pltpu.roll(a2, 64, 1))
    b2 = jnp.where(low, pltpu.roll(a0, 64, 1), a2)
    b1 = jnp.where(low, a1, pltpu.roll(a3, 64, 1))
    b3 = jnp.where(low, pltpu.roll(a1, 64, 1), a3)
    even = (lane // 32) % 2 == 0
    c0 = jnp.where(even, b0, pltpu.roll(b1, 32, 1))
    c1 = jnp.where(even, pltpu.roll(b0, 96, 1), b1)
    c2 = jnp.where(even, b2, pltpu.roll(b3, 32, 1))
    c3 = jnp.where(even, pltpu.roll(b2, 96, 1), b3)
    return c0, c1, c2, c3


def dot(left, right, over):
    return lax.dot_general(left, right, (over, ((), ())), preferred_element_type=f32)


def kernel(
    vel_in, target_in, weight_in, bias, *refs,
):
    tables_in, refs = refs[:6], refs[6:]
    grad, grad_weight, grad_bias, loss = refs[:4]
    (x_plain, x_twice, z_out, z_back, y_out, y_back, target), refs = refs[4:11], refs[11:]
    (
        pz_send, pz_recv, py_send, py_recv, field_in, z_in, stage, spec_out,
        vort, push, v_pad, m_pad, v_shift, m_shift, closure, halo_out, halo_in,
        w_parts, r_own, r_pz, r_mid, r_py, hat_v, hat_r,
        pz_ss, pz_rs, py_ss, py_rs, halo_ss, halo_rs, red_ss, red_rs, in_sem, weight, flat,
    ) = refs
    py = lax.axis_index("py")
    pz = lax.axis_index("pz")

    barrier = pltpu.get_barrier_semaphore()

    def greet(k, _):
        pl.semaphore_signal(
            barrier, inc=1, device_id=(lax.rem(py + k, PY), pz), device_id_type=MESH
        )
        return 0

    lax.fori_loop(1, PY, greet, 0)
    for k in range(1, PZ):
        pl.semaphore_signal(
            barrier, inc=1, device_id=(py, lax.rem(pz + k, PZ)), device_id_type=MESH
        )

    loads = [pltpu.make_async_copy(tables_in[0], x_plain, in_sem.at[0])]
    for c in range(3):
        loads.append(
            pltpu.make_async_copy(
                vel_in.at[c], v_pad.at[c, pl.ds(1, ROWS)], in_sem.at[1 + c]
            )
        )
    later = ((2, z_out), (4, y_out), (5, y_back), (3, z_back), (1, x_twice))
    for k, (at, ref) in enumerate(later):
        loads.append(pltpu.make_async_copy(tables_in[at], ref, in_sem.at[4 + k]))
    loads.append(pltpu.make_async_copy(target_in, target, in_sem.at[9]))
    loads.append(pltpu.make_async_copy(weight_in, weight, in_sem.at[10]))
    for load in loads:
        load.start()

    def remote(src, dst, ss, rs, device):
        return pltpu.make_async_remote_copy(
            src_ref=src, dst_ref=dst, send_sem=ss, recv_sem=rs, device_id=device,
            device_id_type=MESH,
        )

    def send_pz(send_of, landing, ss, rs):
        for dx, dy in FAR_PZ:
            to = lax.rem(pz // 4 + dx, 2) * 4 + lax.rem(lax.rem(pz, 4) + dy, 4)
            remote(send_of(to), landing, ss, rs, (py, to)).start()
        pltpu.make_async_copy(send_of(pz), landing, rs).start()

    def send_py(send_of, recv, ss, rs):
        x, z, core = py // 16, lax.rem(py, 16) // 2, lax.rem(py, 2)
        for dx, dz, dc in FAR_PY:
            to = lax.rem(x + dx, 2) * 16 + lax.rem(z + dz, 8) * 2 + lax.rem(core + dc, 2)
            remote(send_of(to), recv.at[py], ss, rs, (to, pz)).start()
        pltpu.make_async_copy(send_of(py), recv.at[py], rs).start()

    def arrived(ref, sem):
        pltpu.make_async_copy(ref, ref, sem).wait()

    lane16 = lax.broadcasted_iota(jnp.int32, (16, LANES), 1)
    lane64 = lax.broadcasted_iota(jnp.int32, (64, LANES), 1)

    def halo_y_start(pad, n):
        up = lax.rem(py + 1, PY)
        down = lax.rem(py + PY - 1, PY)
        remote(pad.at[:, ROWS], pad.at[:, 0], halo_ss.at[n], halo_rs.at[n], (up, pz)).start()
        remote(
            pad.at[:, 1], pad.at[:, ROWS + 1], halo_ss.at[n + 1], halo_rs.at[n + 1], (down, pz)
        ).start()

    def halo_z_start(pad, n):
        arrived(pad.at[:, 0], halo_rs.at[n])
        arrived(pad.at[:, ROWS + 1], halo_rs.at[n + 1])
        s = n // 4
        halo_out[s, :, 24:, :] = jnp.zeros((2, 8, NX), f32)
        for j in range(3):
            for y in range(ROWS + 2):
                r = j * (ROWS + 2) + y
                halo_out[s, 0, r : r + 1, :] = pad[j, y, DEPTH - 1 : DEPTH, :]
                halo_out[s, 1, r : r + 1, :] = pad[j, y, 0:1, :]
        up = lax.rem(pz + 1, PZ)
        down = lax.rem(pz + PZ - 1, PZ)
        for side, to in ((0, up), (1, down)):
            remote(
                halo_out.at[s, side], halo_in.at[s, side], halo_ss.at[n + 2 + side],
                halo_rs.at[n + 2 + side], (py, to),
            ).start()

    def shifts(pad, out, n):
        s = n // 4
        arrived(halo_in.at[s, 0], halo_rs.at[n + 2])
        arrived(halo_in.at[s, 1], halo_rs.at[n + 3])
        row = lax.broadcasted_iota(jnp.int32, (DEPTH, NX), 0)
        for j in range(3):
            for y in range(ROWS + 2):
                r = j * (ROWS + 2) + y
                here = pad[j, y]
                below = jnp.where(row == 0, halo_in[s, 0, r : r + 1, :], pltpu.roll(here, 1, 0))
                above = jnp.where(
                    row == DEPTH - 1, halo_in[s, 1, r : r + 1, :], pltpu.roll(here, DEPTH - 1, 0)
                )
                for b, cells in enumerate((below, here, above)):
                    out[j * 9 + b * 3, y] = pltpu.roll(cells, 1, 1)
                    out[j * 9 + b * 3 + 1, y] = cells
                    out[j * 9 + b * 3 + 2, y] = pltpu.roll(cells, NX - 1, 1)

    def convolve_row(shifted, factor, y):
        def step(u, sums_here):
            sums_here = list(sums_here)
            for e in range(3):
                for a in range(3):
                    cells = shifted[u * 3 + e, y + a]
                    for i in range(3):
                        sums_here[i] = sums_here[i] + factor(i, a, u, e) * cells
            return tuple(sums_here)

        zero = jnp.zeros((DEPTH, NX), f32)
        return lax.fori_loop(0, 9, step, (zero, zero, zero))

    def flatten_weight():
        loads[10].wait()

        def one(t, _):
            for e in range(3):
                flat[t * 3 + e] = weight[t // 27, (t // 9) % 3, (t // 3) % 3, t % 3, e]
            return 0

        lax.fori_loop(0, 81, one, 0)

    def forward_factor(i, a, u, e):
        return flat[i * 81 + a * 9 + e + u * 3 + (u // 3) * 18]

    def backward_factor(i, a, u, e):
        return flat[i * 27 + (2 - a) * 9 + 8 - e + (u // 3) * 81 - (u % 3) * 3]

    def closure_rows(rows):
        for y in rows:
            for i, cells in enumerate(convolve_row(v_shift, forward_factor, y)):
                closure[i, y] = cells + bias[i]

    def grad_rows(rows):
        for y in rows:
            for i, cells in enumerate(convolve_row(m_shift, backward_factor, y)):
                closure[i, y] = cells

    def fold(cells):
        total = cells[0:8]
        for k in range(8, DEPTH, 8):
            total = total + cells[k : k + 8]
        return total[:, :LANES] + total[:, LANES:]

    def weight_parts(first, last):
        def one(t, _):
            def row(y, parts):
                parts = list(parts)
                for k in range(0, DEPTH, 8):
                    here = [m_pad[i, y + 1, k : k + 8] for i in range(3)]
                    for a in range(3):
                        cells = v_shift[t, y + a, k : k + 8]
                        for i in range(3):
                            parts[i * 3 + a] = parts[i * 3 + a] + here[i] * cells
                return tuple(parts)

            zero = jnp.zeros((8, NX), f32)
            parts = lax.fori_loop(0, ROWS, row, (zero,) * 9)
            at = t + (t // 9) * 18
            for i in range(3):
                for a in range(3):
                    both = parts[i * 3 + a]
                    w_parts[i * 81 + a * 9 + at] = both[:, :LANES] + both[:, LANES:]
            return 0

        lax.fori_loop(first, last, one, 0)

    def reduce_start():
        by_lane = jnp.sum(w_parts[...], axis=1)
        r_own[...] = jnp.sum(by_lane.T, axis=0, keepdims=True) * (1.0 / CELLS)
        send_pz(lambda to: r_own, r_pz.at[pz], red_ss.at[0], red_rs.at[0])

    def reduce_next():
        arrived(r_pz, red_rs.at[0])
        total = r_pz[0]
        for k in range(1, PZ):
            total = total + r_pz[k]
        r_mid[...] = total
        send_py(lambda to: r_mid, r_py, red_ss.at[1], red_rs.at[1])

    def reduce_end():
        arrived(r_py, red_rs.at[1])
        total = r_py[0]
        for k in range(1, PY):
            total = total + r_py[k]
        row = jnp.broadcast_to(total, (8, 256))
        for t in range(81):
            here = pltpu.roll(row, (256 - 3 * t) % 256, 1)
            i, j, a, b = t // 27, (t // 9) % 3, (t // 3) % 3, t % 3
            grad_weight[i, j, a, b : b + 1, :] = here[0:1, 0:3]
        at = lax.broadcasted_iota(jnp.int32, (1, 256), 1)
        for i in range(3):
            grad_bias[i] = jnp.sum(jnp.where(at == 243 + i, total, 0.0))
        loss[0] = jnp.sum(jnp.where(at == 246, total, 0.0))

    lane = lax.broadcasted_iota(jnp.int32, (MODES, LANES), 1)
    group = lane // 32
    kx = (pz * KL + py // 4).astype(f32) + jnp.zeros((MODES, LANES), f32)
    ky = (lax.broadcasted_iota(jnp.int32, (MODES, LANES), 0) - MODES // 2).astype(f32)
    kz = (lane % 32 + (py % 4) * 32 - MODES // 2).astype(f32)
    square = kx * kx + ky * ky + kz * kz

    def pick(first, second, third):
        return jnp.where(group == 0, first, jnp.where(group == 1, second, third))

    def next_one(cells):
        return jnp.where(group == 2, pltpu.roll(cells, 64, 1), pltpu.roll(cells, 96, 1))

    def next_two(cells):
        return jnp.where(group == 0, pltpu.roll(cells, 64, 1), pltpu.roll(cells, 32, 1))

    def turned(cells):
        return pick(ky, kz, kx) * next_two(cells) - pick(kz, kx, ky) * next_one(cells)

    def curl(real, imag):
        return -turned(imag), turned(real)

    def project(cells):
        along = pick(kx, ky, kz)
        part = along * cells
        part = part + next_one(part) + next_two(part)
        return cells - along * (part / jnp.maximum(square, 1.0))

    def out_pz(n):
        send_pz(lambda to: pz_send.at[n, to], pz_recv.at[n, pz], pz_ss.at[n], pz_rs.at[n])

    def out_py(n):
        send_py(lambda to: py_send.at[n, to], py_recv.at[n], py_ss.at[n], py_rs.at[n])

    def in_pz(n):
        arrived(pz_recv.at[n], pz_rs.at[n])

    def in_py(n):
        arrived(py_recv.at[n], py_rs.at[n])

    def x_stage(n, table):
        for c in range(3):
            x_tiles(n, table, c)
        out_pz(n)

    def x_tiles(n, table, c):
        for t in (2 * c, 2 * c + 1):
            out = dot(table[...], field_in[t * 128 : (t + 1) * 128, :], ((1,), (1,)))
            out = out.astype(bf16)
            for p in range(PZ):
                pz_send[n, p, t] = out[p * 16 : (p + 1) * 16]

    def z_stage(n):
        in_pz(n)
        for c in range(3):
            for yh in range(2):
                for h in range(2):
                    tiles = [pz_recv[n, 4 * h + g, 2 * c + yh].astype(f32) for g in range(4)]
                    for m, tile in enumerate(swap_groups(tiles, lane16)):
                        at = c * 128 + (yh * 4 + m) * 16
                        z_in[at : at + 16, h * 128 : (h + 1) * 128] = tile.astype(bf16)
            both = dot(z_in[c * 128 : (c + 1) * 128, :], z_out[...], ((1,), (0,)))
            for y in range(ROWS):
                r0 = both[y * 16 : y * 16 + 8]
                r1 = both[y * 16 + 8 : y * 16 + 16]
                stage[c, 0, pl.ds(y, 8, stride=8), :] = r0[:, :128] - r1[:, 128:]
                stage[c, 1, pl.ds(y, 8, stride=8), :] = r0[:, 128:] + r1[:, :128]
        blocks = [
            swap_groups(
                [stage[0, q], stage[1, q], stage[2, q], jnp.zeros((64, LANES), f32)], lane64
            )
            for q in range(2)
        ]
        for g in range(4):
            for k in range(KL):
                py_send[n, k * 4 + g] = jnp.concatenate(
                    [blocks[0][g][k * 8 : k * 8 + 8], blocks[1][g][k * 8 : k * 8 + 8]], axis=0
                ).astype(bf16)

    def y_stage(n):
        in_py(n)
        return dot(y_out[...], py_recv[n].reshape(512, LANES), ((1,), (0,)))

    def y_back_stage(n, modes):
        rows = dot(y_back[...], modes, ((1,), (0,))).astype(bf16)
        for d in range(PY):
            py_send[n, d] = rows[d * 16 : (d + 1) * 16]

    def z_back_stage(n):
        in_py(n)
        for k in range(KL):
            tiles = [py_recv[n, k * 4 + g].astype(f32) for g in range(4)]
            for c, tile in enumerate(swap_groups(tiles, lane16)[:3]):
                at = c * 128 + k * 16
                z_in[at : at + 16, 0:128] = tile.astype(bf16)
        for c in range(3):
            both = dot(z_in[c * 128 : (c + 1) * 128, 0:128], z_back[...], ((1,), (0,)))
            for k in range(KL):
                r0 = both[k * 16 : k * 16 + 8]
                r1 = both[k * 16 + 8 : k * 16 + 16]
                for half in range(2):
                    re = slice(half * 128, half * 128 + 128)
                    im = slice(half * 128 + 256, half * 128 + 384)
                    spec_out[c, half, pl.ds(k, 8, stride=16), :] = r0[:, re] + r1[:, im]
                    spec_out[c, half, pl.ds(8 + k, 8, stride=16), :] = r1[:, re] - r0[:, im]
            for h in range(2):
                for half in range(2):
                    tiles = [
                        spec_out[c, half, (h * 4 + m) * 16 : (h * 4 + m + 1) * 16]
                        for m in range(4)
                    ]
                    for g, tile in enumerate(swap_groups(tiles, lane16)):
                        pz_send[n, half * 4 + g, c * 2 + h] = tile.astype(bf16)
        out_pz(n)

    def x_back_stage(n, table, out):
        in_pz(n)
        for c in range(3):
            for t in (2 * c, 2 * c + 1):
                block = pz_recv[n, :, t].reshape(128, LANES)
                out(t, dot(block, table[...], ((0,), (0,))))

    def keep(ref):
        def store(t, cells):
            ref[t * 128 : (t + 1) * 128, :] = cells

        return store

    def rows_of(c, y):
        at = (c * ROWS + y) * DEPTH
        return slice(at, at + DEPTH)

    def cross(left, right):
        return (
            left[1] * right[2] - left[2] * right[1],
            left[2] * right[0] - left[0] * right[2],
            left[0] * right[1] - left[1] * right[0],
        )

    loads[0].wait()
    for c in range(3):
        loads[1 + c].wait()
        for y in range(ROWS):
            field_in[rows_of(c, y), :] = v_pad[c, y + 1].astype(bf16)
        x_tiles(0, x_plain, c)
    pl.semaphore_wait(barrier, PY - 1 + PZ - 1)
    out_pz(0)
    halo_y_start(v_pad, 0)
    for load in loads[4:10]:
        load.wait()
    halo_z_start(v_pad, 0)
    z_stage(0)
    out_py(0)
    shifts(v_pad, v_shift, 0)
    flatten_weight()
    modes = y_stage(0).astype(bf16)
    hat_v[...] = modes
    real, imag = curl(modes[:MODES].astype(f32), modes[MODES:].astype(f32))
    y_back_stage(1, jnp.concatenate([real, imag], axis=0).astype(bf16))
    out_py(1)
    closure_rows(range(ROWS))
    z_back_stage(1)

    for c in range(3):
        for y in range(ROWS):
            cells = v_pad[c, y + 1] + closure[c, y] - target[c, y]
            closure[c, y] = cells
            field_in[rows_of(c, y), :] = (time_step * cells).astype(bf16)
    x_stage(2, x_twice)
    x_back_stage(1, x_twice, keep(vort))
    for y in range(ROWS):
        here = [v_pad[c, y + 1] for c in range(3)]
        there = [vort[rows_of(c, y), :] for c in range(3)]
        for c, cells in enumerate(cross(here, there)):
            field_in[rows_of(c, y), :] = cells.astype(bf16)
    x_stage(3, x_plain)
    z_stage(2)
    out_py(2)
    z_stage(3)
    out_py(3)
    again = y_stage(2)
    modes = y_stage(3).astype(bf16).astype(f32)
    drag = viscosity * square
    real = project(modes[:MODES]) - drag * hat_v[:MODES].astype(f32)
    imag = project(modes[MODES:]) - drag * hat_v[MODES:].astype(f32)
    rate_hat = jnp.concatenate([real, imag], axis=0).astype(bf16)
    twice = jnp.where(kx == 0.0, 1.0, 2.0) * (time_step * time_step)
    real = (again[:MODES] + twice * rate_hat[:MODES].astype(f32)).astype(bf16)
    imag = (again[MODES:] + twice * rate_hat[MODES:].astype(f32)).astype(bf16)
    hat_r[:MODES] = real
    hat_r[MODES:] = imag
    modes = jnp.concatenate([project(real.astype(f32)), project(imag.astype(f32))], axis=0)
    y_back_stage(4, modes.astype(bf16))
    out_py(4)
    y_back_stage(5, rate_hat)
    out_py(5)
    z_back_stage(4)
    z_back_stage(5)

    x_back_stage(4, x_plain, keep(push))
    for y in range(ROWS):
        here = [v_pad[c, y + 1] for c in range(3)]
        there = [push[rows_of(c, y), :] for c in range(3)]
        for c, cells in enumerate(cross(there, here)):
            field_in[rows_of(c, y), :] = cells.astype(bf16)
    x_stage(6, x_twice)

    parts = [jnp.zeros((8, LANES), f32) for _ in range(4)]

    def misfit(t, rate):
        c = t // 2
        for m in range(4):
            y = (t % 2) * 4 + m
            cells = closure[c, y] + time_step * rate[m * DEPTH : (m + 1) * DEPTH]
            m_pad[c, y + 1] = cells
            parts[c] = parts[c] + fold(cells)
            parts[3] = parts[3] + fold(cells * cells)

    x_back_stage(5, x_twice, misfit)
    halo_y_start(m_pad, 4)
    for c in range(3):
        w_parts[243 + c] = parts[c]
    w_parts[246] = 0.5 * parts[3]
    for k in range(247, 256):
        w_parts[k] = jnp.zeros((8, LANES), f32)
    weight_parts(0, 6)
    z_stage(6)
    out_py(6)
    halo_z_start(m_pad, 4)
    weight_parts(6, 27)
    reduce_start()
    modes = y_stage(6).astype(bf16).astype(f32)
    real, imag = curl(modes[:MODES], modes[MODES:])
    real = real - drag * hat_r[:MODES].astype(f32)
    imag = imag - drag * hat_r[MODES:].astype(f32)
    y_back_stage(7, jnp.concatenate([real, imag], axis=0).astype(bf16))
    out_py(7)
    shifts(m_pad, m_shift, 4)
    grad_rows(range(0, 3))
    reduce_next()
    z_back_stage(7)
    grad_rows(range(3, ROWS))
    for y in range(ROWS):
        here = [vort[rows_of(c, y), :] for c in range(3)]
        there = [push[rows_of(c, y), :] for c in range(3)]
        for c, cells in enumerate(cross(here, there)):
            closure[c, y] = closure[c, y] + m_pad[c, y + 1] + cells
    reduce_end()

    def finish(t, cells):
        for m in range(4):
            y = (t % 2) * 4 + m
            grad[t // 2, y] = closure[t // 2, y] + cells[m * DEPTH : (m + 1) * DEPTH]

    x_back_stage(7, x_plain, finish)

    for n in range(8):
        arrived(pz_send.at[n, 0 : PZ - 1], pz_ss.at[n])
        arrived(py_send.at[n, 0 : PY - 1], py_ss.at[n])
    for n in (0, 4):
        pad = v_pad if n == 0 else m_pad
        arrived(pad.at[:, 0], halo_ss.at[n])
        arrived(pad.at[:, 0], halo_ss.at[n + 1])
        arrived(halo_out.at[n // 4, 0], halo_ss.at[n + 2])
        arrived(halo_out.at[n // 4, 1], halo_ss.at[n + 3])
    arrived(r_pz.at[0 : PZ - 1], red_ss.at[0])
    arrived(r_py.at[0 : PY - 1], red_ss.at[1])


def on_device(velocity, target, closure_weight, closure_bias):
    shape = velocity.shape
    given = [jnp.asarray(t) for t in tables()]
    in_vmem = pl.BlockSpec(memory_space=pltpu.VMEM)
    in_smem = pl.BlockSpec(memory_space=pltpu.SMEM)
    dma = pltpu.SemaphoreType.DMA
    pad = (3, ROWS + 2, DEPTH, NX)
    in_hbm = pl.BlockSpec(memory_space=pl.ANY)
    landing = (PZ, 6, 16, LANES)
    grad, grad_weight, grad_bias, loss = pl.pallas_call(
        kernel,
        out_shape=(
            jax.ShapeDtypeStruct(shape, f32),
            jax.ShapeDtypeStruct(closure_weight.shape, f32),
            jax.ShapeDtypeStruct((3,), f32),
            jax.ShapeDtypeStruct((1,), f32),
        ),
        in_specs=[in_hbm, in_hbm, in_hbm, in_smem] + [in_hbm] * 6,
        out_specs=(in_vmem, in_vmem, in_smem, in_smem),
        scratch_shapes=[pltpu.VMEM(t.shape, bf16) for t in given]
        + [
            pltpu.VMEM(shape, f32),
            pltpu.VMEM((8,) + landing, bf16),
            pltpu.VMEM((8,) + landing, bf16),
            pltpu.VMEM((8, PY, 16, LANES), bf16),
            pltpu.VMEM((8, PY, 16, LANES), bf16),
            pltpu.VMEM((768, NX), bf16),
            pltpu.VMEM((384, 256), bf16),
            pltpu.VMEM((3, 2, 64, LANES), f32),
            pltpu.VMEM((3, 2, 128, LANES), f32),
            pltpu.VMEM((768, NX), f32),
            pltpu.VMEM((768, NX), f32),
            pltpu.VMEM(pad, f32),
            pltpu.VMEM(pad, f32),
            pltpu.VMEM((27, ROWS + 2, DEPTH, NX), f32),
            pltpu.VMEM((27, ROWS + 2, DEPTH, NX), f32),
            pltpu.VMEM((3, ROWS, DEPTH, NX), f32),
            pltpu.VMEM((2, 2, 32, NX), f32),
            pltpu.VMEM((2, 2, 32, NX), f32),
            pltpu.VMEM((256, 8, LANES), f32),
            pltpu.VMEM((1, 256), f32),
            pltpu.VMEM((PZ, 1, 256), f32),
            pltpu.VMEM((1, 256), f32),
            pltpu.VMEM((PY, 1, 256), f32),
            pltpu.VMEM((256, LANES), bf16),
            pltpu.VMEM((256, LANES), bf16),
            dma((8,)), dma((8,)), dma((8,)), dma((8,)), dma((8,)), dma((8,)), dma((2,)), dma((2,)),
            dma((11,)), pltpu.SMEM(closure_weight.shape, f32),
            pltpu.SMEM((243,), f32),
        ],
        compiler_params=pltpu.CompilerParams(
            collective_id=0, has_side_effects=True, vmem_limit_bytes=56 << 20
        ),
        name="euler",
    )(velocity, target, closure_weight, closure_bias, *given)
    return grad, grad_weight, grad_bias, loss.reshape(())


def solution(mesh):
    in_specs = (P(None, "py", "pz", None), P(None, "py", "pz", None), P(), P())
    out_specs = (P(None, "py", "pz", None), P(), P(), P())
    return jax.shard_map(
        on_device, mesh=mesh, in_specs=in_specs, out_specs=out_specs, check_vma=False
    )
```

```python
import functools
import math

import jax
import jax.numpy as jnp
import ml_dtypes
import numpy as np
from jax import lax
from jax.experimental import pallas as pl
from jax.experimental.pallas import tpu as pltpu
from jax.sharding import PartitionSpec as P

NX = 256
NY = 256
NZ = 256
PY = 32
PZ = 8
ROWS = NY // PY
DEPTH = NZ // PZ
KX = NX // 4
KL = KX // PZ
MODES = 128
LANES = 128
CELLS = float(NX * NY * NZ)
time_step = 0.01
viscosity = 0.002
MESH = pl.DeviceIdType.MESH
f32 = jnp.float32
bf16 = jnp.bfloat16


def ring(offset, length):
    return min(offset, length - offset)


FAR_PY = sorted(
    [(x, z, c) for x in range(2) for z in range(8) for c in range(2) if x + z + c > 0],
    key=lambda o: (-ring(o[1], 8) - o[0], o[1] > 4, o),
)
FAR_PZ = sorted(
    [(x, y) for x in range(2) for y in range(4) if x + y > 0],
    key=lambda o: (-ring(o[1], 4) - 2 * o[0], o),
)


def phases(positions, wavenumbers, length):
    turns = positions[:, None] * (wavenumbers[None, :] % length) % length
    angles = turns.astype(np.float32) * np.float32(2.0 * math.pi / length)
    return np.cos(angles), np.sin(angles)


def tables():
    factor = np.float32(1.0 / math.sqrt(NX))
    cosine, sine = phases(np.arange(NX), np.arange(KX), NX)
    pair = np.stack([factor * cosine, -factor * sine], axis=0)
    plain = pair.transpose(0, 2, 1).reshape(2, PZ, KL, NX).transpose(1, 0, 2, 3)
    plain = plain.reshape(2 * KX, NX)
    weights = np.where(np.arange(KX) == 0, 1.0, 2.0).astype(np.float32)
    weights = np.broadcast_to(weights.reshape(PZ, 1, KL), (PZ, 2, KL)).reshape(2 * KX, 1)
    wavenumbers = np.arange(MODES) - MODES // 2
    retained = (np.abs(wavenumbers) < MODES // 2).astype(np.float32)[None, :]
    cosine, sine = phases(np.arange(NZ), wavenumbers, NZ)
    real = factor * cosine * retained
    imag = -factor * sine * retained
    z_out = np.concatenate([real, imag], axis=1)
    z_back = np.concatenate([real.T, imag.T], axis=1)
    full = np.stack([np.stack([real, imag], 0), np.stack([-imag, real], 0)], 0)
    y_out = full.reshape(2, 2, PY, ROWS, MODES).transpose(1, 4, 2, 0, 3)
    y_out = y_out.reshape(2 * MODES, 2 * NY)
    given = (plain, plain * weights, z_out, z_back, y_out, y_out.T)
    return tuple(np.ascontiguousarray(t).astype(ml_dtypes.bfloat16) for t in given)


def swap_groups(tiles, lane):
    a0, a1, a2, a3 = tiles
    low = lane < 64
    b0 = jnp.where(low, a0, pltpu.roll(a2, 64, 1))
    b2 = jnp.where(low, pltpu.roll(a0, 64, 1), a2)
    b1 = jnp.where(low, a1, pltpu.roll(a3, 64, 1))
    b3 = jnp.where(low, pltpu.roll(a1, 64, 1), a3)
    even = (lane // 32) % 2 == 0
    c0 = jnp.where(even, b0, pltpu.roll(b1, 32, 1))
    c1 = jnp.where(even, pltpu.roll(b0, 96, 1), b1)
    c2 = jnp.where(even, b2, pltpu.roll(b3, 32, 1))
    c3 = jnp.where(even, pltpu.roll(b2, 96, 1), b3)
    return c0, c1, c2, c3


def dot(left, right, over):
    return lax.dot_general(left, right, (over, ((), ())), preferred_element_type=f32)


def kernel(
    vel_in, target_in, weight_in, bias, *refs,
):
    tables_in, refs = refs[:6], refs[6:]
    grad, grad_weight, grad_bias, loss = refs[:4]
    (x_plain, x_twice, z_out, z_back, y_out, y_back, target), refs = refs[4:11], refs[11:]
    (
        pz_send, pz_recv, py_send, py_recv, field_in, z_in, stage, spec_out,
        vort, push, v_pad, m_pad, v_shift, m_shift, closure, halo_out, halo_in,
        w_parts, r_own, r_pz, r_mid, r_py, hat_v, hat_r,
        pz_ss, pz_rs, py_ss, py_rs, halo_ss, halo_rs, red_ss, red_rs, in_sem, weight, flat,
    ) = refs
    py = lax.axis_index("py")
    pz = lax.axis_index("pz")

    barrier = pltpu.get_barrier_semaphore()

    def greet(k, _):
        pl.semaphore_signal(
            barrier, inc=1, device_id=(lax.rem(py + k, PY), pz), device_id_type=MESH
        )
        return 0

    lax.fori_loop(1, PY, greet, 0)
    for k in range(1, PZ):
        pl.semaphore_signal(
            barrier, inc=1, device_id=(py, lax.rem(pz + k, PZ)), device_id_type=MESH
        )

    loads = [pltpu.make_async_copy(tables_in[0], x_plain, in_sem.at[0])]
    for c in range(3):
        loads.append(
            pltpu.make_async_copy(
                vel_in.at[c], v_pad.at[c, pl.ds(1, ROWS)], in_sem.at[1 + c]
            )
        )
    later = ((2, z_out), (4, y_out), (5, y_back), (3, z_back), (1, x_twice))
    for k, (at, ref) in enumerate(later):
        loads.append(pltpu.make_async_copy(tables_in[at], ref, in_sem.at[4 + k]))
    loads.append(pltpu.make_async_copy(target_in, target, in_sem.at[9]))
    loads.append(pltpu.make_async_copy(weight_in, weight, in_sem.at[10]))
    for load in loads:
        load.start()

    def remote(src, dst, ss, rs, device):
        return pltpu.make_async_remote_copy(
            src_ref=src, dst_ref=dst, send_sem=ss, recv_sem=rs, device_id=device,
            device_id_type=MESH,
        )

    def send_pz(send_of, landing, ss, rs):
        for dx, dy in FAR_PZ:
            to = lax.rem(pz // 4 + dx, 2) * 4 + lax.rem(lax.rem(pz, 4) + dy, 4)
            remote(send_of(to), landing, ss, rs, (py, to)).start()
        pltpu.make_async_copy(send_of(pz), landing, rs).start()

    def send_py(send_of, recv, ss, rs):
        x, z, core = py // 16, lax.rem(py, 16) // 2, lax.rem(py, 2)
        for dx, dz, dc in FAR_PY:
            to = lax.rem(x + dx, 2) * 16 + lax.rem(z + dz, 8) * 2 + lax.rem(core + dc, 2)
            remote(send_of(to), recv.at[py], ss, rs, (to, pz)).start()
        pltpu.make_async_copy(send_of(py), recv.at[py], rs).start()

    def arrived(ref, sem):
        pltpu.make_async_copy(ref, ref, sem).wait()

    lane16 = lax.broadcasted_iota(jnp.int32, (16, LANES), 1)
    lane64 = lax.broadcasted_iota(jnp.int32, (64, LANES), 1)

    def halo_y_start(pad, n):
        up = lax.rem(py + 1, PY)
        down = lax.rem(py + PY - 1, PY)
        remote(pad.at[:, ROWS], pad.at[:, 0], halo_ss.at[n], halo_rs.at[n], (up, pz)).start()
        remote(
            pad.at[:, 1], pad.at[:, ROWS + 1], halo_ss.at[n + 1], halo_rs.at[n + 1], (down, pz)
        ).start()

    def halo_z_start(pad, n):
        arrived(pad.at[:, 0], halo_rs.at[n])
        arrived(pad.at[:, ROWS + 1], halo_rs.at[n + 1])
        s = n // 4
        halo_out[s, :, 24:, :] = jnp.zeros((2, 8, NX), f32)
        for j in range(3):
            for y in range(ROWS + 2):
                r = j * (ROWS + 2) + y
                halo_out[s, 0, r : r + 1, :] = pad[j, y, DEPTH - 1 : DEPTH, :]
                halo_out[s, 1, r : r + 1, :] = pad[j, y, 0:1, :]
        up = lax.rem(pz + 1, PZ)
        down = lax.rem(pz + PZ - 1, PZ)
        for side, to in ((0, up), (1, down)):
            remote(
                halo_out.at[s, side], halo_in.at[s, side], halo_ss.at[n + 2 + side],
                halo_rs.at[n + 2 + side], (py, to),
            ).start()

    def shifts(pad, out, n):
        s = n // 4
        arrived(halo_in.at[s, 0], halo_rs.at[n + 2])
        arrived(halo_in.at[s, 1], halo_rs.at[n + 3])
        row = lax.broadcasted_iota(jnp.int32, (DEPTH, NX), 0)
        for j in range(3):
            for y in range(ROWS + 2):
                r = j * (ROWS + 2) + y
                here = pad[j, y]
                below = jnp.where(row == 0, halo_in[s, 0, r : r + 1, :], pltpu.roll(here, 1, 0))
                above = jnp.where(
                    row == DEPTH - 1, halo_in[s, 1, r : r + 1, :], pltpu.roll(here, DEPTH - 1, 0)
                )
                for b, cells in enumerate((below, here, above)):
                    out[j * 9 + b * 3, y] = pltpu.roll(cells, 1, 1)
                    out[j * 9 + b * 3 + 1, y] = cells
                    out[j * 9 + b * 3 + 2, y] = pltpu.roll(cells, NX - 1, 1)

    def convolve_row(shifted, factor, y):
        def step(u, sums_here):
            sums_here = list(sums_here)
            for e in range(3):
                for a in range(3):
                    cells = shifted[u * 3 + e, y + a]
                    for i in range(3):
                        sums_here[i] = sums_here[i] + factor(i, a, u, e) * cells
            return tuple(sums_here)

        zero = jnp.zeros((DEPTH, NX), f32)
        return lax.fori_loop(0, 9, step, (zero, zero, zero))

    def flatten_weight():
        loads[10].wait()

        def one(t, _):
            for e in range(3):
                flat[t * 3 + e] = weight[t // 27, (t // 9) % 3, (t // 3) % 3, t % 3, e]
            return 0

        lax.fori_loop(0, 81, one, 0)

    def forward_factor(i, a, u, e):
        return flat[i * 81 + a * 9 + e + u * 3 + (u // 3) * 18]

    def backward_factor(i, a, u, e):
        return flat[i * 27 + (2 - a) * 9 + 8 - e + (u // 3) * 81 - (u % 3) * 3]

    def closure_rows(rows):
        for y in rows:
            for i, cells in enumerate(convolve_row(v_shift, forward_factor, y)):
                closure[i, y] = cells + bias[i]

    def grad_rows(rows):
        for y in rows:
            for i, cells in enumerate(convolve_row(m_shift, backward_factor, y)):
                closure[i, y] = cells

    def fold(cells):
        total = cells[0:8]
        for k in range(8, DEPTH, 8):
            total = total + cells[k : k + 8]
        return total[:, :LANES] + total[:, LANES:]

    def weight_parts(first, last):
        def one(t, _):
            def row(y, parts):
                parts = list(parts)
                for k in range(0, DEPTH, 8):
                    here = [m_pad[i, y + 1, k : k + 8] for i in range(3)]
                    for a in range(3):
                        cells = v_shift[t, y + a, k : k + 8]
                        for i in range(3):
                            parts[i * 3 + a] = parts[i * 3 + a] + here[i] * cells
                return tuple(parts)

            zero = jnp.zeros((8, NX), f32)
            parts = lax.fori_loop(0, ROWS, row, (zero,) * 9)
            at = t + (t // 9) * 18
            for i in range(3):
                for a in range(3):
                    both = parts[i * 3 + a]
                    w_parts[i * 81 + a * 9 + at] = both[:, :LANES] + both[:, LANES:]
            return 0

        lax.fori_loop(first, last, one, 0)

    def reduce_start():
        by_lane = jnp.sum(w_parts[...], axis=1)
        r_own[...] = jnp.sum(by_lane.T, axis=0, keepdims=True) * (1.0 / CELLS)
        send_pz(lambda to: r_own, r_pz.at[pz], red_ss.at[0], red_rs.at[0])

    def reduce_next():
        arrived(r_pz, red_rs.at[0])
        total = r_pz[0]
        for k in range(1, PZ):
            total = total + r_pz[k]
        r_mid[...] = total
        send_py(lambda to: r_mid, r_py, red_ss.at[1], red_rs.at[1])

    def reduce_end():
        arrived(r_py, red_rs.at[1])
        total = r_py[0]
        for k in range(1, PY):
            total = total + r_py[k]
        row = jnp.broadcast_to(total, (8, 256))
        for t in range(81):
            here = pltpu.roll(row, (256 - 3 * t) % 256, 1)
            i, j, a, b = t // 27, (t // 9) % 3, (t // 3) % 3, t % 3
            grad_weight[i, j, a, b : b + 1, :] = here[0:1, 0:3]
        at = lax.broadcasted_iota(jnp.int32, (1, 256), 1)
        for i in range(3):
            grad_bias[i] = jnp.sum(jnp.where(at == 243 + i, total, 0.0))
        loss[0] = jnp.sum(jnp.where(at == 246, total, 0.0))

    lane = lax.broadcasted_iota(jnp.int32, (MODES, LANES), 1)
    group = lane // 32
    kx = (pz * KL + py // 4).astype(f32) + jnp.zeros((MODES, LANES), f32)
    ky = (lax.broadcasted_iota(jnp.int32, (MODES, LANES), 0) - MODES // 2).astype(f32)
    kz = (lane % 32 + (py % 4) * 32 - MODES // 2).astype(f32)
    square = kx * kx + ky * ky + kz * kz

    def pick(first, second, third):
        return jnp.where(group == 0, first, jnp.where(group == 1, second, third))

    def next_one(cells):
        return jnp.where(group == 2, pltpu.roll(cells, 64, 1), pltpu.roll(cells, 96, 1))

    def next_two(cells):
        return jnp.where(group == 0, pltpu.roll(cells, 64, 1), pltpu.roll(cells, 32, 1))

    def turned(cells):
        return pick(ky, kz, kx) * next_two(cells) - pick(kz, kx, ky) * next_one(cells)

    def curl(real, imag):
        return -turned(imag), turned(real)

    def project(cells):
        along = pick(kx, ky, kz)
        part = along * cells
        part = part + next_one(part) + next_two(part)
        return cells - along * (part / jnp.maximum(square, 1.0))

    def out_pz(n):
        send_pz(lambda to: pz_send.at[n, to], pz_recv.at[n, pz], pz_ss.at[n], pz_rs.at[n])

    def out_py(n):
        send_py(lambda to: py_send.at[n, to], py_recv.at[n], py_ss.at[n], py_rs.at[n])

    def in_pz(n):
        arrived(pz_recv.at[n], pz_rs.at[n])

    def in_py(n):
        arrived(py_recv.at[n], py_rs.at[n])

    def x_stage(n, table):
        for c in range(3):
            x_tiles(n, table, c)
        out_pz(n)

    def x_tiles(n, table, c):
        for t in (2 * c, 2 * c + 1):
            out = dot(table[...], field_in[t * 128 : (t + 1) * 128, :], ((1,), (1,)))
            out = out.astype(bf16)
            for p in range(PZ):
                pz_send[n, p, t] = out[p * 16 : (p + 1) * 16]

    def z_stage(n):
        in_pz(n)
        for c in range(3):
            for yh in range(2):
                for h in range(2):
                    tiles = [pz_recv[n, 4 * h + g, 2 * c + yh].astype(f32) for g in range(4)]
                    for m, tile in enumerate(swap_groups(tiles, lane16)):
                        at = c * 128 + (yh * 4 + m) * 16
                        z_in[at : at + 16, h * 128 : (h + 1) * 128] = tile.astype(bf16)
            both = dot(z_in[c * 128 : (c + 1) * 128, :], z_out[...], ((1,), (0,)))
            for y in range(ROWS):
                r0 = both[y * 16 : y * 16 + 8]
                r1 = both[y * 16 + 8 : y * 16 + 16]
                stage[c, 0, pl.ds(y, 8, stride=8), :] = r0[:, :128] - r1[:, 128:]
                stage[c, 1, pl.ds(y, 8, stride=8), :] = r0[:, 128:] + r1[:, :128]
        blocks = [
            swap_groups(
                [stage[c, q, 0:64] for c in range(3)] + [jnp.zeros((64, LANES), f32)], lane64
            )
            for q in range(2)
        ]
        for g in range(4):
            for k in range(KL):
                py_send[n, k * 4 + g] = jnp.concatenate(
                    [blocks[0][g][k * 8 : k * 8 + 8], blocks[1][g][k * 8 : k * 8 + 8]], axis=0
                ).astype(bf16)

    def y_stage(n):
        in_py(n)
        return dot(y_out[...], py_recv[n].reshape(512, LANES), ((1,), (0,)))

    def y_back_stage(n, modes):
        rows = dot(y_back[...], modes, ((1,), (0,))).astype(bf16)
        for d in range(PY):
            py_send[n, d] = rows[d * 16 : (d + 1) * 16]

    def z_back_stage(n):
        in_py(n)
        for k in range(KL):
            tiles = [py_recv[n, k * 4 + g].astype(f32) for g in range(4)]
            for c, tile in enumerate(swap_groups(tiles, lane16)[:3]):
                at = c * 128 + k * 16
                z_in[at : at + 16, 0:128] = tile.astype(bf16)
        for c in range(3):
            both = dot(z_in[c * 128 : (c + 1) * 128, 0:128], z_back[...], ((1,), (0,)))
            for k in range(KL):
                r0 = both[k * 16 : k * 16 + 8]
                r1 = both[k * 16 + 8 : k * 16 + 16]
                for half in range(2):
                    re = slice(half * 128, half * 128 + 128)
                    im = slice(half * 128 + 256, half * 128 + 384)
                    spec_out[c, half, pl.ds(k, 8, stride=16), :] = r0[:, re] + r1[:, im]
                    spec_out[c, half, pl.ds(8 + k, 8, stride=16), :] = r1[:, re] - r0[:, im]
            for h in range(2):
                for half in range(2):
                    tiles = [
                        spec_out[c, half, (h * 4 + m) * 16 : (h * 4 + m + 1) * 16]
                        for m in range(4)
                    ]
                    for g, tile in enumerate(swap_groups(tiles, lane16)):
                        pz_send[n, half * 4 + g, c * 2 + h] = tile.astype(bf16)
        out_pz(n)

    def x_back_stage(n, table, out):
        in_pz(n)
        for c in range(3):
            for t in (2 * c, 2 * c + 1):
                block = pz_recv[n, :, t].reshape(128, LANES)
                out(t, dot(block, table[...], ((0,), (0,))))

    def keep(ref):
        def store(t, cells):
            ref[t * 128 : (t + 1) * 128, :] = cells

        return store

    def rows_of(c, y):
        at = (c * ROWS + y) * DEPTH
        return slice(at, at + DEPTH)

    def cross(left, right):
        return (
            left[1] * right[2] - left[2] * right[1],
            left[2] * right[0] - left[0] * right[2],
            left[0] * right[1] - left[1] * right[0],
        )

    loads[0].wait()
    for c in range(3):
        loads[1 + c].wait()
        for y in range(ROWS):
            field_in[rows_of(c, y), :] = v_pad[c, y + 1].astype(bf16)
        x_tiles(0, x_plain, c)
    pl.semaphore_wait(barrier, PY - 1 + PZ - 1)
    out_pz(0)
    halo_y_start(v_pad, 0)
    for load in loads[4:10]:
        load.wait()
    halo_z_start(v_pad, 0)
    z_stage(0)
    out_py(0)
    shifts(v_pad, v_shift, 0)
    flatten_weight()
    modes = y_stage(0).astype(bf16)
    hat_v[...] = modes
    real, imag = curl(modes[:MODES].astype(f32), modes[MODES:].astype(f32))
    y_back_stage(1, jnp.concatenate([real, imag], axis=0).astype(bf16))
    out_py(1)
    closure_rows(range(ROWS))
    z_back_stage(1)

    for c in range(3):
        for y in range(ROWS):
            cells = v_pad[c, y + 1] + closure[c, y] - target[c, y]
            closure[c, y] = cells
            field_in[rows_of(c, y), :] = (time_step * cells).astype(bf16)
    x_stage(2, x_twice)
    x_back_stage(1, x_twice, keep(vort))
    for y in range(ROWS):
        here = [v_pad[c, y + 1] for c in range(3)]
        there = [vort[rows_of(c, y), :] for c in range(3)]
        for c, cells in enumerate(cross(here, there)):
            field_in[rows_of(c, y), :] = cells.astype(bf16)
    x_stage(3, x_plain)
    z_stage(2)
    out_py(2)
    z_stage(3)
    out_py(3)
    again = y_stage(2)
    modes = y_stage(3).astype(bf16).astype(f32)
    drag = viscosity * square
    real = project(modes[:MODES]) - drag * hat_v[:MODES].astype(f32)
    imag = project(modes[MODES:]) - drag * hat_v[MODES:].astype(f32)
    rate_hat = jnp.concatenate([real, imag], axis=0).astype(bf16)
    twice = jnp.where(kx == 0.0, 1.0, 2.0) * (time_step * time_step)
    real = (again[:MODES] + twice * rate_hat[:MODES].astype(f32)).astype(bf16)
    imag = (again[MODES:] + twice * rate_hat[MODES:].astype(f32)).astype(bf16)
    hat_r[:MODES] = real
    hat_r[MODES:] = imag
    modes = jnp.concatenate([project(real.astype(f32)), project(imag.astype(f32))], axis=0)
    y_back_stage(4, modes.astype(bf16))
    out_py(4)
    y_back_stage(5, rate_hat)
    out_py(5)
    z_back_stage(4)
    z_back_stage(5)

    x_back_stage(4, x_plain, keep(push))
    for y in range(ROWS):
        here = [v_pad[c, y + 1] for c in range(3)]
        there = [push[rows_of(c, y), :] for c in range(3)]
        for c, cells in enumerate(cross(there, here)):
            field_in[rows_of(c, y), :] = cells.astype(bf16)
    x_stage(6, x_twice)

    parts = [jnp.zeros((8, LANES), f32) for _ in range(4)]

    def misfit(t, rate):
        c = t // 2
        for m in range(4):
            y = (t % 2) * 4 + m
            cells = closure[c, y] + time_step * rate[m * DEPTH : (m + 1) * DEPTH]
            m_pad[c, y + 1] = cells
            parts[c] = parts[c] + fold(cells)
            parts[3] = parts[3] + fold(cells * cells)

    x_back_stage(5, x_twice, misfit)
    halo_y_start(m_pad, 4)
    for c in range(3):
        w_parts[243 + c] = parts[c]
    w_parts[246] = 0.5 * parts[3]
    for k in range(247, 256):
        w_parts[k] = jnp.zeros((8, LANES), f32)
    weight_parts(0, 6)
    z_stage(6)
    out_py(6)
    halo_z_start(m_pad, 4)
    weight_parts(6, 27)
    reduce_start()
    modes = y_stage(6).astype(bf16).astype(f32)
    real, imag = curl(modes[:MODES], modes[MODES:])
    real = real - drag * hat_r[:MODES].astype(f32)
    imag = imag - drag * hat_r[MODES:].astype(f32)
    y_back_stage(7, jnp.concatenate([real, imag], axis=0).astype(bf16))
    out_py(7)
    shifts(m_pad, m_shift, 4)
    grad_rows(range(0, 3))
    reduce_next()
    z_back_stage(7)
    grad_rows(range(3, ROWS))
    for y in range(ROWS):
        here = [vort[rows_of(c, y), :] for c in range(3)]
        there = [push[rows_of(c, y), :] for c in range(3)]
        for c, cells in enumerate(cross(here, there)):
            closure[c, y] = closure[c, y] + m_pad[c, y + 1] + cells
    reduce_end()

    def finish(t, cells):
        for m in range(4):
            y = (t % 2) * 4 + m
            grad[t // 2, y] = closure[t // 2, y] + cells[m * DEPTH : (m + 1) * DEPTH]

    x_back_stage(7, x_plain, finish)

    for n in range(8):
        arrived(pz_send.at[n, 0 : PZ - 1], pz_ss.at[n])
        arrived(py_send.at[n, 0 : PY - 1], py_ss.at[n])
    for n in (0, 4):
        pad = v_pad if n == 0 else m_pad
        arrived(pad.at[:, 0], halo_ss.at[n])
        arrived(pad.at[:, 0], halo_ss.at[n + 1])
        arrived(halo_out.at[n // 4, 0], halo_ss.at[n + 2])
        arrived(halo_out.at[n // 4, 1], halo_ss.at[n + 3])
    arrived(r_pz.at[0 : PZ - 1], red_ss.at[0])
    arrived(r_py.at[0 : PY - 1], red_ss.at[1])


def on_device(velocity, target, closure_weight, closure_bias):
    shape = velocity.shape
    given = [jnp.asarray(t) for t in tables()]
    in_vmem = pl.BlockSpec(memory_space=pltpu.VMEM)
    in_smem = pl.BlockSpec(memory_space=pltpu.SMEM)
    dma = pltpu.SemaphoreType.DMA
    pad = (3, ROWS + 2, DEPTH, NX)
    in_hbm = pl.BlockSpec(memory_space=pl.ANY)
    landing = (PZ, 6, 16, LANES)
    grad, grad_weight, grad_bias, loss = pl.pallas_call(
        kernel,
        out_shape=(
            jax.ShapeDtypeStruct(shape, f32),
            jax.ShapeDtypeStruct(closure_weight.shape, f32),
            jax.ShapeDtypeStruct((3,), f32),
            jax.ShapeDtypeStruct((1,), f32),
        ),
        in_specs=[in_hbm, in_hbm, in_hbm, in_smem] + [in_hbm] * 6,
        out_specs=(in_vmem, in_vmem, in_smem, in_smem),
        scratch_shapes=[pltpu.VMEM(t.shape, bf16) for t in given]
        + [
            pltpu.VMEM(shape, f32),
            pltpu.VMEM((8,) + landing, bf16),
            pltpu.VMEM((8,) + landing, bf16),
            pltpu.VMEM((8, PY, 16, LANES), bf16),
            pltpu.VMEM((8, PY, 16, LANES), bf16),
            pltpu.VMEM((768, NX), bf16),
            pltpu.VMEM((384, 256), bf16),
            pltpu.VMEM((3, 2, 72, LANES), f32),
            pltpu.VMEM((3, 2, 144, LANES), f32),
            pltpu.VMEM((768, NX), f32),
            pltpu.VMEM((768, NX), f32),
            pltpu.VMEM(pad, f32),
            pltpu.VMEM(pad, f32),
            pltpu.VMEM((27, ROWS + 2, DEPTH, NX), f32),
            pltpu.VMEM((27, ROWS + 2, DEPTH, NX), f32),
            pltpu.VMEM((3, ROWS, DEPTH, NX), f32),
            pltpu.VMEM((2, 2, 32, NX), f32),
            pltpu.VMEM((2, 2, 32, NX), f32),
            pltpu.VMEM((256, 8, LANES), f32),
            pltpu.VMEM((1, 256), f32),
            pltpu.VMEM((PZ, 1, 256), f32),
            pltpu.VMEM((1, 256), f32),
            pltpu.VMEM((PY, 1, 256), f32),
            pltpu.VMEM((256, LANES), bf16),
            pltpu.VMEM((256, LANES), bf16),
            dma((8,)), dma((8,)), dma((8,)), dma((8,)), dma((8,)), dma((8,)), dma((2,)), dma((2,)),
            dma((11,)), pltpu.SMEM(closure_weight.shape, f32),
            pltpu.SMEM((243,), f32),
        ],
        compiler_params=pltpu.CompilerParams(
            collective_id=0, has_side_effects=True, vmem_limit_bytes=56 << 20
        ),
        name="euler",
    )(velocity, target, closure_weight, closure_bias, *given)
    return grad, grad_weight, grad_bias, loss.reshape(())


def solution(mesh):
    in_specs = (P(None, "py", "pz", None), P(None, "py", "pz", None), P(), P())
    out_specs = (P(None, "py", "pz", None), P(), P(), P())
    return jax.shard_map(
        on_device, mesh=mesh, in_specs=in_specs, out_specs=out_specs, check_vma=False
    )
```

```python
import functools
import math

import jax
import jax.numpy as jnp
import ml_dtypes
import numpy as np
from jax import lax
from jax.experimental import pallas as pl
from jax.experimental.pallas import tpu as pltpu
from jax.sharding import PartitionSpec as P

NX = 256
NY = 256
NZ = 256
PY = 32
PZ = 8
ROWS = NY // PY
DEPTH = NZ // PZ
KX = NX // 4
KL = KX // PZ
MODES = 128
LANES = 128
CELLS = float(NX * NY * NZ)
time_step = 0.01
viscosity = 0.002
MESH = pl.DeviceIdType.MESH
f32 = jnp.float32
bf16 = jnp.bfloat16


def ring(offset, length):
    return min(offset, length - offset)


FAR_PY = sorted(
    [(x, z, c) for x in range(2) for z in range(8) for c in range(2) if x + z + c > 0],
    key=lambda o: (-ring(o[1], 8) - o[0], o[1] > 4, o),
)
FAR_PZ = sorted(
    [(x, y) for x in range(2) for y in range(4) if x + y > 0],
    key=lambda o: (-ring(o[1], 4) - 2 * o[0], o),
)


def phases(positions, wavenumbers, length):
    turns = positions[:, None] * (wavenumbers[None, :] % length) % length
    angles = turns.astype(np.float32) * np.float32(2.0 * math.pi / length)
    return np.cos(angles), np.sin(angles)


def tables():
    factor = np.float32(1.0 / math.sqrt(NX))
    cosine, sine = phases(np.arange(NX), np.arange(KX), NX)
    pair = np.stack([factor * cosine, -factor * sine], axis=0)
    plain = pair.transpose(0, 2, 1).reshape(2, PZ, KL, NX).transpose(1, 0, 2, 3)
    plain = plain.reshape(2 * KX, NX)
    weights = np.where(np.arange(KX) == 0, 1.0, 2.0).astype(np.float32)
    weights = np.broadcast_to(weights.reshape(PZ, 1, KL), (PZ, 2, KL)).reshape(2 * KX, 1)
    wavenumbers = np.arange(MODES) - MODES // 2
    retained = (np.abs(wavenumbers) < MODES // 2).astype(np.float32)[None, :]
    cosine, sine = phases(np.arange(NZ), wavenumbers, NZ)
    real = factor * cosine * retained
    imag = -factor * sine * retained
    z_out = np.concatenate([real, imag], axis=1)
    z_back = np.concatenate([real.T, imag.T], axis=1)
    full = np.stack([np.stack([real, imag], 0), np.stack([-imag, real], 0)], 0)
    y_out = full.reshape(2, 2, PY, ROWS, MODES).transpose(1, 4, 2, 0, 3)
    y_out = y_out.reshape(2 * MODES, 2 * NY)
    given = (plain, plain * weights, z_out, z_back, y_out, y_out.T)
    return tuple(np.ascontiguousarray(t).astype(ml_dtypes.bfloat16) for t in given)


def swap_groups(tiles, lane):
    a0, a1, a2, a3 = tiles
    low = lane < 64
    b0 = jnp.where(low, a0, pltpu.roll(a2, 64, 1))
    b2 = jnp.where(low, pltpu.roll(a0, 64, 1), a2)
    b1 = jnp.where(low, a1, pltpu.roll(a3, 64, 1))
    b3 = jnp.where(low, pltpu.roll(a1, 64, 1), a3)
    even = (lane // 32) % 2 == 0
    c0 = jnp.where(even, b0, pltpu.roll(b1, 32, 1))
    c1 = jnp.where(even, pltpu.roll(b0, 96, 1), b1)
    c2 = jnp.where(even, b2, pltpu.roll(b3, 32, 1))
    c3 = jnp.where(even, pltpu.roll(b2, 96, 1), b3)
    return c0, c1, c2, c3


def dot(left, right, over):
    return lax.dot_general(left, right, (over, ((), ())), preferred_element_type=f32)


def kernel(
    vel_in, target_in, weight_in, bias, *refs,
):
    tables_in, refs = refs[:6], refs[6:]
    grad, grad_weight, grad_bias, loss = refs[:4]
    (x_plain, x_twice, z_out, z_back, y_out, y_back, target), refs = refs[4:11], refs[11:]
    (
        pz_send, pz_recv, py_send, py_recv, field_in, z_in, stage, spec_out,
        vort, push, v_pad, m_pad, v_shift, m_shift, closure, halo_out, halo_in,
        w_parts, r_own, r_pz, r_mid, r_py, hat_v, hat_r,
        pz_ss, pz_rs, py_ss, py_rs, halo_ss, halo_rs, red_ss, red_rs, in_sem, weight, flat,
    ) = refs
    py = lax.axis_index("py")
    pz = lax.axis_index("pz")

    barrier = pltpu.get_barrier_semaphore()

    def greet(k, _):
        pl.semaphore_signal(
            barrier, inc=1, device_id=(lax.rem(py + k, PY), pz), device_id_type=MESH
        )
        return 0

    lax.fori_loop(1, PY, greet, 0)
    for k in range(1, PZ):
        pl.semaphore_signal(
            barrier, inc=1, device_id=(py, lax.rem(pz + k, PZ)), device_id_type=MESH
        )

    loads = [pltpu.make_async_copy(tables_in[0], x_plain, in_sem.at[0])]
    for c in range(3):
        loads.append(
            pltpu.make_async_copy(
                vel_in.at[c], v_pad.at[c, pl.ds(1, ROWS)], in_sem.at[1 + c]
            )
        )
    later = ((2, z_out), (4, y_out), (5, y_back), (3, z_back), (1, x_twice))
    for k, (at, ref) in enumerate(later):
        loads.append(pltpu.make_async_copy(tables_in[at], ref, in_sem.at[4 + k]))
    loads.append(pltpu.make_async_copy(target_in, target, in_sem.at[9]))
    loads.append(pltpu.make_async_copy(weight_in, weight, in_sem.at[10]))
    for load in loads:
        load.start()

    def remote(src, dst, ss, rs, device):
        return pltpu.make_async_remote_copy(
            src_ref=src, dst_ref=dst, send_sem=ss, recv_sem=rs, device_id=device,
            device_id_type=MESH,
        )

    def send_pz(send_of, landing, ss, rs):
        for dx, dy in FAR_PZ:
            to = lax.rem(pz // 4 + dx, 2) * 4 + lax.rem(lax.rem(pz, 4) + dy, 4)
            remote(send_of(to), landing, ss, rs, (py, to)).start()
        pltpu.make_async_copy(send_of(pz), landing, rs).start()

    def send_py(send_of, recv, ss, rs):
        x, z, core = py // 16, lax.rem(py, 16) // 2, lax.rem(py, 2)
        for dx, dz, dc in FAR_PY:
            to = lax.rem(x + dx, 2) * 16 + lax.rem(z + dz, 8) * 2 + lax.rem(core + dc, 2)
            remote(send_of(to), recv.at[py], ss, rs, (to, pz)).start()
        pltpu.make_async_copy(send_of(py), recv.at[py], rs).start()

    def arrived(ref, sem):
        pltpu.make_async_copy(ref, ref, sem).wait()

    lane16 = lax.broadcasted_iota(jnp.int32, (16, LANES), 1)
    lane64 = lax.broadcasted_iota(jnp.int32, (64, LANES), 1)

    def halo_y_start(pad, n):
        up = lax.rem(py + 1, PY)
        down = lax.rem(py + PY - 1, PY)
        remote(pad.at[:, ROWS], pad.at[:, 0], halo_ss.at[n], halo_rs.at[n], (up, pz)).start()
        remote(
            pad.at[:, 1], pad.at[:, ROWS + 1], halo_ss.at[n + 1], halo_rs.at[n + 1], (down, pz)
        ).start()

    def halo_z_start(pad, n):
        arrived(pad.at[:, 0], halo_rs.at[n])
        arrived(pad.at[:, ROWS + 1], halo_rs.at[n + 1])
        s = n // 4
        halo_out[s, :, 24:, :] = jnp.zeros((2, 8, NX), f32)
        for j in range(3):
            for y in range(ROWS + 2):
                r = j * (ROWS + 2) + y
                halo_out[s, 0, r : r + 1, :] = pad[j, y, DEPTH - 1 : DEPTH, :]
                halo_out[s, 1, r : r + 1, :] = pad[j, y, 0:1, :]
        up = lax.rem(pz + 1, PZ)
        down = lax.rem(pz + PZ - 1, PZ)
        for side, to in ((0, up), (1, down)):
            remote(
                halo_out.at[s, side], halo_in.at[s, side], halo_ss.at[n + 2 + side],
                halo_rs.at[n + 2 + side], (py, to),
            ).start()

    def shifts(pad, out, n):
        s = n // 4
        arrived(halo_in.at[s, 0], halo_rs.at[n + 2])
        arrived(halo_in.at[s, 1], halo_rs.at[n + 3])
        row = lax.broadcasted_iota(jnp.int32, (DEPTH, NX), 0)
        for j in range(3):
            for y in range(ROWS + 2):
                r = j * (ROWS + 2) + y
                here = pad[j, y]
                below = jnp.where(row == 0, halo_in[s, 0, r : r + 1, :], pltpu.roll(here, 1, 0))
                above = jnp.where(
                    row == DEPTH - 1, halo_in[s, 1, r : r + 1, :], pltpu.roll(here, DEPTH - 1, 0)
                )
                for b, cells in enumerate((below, here, above)):
                    out[j * 9 + b * 3, y] = pltpu.roll(cells, 1, 1)
                    out[j * 9 + b * 3 + 1, y] = cells
                    out[j * 9 + b * 3 + 2, y] = pltpu.roll(cells, NX - 1, 1)

    def convolve_row(shifted, factor, y):
        def step(u, sums_here):
            sums_here = list(sums_here)
            for e in range(3):
                for a in range(3):
                    cells = shifted[u * 3 + e, y + a]
                    for i in range(3):
                        sums_here[i] = sums_here[i] + factor(i, a, u, e) * cells
            return tuple(sums_here)

        zero = jnp.zeros((DEPTH, NX), f32)
        return lax.fori_loop(0, 9, step, (zero, zero, zero))

    def flatten_weight():
        loads[10].wait()

        def one(t, _):
            for e in range(3):
                flat[t * 3 + e] = weight[t // 27, (t // 9) % 3, (t // 3) % 3, t % 3, e]
            return 0

        lax.fori_loop(0, 81, one, 0)

    def forward_factor(i, a, u, e):
        return flat[i * 81 + a * 9 + e + u * 3 + (u // 3) * 18]

    def backward_factor(i, a, u, e):
        return flat[i * 27 + (2 - a) * 9 + 8 - e + (u // 3) * 81 - (u % 3) * 3]

    def closure_rows(rows):
        for y in rows:
            for i, cells in enumerate(convolve_row(v_shift, forward_factor, y)):
                closure[i, y] = cells + bias[i]

    def grad_rows(rows):
        for y in rows:
            for i, cells in enumerate(convolve_row(m_shift, backward_factor, y)):
                closure[i, y] = cells

    def fold(cells):
        total = cells[0:8]
        for k in range(8, DEPTH, 8):
            total = total + cells[k : k + 8]
        return total[:, :LANES] + total[:, LANES:]

    def weight_parts(first, last):
        def one(t, _):
            def row(y, parts):
                parts = list(parts)
                for k in range(0, DEPTH, 8):
                    here = [m_pad[i, y + 1, k : k + 8] for i in range(3)]
                    for a in range(3):
                        cells = v_shift[t, y + a, k : k + 8]
                        for i in range(3):
                            parts[i * 3 + a] = parts[i * 3 + a] + here[i] * cells
                return tuple(parts)

            zero = jnp.zeros((8, NX), f32)
            parts = lax.fori_loop(0, ROWS, row, (zero,) * 9)
            at = t + (t // 9) * 18
            for i in range(3):
                for a in range(3):
                    both = parts[i * 3 + a]
                    w_parts[i * 81 + a * 9 + at] = both[:, :LANES] + both[:, LANES:]
            return 0

        lax.fori_loop(first, last, one, 0)

    def reduce_start():
        by_lane = jnp.sum(w_parts[...], axis=1)
        r_own[...] = jnp.sum(by_lane.T, axis=0, keepdims=True) * (1.0 / CELLS)
        send_pz(lambda to: r_own, r_pz.at[pz], red_ss.at[0], red_rs.at[0])

    def reduce_next():
        arrived(r_pz, red_rs.at[0])
        total = r_pz[0]
        for k in range(1, PZ):
            total = total + r_pz[k]
        r_mid[...] = total
        send_py(lambda to: r_mid, r_py, red_ss.at[1], red_rs.at[1])

    def reduce_end():
        arrived(r_py, red_rs.at[1])
        total = r_py[0]
        for k in range(1, PY):
            total = total + r_py[k]
        row = jnp.broadcast_to(total, (8, 256))
        for t in range(81):
            here = pltpu.roll(row, (256 - 3 * t) % 256, 1)
            i, j, a, b = t // 27, (t // 9) % 3, (t // 3) % 3, t % 3
            grad_weight[i, j, a, b : b + 1, :] = here[0:1, 0:3]
        at = lax.broadcasted_iota(jnp.int32, (1, 256), 1)
        for i in range(3):
            grad_bias[i] = jnp.sum(jnp.where(at == 243 + i, total, 0.0))
        loss[0] = jnp.sum(jnp.where(at == 246, total, 0.0))

    lane = lax.broadcasted_iota(jnp.int32, (MODES, LANES), 1)
    group = lane // 32
    kx = (pz * KL + py // 4).astype(f32) + jnp.zeros((MODES, LANES), f32)
    ky = (lax.broadcasted_iota(jnp.int32, (MODES, LANES), 0) - MODES // 2).astype(f32)
    kz = (lane % 32 + (py % 4) * 32 - MODES // 2).astype(f32)
    square = kx * kx + ky * ky + kz * kz

    def pick(first, second, third):
        return jnp.where(group == 0, first, jnp.where(group == 1, second, third))

    def next_one(cells):
        return jnp.where(group == 2, pltpu.roll(cells, 64, 1), pltpu.roll(cells, 96, 1))

    def next_two(cells):
        return jnp.where(group == 0, pltpu.roll(cells, 64, 1), pltpu.roll(cells, 32, 1))

    def turned(cells):
        return pick(ky, kz, kx) * next_two(cells) - pick(kz, kx, ky) * next_one(cells)

    def curl(real, imag):
        return -turned(imag), turned(real)

    def project(cells):
        along = pick(kx, ky, kz)
        part = along * cells
        part = part + next_one(part) + next_two(part)
        return cells - along * (part / jnp.maximum(square, 1.0))

    def out_pz(n):
        send_pz(lambda to: pz_send.at[n, to], pz_recv.at[n, pz], pz_ss.at[n], pz_rs.at[n])

    def out_py(n):
        send_py(lambda to: py_send.at[n, to], py_recv.at[n], py_ss.at[n], py_rs.at[n])

    def in_pz(n):
        arrived(pz_recv.at[n], pz_rs.at[n])

    def in_py(n):
        arrived(py_recv.at[n], py_rs.at[n])

    def x_stage(n, table):
        for c in range(3):
            x_tiles(n, table, c)
        out_pz(n)

    def x_tiles(n, table, c):
        for t in (2 * c, 2 * c + 1):
            out = dot(table[...], field_in[t * 128 : (t + 1) * 128, :], ((1,), (1,)))
            out = out.astype(bf16)
            for p in range(PZ):
                pz_send[n, p, t] = out[p * 16 : (p + 1) * 16]

    def z_stage(n):
        in_pz(n)
        for c in range(3):
            for yh in range(2):
                for h in range(2):
                    tiles = [pz_recv[n, 4 * h + g, 2 * c + yh].astype(f32) for g in range(4)]
                    for m, tile in enumerate(swap_groups(tiles, lane16)):
                        at = c * 128 + (yh * 4 + m) * 16
                        z_in[at : at + 16, h * 128 : (h + 1) * 128] = tile.astype(bf16)
            both = dot(z_in[c * 128 : (c + 1) * 128, :], z_out[...], ((1,), (0,)))
            for y in range(ROWS):
                r0 = both[y * 16 : y * 16 + 8]
                r1 = both[y * 16 + 8 : y * 16 + 16]
                stage[c, 0, pl.ds(y, 8, stride=8), :] = r0[:, :128] - r1[:, 128:]
                stage[c, 1, pl.ds(y, 8, stride=8), :] = r0[:, 128:] + r1[:, :128]
        blocks = [
            swap_groups(
                [stage[0, q], stage[1, q], stage[2, q], jnp.zeros((64, LANES), f32)], lane64
            )
            for q in range(2)
        ]
        for g in range(4):
            for k in range(KL):
                py_send[n, k * 4 + g] = jnp.concatenate(
                    [blocks[0][g][k * 8 : k * 8 + 8], blocks[1][g][k * 8 : k * 8 + 8]], axis=0
                ).astype(bf16)

    def y_stage(n):
        in_py(n)
        return dot(y_out[...], py_recv[n].reshape(512, LANES), ((1,), (0,)))

    def y_back_stage(n, modes):
        rows = dot(y_back[...], modes, ((1,), (0,))).astype(bf16)
        for d in range(PY):
            py_send[n, d] = rows[d * 16 : (d + 1) * 16]

    def z_back_stage(n):
        in_py(n)
        for k in range(KL):
            tiles = [py_recv[n, k * 4 + g].astype(f32) for g in range(4)]
            for c, tile in enumerate(swap_groups(tiles, lane16)[:3]):
                at = c * 128 + k * 16
                z_in[at : at + 16, 0:128] = tile.astype(bf16)
        for c in range(3):
            both = dot(z_in[c * 128 : (c + 1) * 128, 0:128], z_back[...], ((1,), (0,)))
            for k in range(KL):
                r0 = both[k * 16 : k * 16 + 8]
                r1 = both[k * 16 + 8 : k * 16 + 16]
                for half in range(2):
                    re = slice(half * 128, half * 128 + 128)
                    im = slice(half * 128 + 256, half * 128 + 384)
                    spec_out[c, half, pl.ds(k, 8, stride=16), :] = r0[:, re] + r1[:, im]
                    spec_out[c, half, pl.ds(8 + k, 8, stride=16), :] = r1[:, re] - r0[:, im]
            for h in range(2):
                for half in range(2):
                    tiles = [
                        spec_out[c, half, (h * 4 + m) * 16 : (h * 4 + m + 1) * 16]
                        for m in range(4)
                    ]
                    for g, tile in enumerate(swap_groups(tiles, lane16)):
                        pz_send[n, half * 4 + g, c * 2 + h] = tile.astype(bf16)
        out_pz(n)

    def x_back_stage(n, table, out):
        in_pz(n)
        for c in range(3):
            for t in (2 * c, 2 * c + 1):
                block = pz_recv[n, :, t].reshape(128, LANES)
                out(t, dot(block, table[...], ((0,), (0,))))

    def keep(ref):
        def store(t, cells):
            ref[t * 128 : (t + 1) * 128, :] = cells

        return store

    def rows_of(c, y):
        at = (c * ROWS + y) * DEPTH
        return slice(at, at + DEPTH)

    def cross(left, right):
        return (
            left[1] * right[2] - left[2] * right[1],
            left[2] * right[0] - left[0] * right[2],
            left[0] * right[1] - left[1] * right[0],
        )

    loads[0].wait()
    for c in range(3):
        loads[1 + c].wait()
        for y in range(ROWS):
            field_in[rows_of(c, y), :] = v_pad[c, y + 1].astype(bf16)
        x_tiles(0, x_plain, c)
    pl.semaphore_wait(barrier, PY - 1 + PZ - 1)
    out_pz(0)
    halo_y_start(v_pad, 0)
    for load in loads[4:10]:
        load.wait()
    halo_z_start(v_pad, 0)
    z_stage(0)
    out_py(0)
    shifts(v_pad, v_shift, 0)
    flatten_weight()
    modes = y_stage(0).astype(bf16)
    hat_v[...] = modes
    real, imag = curl(modes[:MODES].astype(f32), modes[MODES:].astype(f32))
    y_back_stage(1, jnp.concatenate([real, imag], axis=0).astype(bf16))
    out_py(1)
    closure_rows(range(ROWS))
    z_back_stage(1)

    for c in range(3):
        for y in range(ROWS):
            cells = v_pad[c, y + 1] + closure[c, y] - target[c, y]
            closure[c, y] = cells
            field_in[rows_of(c, y), :] = (time_step * cells).astype(bf16)
    x_stage(2, x_twice)
    x_back_stage(1, x_twice, keep(vort))
    for y in range(ROWS):
        here = [v_pad[c, y + 1] for c in range(3)]
        there = [vort[rows_of(c, y), :] for c in range(3)]
        for c, cells in enumerate(cross(here, there)):
            field_in[rows_of(c, y), :] = cells.astype(bf16)
    x_stage(3, x_plain)
    z_stage(2)
    out_py(2)
    z_stage(3)
    out_py(3)
    again = y_stage(2)
    modes = y_stage(3).astype(bf16).astype(f32)
    drag = viscosity * square
    real = project(modes[:MODES]) - drag * hat_v[:MODES].astype(f32)
    imag = project(modes[MODES:]) - drag * hat_v[MODES:].astype(f32)
    rate_hat = jnp.concatenate([real, imag], axis=0).astype(bf16)
    twice = jnp.where(kx == 0.0, 1.0, 2.0) * (time_step * time_step)
    real = (again[:MODES] + twice * rate_hat[:MODES].astype(f32)).astype(bf16)
    imag = (again[MODES:] + twice * rate_hat[MODES:].astype(f32)).astype(bf16)
    hat_r[:MODES] = real
    hat_r[MODES:] = imag
    modes = jnp.concatenate([project(real.astype(f32)), project(imag.astype(f32))], axis=0)
    y_back_stage(4, modes.astype(bf16))
    out_py(4)
    y_back_stage(5, rate_hat)
    out_py(5)
    z_back_stage(4)
    z_back_stage(5)

    x_back_stage(4, x_plain, keep(push))
    for y in range(ROWS):
        here = [v_pad[c, y + 1] for c in range(3)]
        there = [push[rows_of(c, y), :] for c in range(3)]
        for c, cells in enumerate(cross(there, here)):
            field_in[rows_of(c, y), :] = cells.astype(bf16)
    x_stage(6, x_twice)

    parts = [jnp.zeros((8, LANES), f32) for _ in range(4)]

    def misfit(t, rate):
        c = t // 2
        for m in range(4):
            y = (t % 2) * 4 + m
            cells = closure[c, y] + time_step * rate[m * DEPTH : (m + 1) * DEPTH]
            m_pad[c, y + 1] = cells
            parts[c] = parts[c] + fold(cells)
            parts[3] = parts[3] + fold(cells * cells)

    x_back_stage(5, x_twice, misfit)
    for c in range(3):
        w_parts[243 + c] = parts[c]
    w_parts[246] = 0.5 * parts[3]
    for k in range(247, 256):
        w_parts[k] = jnp.zeros((8, LANES), f32)
    weight_parts(0, 6)
    z_stage(6)
    out_py(6)
    halo_y_start(m_pad, 4)
    weight_parts(6, 27)
    halo_z_start(m_pad, 4)
    reduce_start()
    modes = y_stage(6).astype(bf16).astype(f32)
    real, imag = curl(modes[:MODES], modes[MODES:])
    real = real - drag * hat_r[:MODES].astype(f32)
    imag = imag - drag * hat_r[MODES:].astype(f32)
    y_back_stage(7, jnp.concatenate([real, imag], axis=0).astype(bf16))
    out_py(7)
    shifts(m_pad, m_shift, 4)
    grad_rows(range(0, 3))
    reduce_next()
    z_back_stage(7)
    grad_rows(range(3, ROWS))
    for y in range(ROWS):
        here = [vort[rows_of(c, y), :] for c in range(3)]
        there = [push[rows_of(c, y), :] for c in range(3)]
        for c, cells in enumerate(cross(here, there)):
            closure[c, y] = closure[c, y] + m_pad[c, y + 1] + cells
    reduce_end()

    def finish(t, cells):
        for m in range(4):
            y = (t % 2) * 4 + m
            grad[t // 2, y] = closure[t // 2, y] + cells[m * DEPTH : (m + 1) * DEPTH]

    x_back_stage(7, x_plain, finish)

    for n in range(8):
        arrived(pz_send.at[n, 0 : PZ - 1], pz_ss.at[n])
        arrived(py_send.at[n, 0 : PY - 1], py_ss.at[n])
    for n in (0, 4):
        pad = v_pad if n == 0 else m_pad
        arrived(pad.at[:, 0], halo_ss.at[n])
        arrived(pad.at[:, 0], halo_ss.at[n + 1])
        arrived(halo_out.at[n // 4, 0], halo_ss.at[n + 2])
        arrived(halo_out.at[n // 4, 1], halo_ss.at[n + 3])
    arrived(r_pz.at[0 : PZ - 1], red_ss.at[0])
    arrived(r_py.at[0 : PY - 1], red_ss.at[1])


def on_device(velocity, target, closure_weight, closure_bias):
    shape = velocity.shape
    given = [jnp.asarray(t) for t in tables()]
    in_vmem = pl.BlockSpec(memory_space=pltpu.VMEM)
    in_smem = pl.BlockSpec(memory_space=pltpu.SMEM)
    dma = pltpu.SemaphoreType.DMA
    pad = (3, ROWS + 2, DEPTH, NX)
    in_hbm = pl.BlockSpec(memory_space=pl.ANY)
    landing = (PZ, 6, 16, LANES)
    grad, grad_weight, grad_bias, loss = pl.pallas_call(
        kernel,
        out_shape=(
            jax.ShapeDtypeStruct(shape, f32),
            jax.ShapeDtypeStruct(closure_weight.shape, f32),
            jax.ShapeDtypeStruct((3,), f32),
            jax.ShapeDtypeStruct((1,), f32),
        ),
        in_specs=[in_hbm, in_hbm, in_hbm, in_smem] + [in_hbm] * 6,
        out_specs=(in_vmem, in_vmem, in_smem, in_smem),
        scratch_shapes=[pltpu.VMEM(t.shape, bf16) for t in given]
        + [
            pltpu.VMEM(shape, f32),
            pltpu.VMEM((8,) + landing, bf16),
            pltpu.VMEM((8,) + landing, bf16),
            pltpu.VMEM((8, PY, 16, LANES), bf16),
            pltpu.VMEM((8, PY, 16, LANES), bf16),
            pltpu.VMEM((768, NX), bf16),
            pltpu.VMEM((384, 256), bf16),
            pltpu.VMEM((3, 2, 64, LANES), f32),
            pltpu.VMEM((3, 2, 128, LANES), f32),
            pltpu.VMEM((768, NX), f32),
            pltpu.VMEM((768, NX), f32),
            pltpu.VMEM(pad, f32),
            pltpu.VMEM(pad, f32),
            pltpu.VMEM((27, ROWS + 2, DEPTH, NX), f32),
            pltpu.VMEM((27, ROWS + 2, DEPTH, NX), f32),
            pltpu.VMEM((3, ROWS, DEPTH, NX), f32),
            pltpu.VMEM((2, 2, 32, NX), f32),
            pltpu.VMEM((2, 2, 32, NX), f32),
            pltpu.VMEM((256, 8, LANES), f32),
            pltpu.VMEM((1, 256), f32),
            pltpu.VMEM((PZ, 1, 256), f32),
            pltpu.VMEM((1, 256), f32),
            pltpu.VMEM((PY, 1, 256), f32),
            pltpu.VMEM((256, LANES), bf16),
            pltpu.VMEM((256, LANES), bf16),
            dma((8,)), dma((8,)), dma((8,)), dma((8,)), dma((8,)), dma((8,)), dma((2,)), dma((2,)),
            dma((11,)), pltpu.SMEM(closure_weight.shape, f32),
            pltpu.SMEM((243,), f32),
        ],
        compiler_params=pltpu.CompilerParams(
            collective_id=0, has_side_effects=True, vmem_limit_bytes=56 << 20
        ),
        name="euler",
    )(velocity, target, closure_weight, closure_bias, *given)
    return grad, grad_weight, grad_bias, loss.reshape(())


def solution(mesh):
    in_specs = (P(None, "py", "pz", None), P(None, "py", "pz", None), P(), P())
    out_specs = (P(None, "py", "pz", None), P(), P(), P())
    return jax.shard_map(
        on_device, mesh=mesh, in_specs=in_specs, out_specs=out_specs, check_vma=False
    )
```

```python
import functools
import math

import jax
import jax.numpy as jnp
import ml_dtypes
import numpy as np
from jax import lax
from jax.experimental import pallas as pl
from jax.experimental.pallas import tpu as pltpu
from jax.sharding import PartitionSpec as P

NX = 256
NY = 256
NZ = 256
PY = 32
PZ = 8
ROWS = NY // PY
DEPTH = NZ // PZ
KX = NX // 4
KL = KX // PZ
MODES = 128
LANES = 128
CELLS = float(NX * NY * NZ)
time_step = 0.01
viscosity = 0.002
MESH = pl.DeviceIdType.MESH
f32 = jnp.float32
bf16 = jnp.bfloat16


def ring(offset, length):
    return min(offset, length - offset)


FAR_PY = sorted(
    [(x, z, c) for x in range(2) for z in range(8) for c in range(2) if x + z + c > 0],
    key=lambda o: (-ring(o[1], 8) - o[0], o[1] > 4, o),
)
FAR_PZ = sorted(
    [(x, y) for x in range(2) for y in range(4) if x + y > 0],
    key=lambda o: (-ring(o[1], 4) - 2 * o[0], o),
)


def phases(positions, wavenumbers, length):
    turns = positions[:, None] * (wavenumbers[None, :] % length) % length
    angles = turns.astype(np.float32) * np.float32(2.0 * math.pi / length)
    return np.cos(angles), np.sin(angles)


def tables():
    factor = np.float32(1.0 / math.sqrt(NX))
    cosine, sine = phases(np.arange(NX), np.arange(KX), NX)
    pair = np.stack([factor * cosine, -factor * sine], axis=0)
    plain = pair.transpose(0, 2, 1).reshape(2, PZ, KL, NX).transpose(1, 0, 2, 3)
    plain = plain.reshape(2 * KX, NX)
    weights = np.where(np.arange(KX) == 0, 1.0, 2.0).astype(np.float32)
    weights = np.broadcast_to(weights.reshape(PZ, 1, KL), (PZ, 2, KL)).reshape(2 * KX, 1)
    wavenumbers = np.arange(MODES) - MODES // 2
    retained = (np.abs(wavenumbers) < MODES // 2).astype(np.float32)[None, :]
    cosine, sine = phases(np.arange(NZ), wavenumbers, NZ)
    real = factor * cosine * retained
    imag = -factor * sine * retained
    z_out = np.concatenate([real, imag], axis=1)
    z_back = np.concatenate([real.T, imag.T], axis=1)
    full = np.stack([np.stack([real, imag], 0), np.stack([-imag, real], 0)], 0)
    y_out = full.reshape(2, 2, PY, ROWS, MODES).transpose(1, 4, 2, 0, 3)
    y_out = y_out.reshape(2 * MODES, 2 * NY)
    given = (plain, plain * weights, z_out, z_back, y_out, y_out.T)
    return tuple(np.ascontiguousarray(t).astype(ml_dtypes.bfloat16) for t in given)


def swap_groups(tiles, lane):
    a0, a1, a2, a3 = tiles
    low = lane < 64
    b0 = jnp.where(low, a0, pltpu.roll(a2, 64, 1))
    b2 = jnp.where(low, pltpu.roll(a0, 64, 1), a2)
    b1 = jnp.where(low, a1, pltpu.roll(a3, 64, 1))
    b3 = jnp.where(low, pltpu.roll(a1, 64, 1), a3)
    even = (lane // 32) % 2 == 0
    c0 = jnp.where(even, b0, pltpu.roll(b1, 32, 1))
    c1 = jnp.where(even, pltpu.roll(b0, 96, 1), b1)
    c2 = jnp.where(even, b2, pltpu.roll(b3, 32, 1))
    c3 = jnp.where(even, pltpu.roll(b2, 96, 1), b3)
    return c0, c1, c2, c3


def dot(left, right, over):
    return lax.dot_general(left, right, (over, ((), ())), preferred_element_type=f32)


def kernel(
    vel_in, target_in, weight_in, bias, *refs,
):
    tables_in, refs = refs[:6], refs[6:]
    grad, grad_weight, grad_bias, loss = refs[:4]
    (x_plain, x_twice, z_out, z_back, y_out, y_back, target), refs = refs[4:11], refs[11:]
    (
        pz_send, pz_recv, py_send, py_recv, field_in, z_in, stage, spec_out,
        vort, push, v_pad, m_pad, v_shift, m_shift, closure, halo_out, halo_in,
        w_parts, r_own, r_pz, r_mid, r_py, hat_v, hat_r,
        pz_ss, pz_rs, py_ss, py_rs, halo_ss, halo_rs, red_ss, red_rs, in_sem, weight, flat,
    ) = refs
    py = lax.axis_index("py")
    pz = lax.axis_index("pz")

    barrier = pltpu.get_barrier_semaphore()

    def greet(k, _):
        pl.semaphore_signal(
            barrier, inc=1, device_id=(lax.rem(py + k, PY), pz), device_id_type=MESH
        )
        return 0

    lax.fori_loop(1, PY, greet, 0)
    for k in range(1, PZ):
        pl.semaphore_signal(
            barrier, inc=1, device_id=(py, lax.rem(pz + k, PZ)), device_id_type=MESH
        )

    loads = [pltpu.make_async_copy(tables_in[0], x_plain, in_sem.at[0])]
    for c in range(3):
        loads.append(
            pltpu.make_async_copy(
                vel_in.at[c], v_pad.at[c, pl.ds(1, ROWS)], in_sem.at[1 + c]
            )
        )
    later = ((2, z_out), (4, y_out), (5, y_back), (3, z_back), (1, x_twice))
    for k, (at, ref) in enumerate(later):
        loads.append(pltpu.make_async_copy(tables_in[at], ref, in_sem.at[4 + k]))
    loads.append(pltpu.make_async_copy(target_in, target, in_sem.at[9]))
    loads.append(pltpu.make_async_copy(weight_in, weight, in_sem.at[10]))
    for load in loads:
        load.start()

    def remote(src, dst, ss, rs, device):
        return pltpu.make_async_remote_copy(
            src_ref=src, dst_ref=dst, send_sem=ss, recv_sem=rs, device_id=device,
            device_id_type=MESH,
        )

    x, z, core = py // 16, lax.rem(py, 16) // 2, lax.rem(py, 2)
    far_py = [
        lax.rem(x + dx, 2) * 16 + lax.rem(z + dz, 8) * 2 + lax.rem(core + dc, 2)
        for dx, dz, dc in FAR_PY
    ]
    far_pz = [
        lax.rem(pz // 4 + dx, 2) * 4 + lax.rem(lax.rem(pz, 4) + dy, 4) for dx, dy in FAR_PZ
    ]

    def send_pz(send_of, landing, ss, rs):
        for to in far_pz:
            remote(send_of(to), landing, ss, rs, (py, to)).start()
        pltpu.make_async_copy(send_of(pz), landing, rs).start()

    def send_py(send_of, recv, ss, rs):
        for to in far_py:
            remote(send_of(to), recv.at[py], ss, rs, (to, pz)).start()
        pltpu.make_async_copy(send_of(py), recv.at[py], rs).start()

    def arrived(ref, sem):
        pltpu.make_async_copy(ref, ref, sem).wait()

    lane16 = lax.broadcasted_iota(jnp.int32, (16, LANES), 1)
    lane64 = lax.broadcasted_iota(jnp.int32, (64, LANES), 1)

    def halo_y_start(pad, n):
        up = lax.rem(py + 1, PY)
        down = lax.rem(py + PY - 1, PY)
        remote(pad.at[:, ROWS], pad.at[:, 0], halo_ss.at[n], halo_rs.at[n], (up, pz)).start()
        remote(
            pad.at[:, 1], pad.at[:, ROWS + 1], halo_ss.at[n + 1], halo_rs.at[n + 1], (down, pz)
        ).start()

    def halo_z_start(pad, n):
        arrived(pad.at[:, 0], halo_rs.at[n])
        arrived(pad.at[:, ROWS + 1], halo_rs.at[n + 1])
        s = n // 4
        halo_out[s, :, 24:, :] = jnp.zeros((2, 8, NX), f32)
        for j in range(3):
            for y in range(ROWS + 2):
                r = j * (ROWS + 2) + y
                halo_out[s, 0, r : r + 1, :] = pad[j, y, DEPTH - 1 : DEPTH, :]
                halo_out[s, 1, r : r + 1, :] = pad[j, y, 0:1, :]
        up = lax.rem(pz + 1, PZ)
        down = lax.rem(pz + PZ - 1, PZ)
        for side, to in ((0, up), (1, down)):
            remote(
                halo_out.at[s, side], halo_in.at[s, side], halo_ss.at[n + 2 + side],
                halo_rs.at[n + 2 + side], (py, to),
            ).start()

    def shifts(pad, out, n):
        s = n // 4
        arrived(halo_in.at[s, 0], halo_rs.at[n + 2])
        arrived(halo_in.at[s, 1], halo_rs.at[n + 3])
        row = lax.broadcasted_iota(jnp.int32, (DEPTH, NX), 0)
        for j in range(3):
            for y in range(ROWS + 2):
                r = j * (ROWS + 2) + y
                here = pad[j, y]
                below = jnp.where(row == 0, halo_in[s, 0, r : r + 1, :], pltpu.roll(here, 1, 0))
                above = jnp.where(
                    row == DEPTH - 1, halo_in[s, 1, r : r + 1, :], pltpu.roll(here, DEPTH - 1, 0)
                )
                for b, cells in enumerate((below, here, above)):
                    out[j * 9 + b * 3, y] = pltpu.roll(cells, 1, 1)
                    out[j * 9 + b * 3 + 1, y] = cells
                    out[j * 9 + b * 3 + 2, y] = pltpu.roll(cells, NX - 1, 1)

    def convolve_row(shifted, factor, y):
        def step(u, sums_here):
            sums_here = list(sums_here)
            for e in range(3):
                for a in range(3):
                    cells = shifted[u * 3 + e, y + a]
                    for i in range(3):
                        sums_here[i] = sums_here[i] + factor(i, a, u, e) * cells
            return tuple(sums_here)

        zero = jnp.zeros((DEPTH, NX), f32)
        return lax.fori_loop(0, 9, step, (zero, zero, zero))

    def flatten_weight():
        loads[10].wait()

        def one(t, _):
            for e in range(3):
                flat[t * 3 + e] = weight[t // 27, (t // 9) % 3, (t // 3) % 3, t % 3, e]
            return 0

        lax.fori_loop(0, 81, one, 0)

    def forward_factor(i, a, u, e):
        return flat[i * 81 + a * 9 + e + u * 3 + (u // 3) * 18]

    def backward_factor(i, a, u, e):
        return flat[i * 27 + (2 - a) * 9 + 8 - e + (u // 3) * 81 - (u % 3) * 3]

    def closure_rows(rows):
        for y in rows:
            for i, cells in enumerate(convolve_row(v_shift, forward_factor, y)):
                closure[i, y] = cells + bias[i]

    def grad_rows(rows):
        for y in rows:
            for i, cells in enumerate(convolve_row(m_shift, backward_factor, y)):
                closure[i, y] = cells

    def fold(cells):
        total = cells[0:8]
        for k in range(8, DEPTH, 8):
            total = total + cells[k : k + 8]
        return total[:, :LANES] + total[:, LANES:]

    def weight_parts(first, last):
        def one(t, _):
            def row(y, parts):
                parts = list(parts)
                for k in range(0, DEPTH, 8):
                    here = [m_pad[i, y + 1, k : k + 8] for i in range(3)]
                    for a in range(3):
                        cells = v_shift[t, y + a, k : k + 8]
                        for i in range(3):
                            parts[i * 3 + a] = parts[i * 3 + a] + here[i] * cells
                return tuple(parts)

            zero = jnp.zeros((8, NX), f32)
            parts = lax.fori_loop(0, ROWS, row, (zero,) * 9)
            at = t + (t // 9) * 18
            for i in range(3):
                for a in range(3):
                    both = parts[i * 3 + a]
                    w_parts[i * 81 + a * 9 + at] = both[:, :LANES] + both[:, LANES:]
            return 0

        lax.fori_loop(first, last, one, 0)

    def reduce_start():
        by_lane = jnp.sum(w_parts[...], axis=1)
        r_own[...] = jnp.sum(by_lane.T, axis=0, keepdims=True) * (1.0 / CELLS)
        send_pz(lambda to: r_own, r_pz.at[pz], red_ss.at[0], red_rs.at[0])

    def reduce_next():
        arrived(r_pz, red_rs.at[0])
        total = r_pz[0]
        for k in range(1, PZ):
            total = total + r_pz[k]
        r_mid[...] = total
        send_py(lambda to: r_mid, r_py, red_ss.at[1], red_rs.at[1])

    def reduce_end():
        arrived(r_py, red_rs.at[1])
        total = r_py[0]
        for k in range(1, PY):
            total = total + r_py[k]
        row = jnp.broadcast_to(total, (8, 256))
        for t in range(81):
            here = pltpu.roll(row, (256 - 3 * t) % 256, 1)
            i, j, a, b = t // 27, (t // 9) % 3, (t // 3) % 3, t % 3
            grad_weight[i, j, a, b : b + 1, :] = here[0:1, 0:3]
        at = lax.broadcasted_iota(jnp.int32, (1, 256), 1)
        for i in range(3):
            grad_bias[i] = jnp.sum(jnp.where(at == 243 + i, total, 0.0))
        loss[0] = jnp.sum(jnp.where(at == 246, total, 0.0))

    lane = lax.broadcasted_iota(jnp.int32, (MODES, LANES), 1)
    group = lane // 32
    kx = (pz * KL + py // 4).astype(f32) + jnp.zeros((MODES, LANES), f32)
    ky = (lax.broadcasted_iota(jnp.int32, (MODES, LANES), 0) - MODES // 2).astype(f32)
    kz = (lane % 32 + (py % 4) * 32 - MODES // 2).astype(f32)
    square = kx * kx + ky * ky + kz * kz

    def pick(first, second, third):
        return jnp.where(group == 0, first, jnp.where(group == 1, second, third))

    def next_one(cells):
        return jnp.where(group == 2, pltpu.roll(cells, 64, 1), pltpu.roll(cells, 96, 1))

    def next_two(cells):
        return jnp.where(group == 0, pltpu.roll(cells, 64, 1), pltpu.roll(cells, 32, 1))

    def turned(cells):
        return pick(ky, kz, kx) * next_two(cells) - pick(kz, kx, ky) * next_one(cells)

    def curl(real, imag):
        return -turned(imag), turned(real)

    along = pick(kx, ky, kz)
    share = along / jnp.maximum(square, 1.0)

    def project(cells):
        part = along * cells
        part = part + next_one(part) + next_two(part)
        return cells - share * part

    def out_pz(n):
        send_pz(lambda to: pz_send.at[n, to], pz_recv.at[n, pz], pz_ss.at[n], pz_rs.at[n])

    def out_py(n):
        send_py(lambda to: py_send.at[n, to], py_recv.at[n], py_ss.at[n], py_rs.at[n])

    def in_pz(n):
        arrived(pz_recv.at[n], pz_rs.at[n])

    def in_py(n):
        arrived(py_recv.at[n], py_rs.at[n])

    def x_stage(n, table):
        for c in range(3):
            x_tiles(n, table, c)
        out_pz(n)

    def x_tiles(n, table, c):
        for t in (2 * c, 2 * c + 1):
            out = dot(table[...], field_in[t * 128 : (t + 1) * 128, :], ((1,), (1,)))
            out = out.astype(bf16)
            for p in range(PZ):
                pz_send[n, p, t] = out[p * 16 : (p + 1) * 16]

    def z_stage(n):
        in_pz(n)
        for c in range(3):
            for yh in range(2):
                for h in range(2):
                    tiles = [pz_recv[n, 4 * h + g, 2 * c + yh].astype(f32) for g in range(4)]
                    for m, tile in enumerate(swap_groups(tiles, lane16)):
                        at = c * 128 + (yh * 4 + m) * 16
                        z_in[at : at + 16, h * 128 : (h + 1) * 128] = tile.astype(bf16)
        whole = dot(z_in[...], z_out[...], ((1,), (0,)))
        for c in range(3):
            for y in range(ROWS):
                r0 = whole[c * 128 + y * 16 : c * 128 + y * 16 + 8]
                r1 = whole[c * 128 + y * 16 + 8 : c * 128 + y * 16 + 16]
                stage[c, 0, pl.ds(y, 8, stride=8), :] = r0[:, :128] - r1[:, 128:]
                stage[c, 1, pl.ds(y, 8, stride=8), :] = r0[:, 128:] + r1[:, :128]
        blocks = [
            swap_groups(
                [stage[0, q], stage[1, q], stage[2, q], jnp.zeros((64, LANES), f32)], lane64
            )
            for q in range(2)
        ]
        for g in range(4):
            for k in range(KL):
                py_send[n, k * 4 + g] = jnp.concatenate(
                    [blocks[0][g][k * 8 : k * 8 + 8], blocks[1][g][k * 8 : k * 8 + 8]], axis=0
                ).astype(bf16)

    def y_stage(n):
        in_py(n)
        return dot(y_out[...], py_recv[n].reshape(512, LANES), ((1,), (0,)))

    def y_back_stage(n, modes):
        rows = dot(y_back[...], modes, ((1,), (0,))).astype(bf16)
        for d in range(PY):
            py_send[n, d] = rows[d * 16 : (d + 1) * 16]

    def z_back_stage(n):
        in_py(n)
        for k in range(KL):
            tiles = [py_recv[n, k * 4 + g].astype(f32) for g in range(4)]
            for c, tile in enumerate(swap_groups(tiles, lane16)[:3]):
                at = c * 128 + k * 16
                z_in[at : at + 16, 0:128] = tile.astype(bf16)
        whole = dot(z_in[:, 0:128], z_back[...], ((1,), (0,)))
        for c in range(3):
            both = whole[c * 128 : (c + 1) * 128]
            for k in range(KL):
                r0 = both[k * 16 : k * 16 + 8]
                r1 = both[k * 16 + 8 : k * 16 + 16]
                for half in range(2):
                    re = slice(half * 128, half * 128 + 128)
                    im = slice(half * 128 + 256, half * 128 + 384)
                    spec_out[c, half, pl.ds(k, 8, stride=16), :] = r0[:, re] + r1[:, im]
                    spec_out[c, half, pl.ds(8 + k, 8, stride=16), :] = r1[:, re] - r0[:, im]
            for h in range(2):
                for half in range(2):
                    tiles = [
                        spec_out[c, half, (h * 4 + m) * 16 : (h * 4 + m + 1) * 16]
                        for m in range(4)
                    ]
                    for g, tile in enumerate(swap_groups(tiles, lane16)):
                        pz_send[n, half * 4 + g, c * 2 + h] = tile.astype(bf16)
        out_pz(n)

    def x_back_stage(n, table, out):
        in_pz(n)
        for c in range(3):
            for t in (2 * c, 2 * c + 1):
                block = pz_recv[n, :, t].reshape(128, LANES)
                out(t, dot(block, table[...], ((0,), (0,))))

    def keep(ref):
        def store(t, cells):
            ref[t * 128 : (t + 1) * 128, :] = cells

        return store

    def rows_of(c, y):
        at = (c * ROWS + y) * DEPTH
        return slice(at, at + DEPTH)

    def cross(left, right):
        return (
            left[1] * right[2] - left[2] * right[1],
            left[2] * right[0] - left[0] * right[2],
            left[0] * right[1] - left[1] * right[0],
        )

    loads[0].wait()
    for c in range(3):
        loads[1 + c].wait()
        for y in range(ROWS):
            field_in[rows_of(c, y), :] = v_pad[c, y + 1].astype(bf16)
        x_tiles(0, x_plain, c)
    pl.semaphore_wait(barrier, PY - 1 + PZ - 1)
    out_pz(0)
    halo_y_start(v_pad, 0)
    for load in loads[4:10]:
        load.wait()
    halo_z_start(v_pad, 0)
    z_stage(0)
    out_py(0)
    shifts(v_pad, v_shift, 0)
    flatten_weight()
    modes = y_stage(0).astype(bf16)
    hat_v[...] = modes
    real, imag = curl(modes[:MODES].astype(f32), modes[MODES:].astype(f32))
    y_back_stage(1, jnp.concatenate([real, imag], axis=0).astype(bf16))
    out_py(1)
    closure_rows(range(ROWS))
    z_back_stage(1)

    for c in range(3):
        for y in range(ROWS):
            cells = v_pad[c, y + 1] + closure[c, y] - target[c, y]
            closure[c, y] = cells
            field_in[rows_of(c, y), :] = (time_step * cells).astype(bf16)
    x_stage(2, x_twice)
    x_back_stage(1, x_twice, keep(vort))
    for y in range(ROWS):
        here = [v_pad[c, y + 1] for c in range(3)]
        there = [vort[rows_of(c, y), :] for c in range(3)]
        for c, cells in enumerate(cross(here, there)):
            field_in[rows_of(c, y), :] = cells.astype(bf16)
    x_stage(3, x_plain)
    z_stage(2)
    out_py(2)
    z_stage(3)
    out_py(3)
    again = y_stage(2)
    modes = y_stage(3).astype(bf16).astype(f32)
    drag = viscosity * square
    real = project(modes[:MODES]) - drag * hat_v[:MODES].astype(f32)
    imag = project(modes[MODES:]) - drag * hat_v[MODES:].astype(f32)
    rate_hat = jnp.concatenate([real, imag], axis=0).astype(bf16)
    twice = jnp.where(kx == 0.0, 1.0, 2.0) * (time_step * time_step)
    real = (again[:MODES] + twice * rate_hat[:MODES].astype(f32)).astype(bf16)
    imag = (again[MODES:] + twice * rate_hat[MODES:].astype(f32)).astype(bf16)
    hat_r[:MODES] = real
    hat_r[MODES:] = imag
    modes = jnp.concatenate([project(real.astype(f32)), project(imag.astype(f32))], axis=0)
    y_back_stage(4, modes.astype(bf16))
    out_py(4)
    y_back_stage(5, rate_hat)
    out_py(5)
    z_back_stage(4)
    z_back_stage(5)

    x_back_stage(4, x_plain, keep(push))
    for y in range(ROWS):
        here = [v_pad[c, y + 1] for c in range(3)]
        there = [push[rows_of(c, y), :] for c in range(3)]
        for c, cells in enumerate(cross(there, here)):
            field_in[rows_of(c, y), :] = cells.astype(bf16)
    x_stage(6, x_twice)

    parts = [jnp.zeros((8, LANES), f32) for _ in range(4)]

    def misfit(t, rate):
        c = t // 2
        for m in range(4):
            y = (t % 2) * 4 + m
            cells = closure[c, y] + time_step * rate[m * DEPTH : (m + 1) * DEPTH]
            m_pad[c, y + 1] = cells
            parts[c] = parts[c] + fold(cells)
            parts[3] = parts[3] + fold(cells * cells)

    x_back_stage(5, x_twice, misfit)
    halo_y_start(m_pad, 4)
    for c in range(3):
        w_parts[243 + c] = parts[c]
    w_parts[246] = 0.5 * parts[3]
    for k in range(247, 256):
        w_parts[k] = jnp.zeros((8, LANES), f32)
    weight_parts(0, 6)
    z_stage(6)
    out_py(6)
    halo_z_start(m_pad, 4)
    weight_parts(6, 27)
    reduce_start()
    modes = y_stage(6).astype(bf16).astype(f32)
    real, imag = curl(modes[:MODES], modes[MODES:])
    real = real - drag * hat_r[:MODES].astype(f32)
    imag = imag - drag * hat_r[MODES:].astype(f32)
    y_back_stage(7, jnp.concatenate([real, imag], axis=0).astype(bf16))
    out_py(7)
    shifts(m_pad, m_shift, 4)
    grad_rows(range(0, 3))
    reduce_next()
    z_back_stage(7)
    grad_rows(range(3, ROWS))
    for y in range(ROWS):
        here = [vort[rows_of(c, y), :] for c in range(3)]
        there = [push[rows_of(c, y), :] for c in range(3)]
        for c, cells in enumerate(cross(here, there)):
            closure[c, y] = closure[c, y] + m_pad[c, y + 1] + cells
    reduce_end()

    def finish(t, cells):
        for m in range(4):
            y = (t % 2) * 4 + m
            grad[t // 2, y] = closure[t // 2, y] + cells[m * DEPTH : (m + 1) * DEPTH]

    x_back_stage(7, x_plain, finish)

    for n in range(8):
        arrived(pz_send.at[n, 0 : PZ - 1], pz_ss.at[n])
        arrived(py_send.at[n, 0 : PY - 1], py_ss.at[n])
    for n in (0, 4):
        pad = v_pad if n == 0 else m_pad
        arrived(pad.at[:, 0], halo_ss.at[n])
        arrived(pad.at[:, 0], halo_ss.at[n + 1])
        arrived(halo_out.at[n // 4, 0], halo_ss.at[n + 2])
        arrived(halo_out.at[n // 4, 1], halo_ss.at[n + 3])
    arrived(r_pz.at[0 : PZ - 1], red_ss.at[0])
    arrived(r_py.at[0 : PY - 1], red_ss.at[1])


def on_device(velocity, target, closure_weight, closure_bias):
    shape = velocity.shape
    given = [jnp.asarray(t) for t in tables()]
    in_vmem = pl.BlockSpec(memory_space=pltpu.VMEM)
    in_smem = pl.BlockSpec(memory_space=pltpu.SMEM)
    dma = pltpu.SemaphoreType.DMA
    pad = (3, ROWS + 2, DEPTH, NX)
    in_hbm = pl.BlockSpec(memory_space=pl.ANY)
    landing = (PZ, 6, 16, LANES)
    grad, grad_weight, grad_bias, loss = pl.pallas_call(
        kernel,
        out_shape=(
            jax.ShapeDtypeStruct(shape, f32),
            jax.ShapeDtypeStruct(closure_weight.shape, f32),
            jax.ShapeDtypeStruct((3,), f32),
            jax.ShapeDtypeStruct((1,), f32),
        ),
        in_specs=[in_hbm, in_hbm, in_hbm, in_smem] + [in_hbm] * 6,
        out_specs=(in_vmem, in_vmem, in_smem, in_smem),
        scratch_shapes=[pltpu.VMEM(t.shape, bf16) for t in given]
        + [
            pltpu.VMEM(shape, f32),
            pltpu.VMEM((8,) + landing, bf16),
            pltpu.VMEM((8,) + landing, bf16),
            pltpu.VMEM((8, PY, 16, LANES), bf16),
            pltpu.VMEM((8, PY, 16, LANES), bf16),
            pltpu.VMEM((768, NX), bf16),
            pltpu.VMEM((384, 256), bf16),
            pltpu.VMEM((3, 2, 64, LANES), f32),
            pltpu.VMEM((3, 2, 128, LANES), f32),
            pltpu.VMEM((768, NX), f32),
            pltpu.VMEM((768, NX), f32),
            pltpu.VMEM(pad, f32),
            pltpu.VMEM(pad, f32),
            pltpu.VMEM((27, ROWS + 2, DEPTH, NX), f32),
            pltpu.VMEM((27, ROWS + 2, DEPTH, NX), f32),
            pltpu.VMEM((3, ROWS, DEPTH, NX), f32),
            pltpu.VMEM((2, 2, 32, NX), f32),
            pltpu.VMEM((2, 2, 32, NX), f32),
            pltpu.VMEM((256, 8, LANES), f32),
            pltpu.VMEM((1, 256), f32),
            pltpu.VMEM((PZ, 1, 256), f32),
            pltpu.VMEM((1, 256), f32),
            pltpu.VMEM((PY, 1, 256), f32),
            pltpu.VMEM((256, LANES), bf16),
            pltpu.VMEM((256, LANES), bf16),
            dma((8,)), dma((8,)), dma((8,)), dma((8,)), dma((8,)), dma((8,)), dma((2,)), dma((2,)),
            dma((11,)), pltpu.SMEM(closure_weight.shape, f32),
            pltpu.SMEM((243,), f32),
        ],
        compiler_params=pltpu.CompilerParams(
            collective_id=0, has_side_effects=True, vmem_limit_bytes=56 << 20
        ),
        name="euler",
    )(velocity, target, closure_weight, closure_bias, *given)
    return grad, grad_weight, grad_bias, loss.reshape(())


def solution(mesh):
    in_specs = (P(None, "py", "pz", None), P(None, "py", "pz", None), P(), P())
    out_specs = (P(None, "py", "pz", None), P(), P(), P())
    return jax.shard_map(
        on_device, mesh=mesh, in_specs=in_specs, out_specs=out_specs, check_vma=False
    )
```
